256 devices in a mesh: grp: 4 (over y), blk: 64 (over x, z, core).
Axes of the slice: x: 4, y: 4, z: 8, core: 2. Of those that a mesh axis runs over, the one named last changes fastest.
Arguments:
- atmos_state: float32 [4, 16, 16, 262144], P(None, None, None, ('grp', 'blk')), may hold values from -6 to 6
- neighbours: int32 [4, 262144], P(None, ('grp', 'blk')), may hold values from 0 to 262143, as said below
- flux_weight: float32 [12, 4], replicated, may hold values from -3 to 3
- block_weights: bfloat16 [1024, 16, 128, 128], P('blk'), may hold values from -0.125 to 0.125
- block_ids: int32 [1024, 16], P('blk'), may hold values from 0 to 32767, as said below
- block_counts: int32 [1024], P('blk'), may hold values from 10 to 16, as said below
- ocean_cells: int32 [131072], P('blk'), may hold values from 0 to 131071, as said below
Outputs:
- new_state: float32 [4, 16, 16, 262144], P(None, None, None, ('grp', 'blk'))
- ocean_flux: float32 [12, 131072], P('grp', 'blk')
The draws below stay inside these ranges and needn't reach their ends.
Inputs may be any that keep to these rules, and one draw needn't show every extreme that they name: `neighbours`: each neighbour lies within 256 positions of its element in the cyclic order of elements, and some lie exactly 256 away. `block_ids`: the live entries (b < block_counts) of the row blocks of one index of blk name at most 32 column blocks c of any one atmosphere device (same c // 128, devices counted along grp+blk), and exactly 32 for some device. `block_counts`: some row block of every index of blk has 16 live entries. A permutation of the ocean cells. Of the 2048 cells of one index of blk, at most 48 have the same ocean_cells // 2048, and exactly 48 for some.
All inputs are finite; a program needn't handle non-finite values.
Results may differ from the reference program's by a relative error of at most 0.0029.
Values may be sent and summed in bfloat16 or wider, within the bound.
No kernel may reach another device: no remote copies, remote signals or barrier semaphores. Data moves between devices by JAX's collectives and lax.ppermute only.
A program may use at most 128 MiB of HBM per device.

```python
import jax
import jax.numpy as jnp
import numpy as np
from jax import lax

NVAR = 4
LEV = 16
EDEV = 1024
FIELDS = 12
BLOCK = 128
NNZB = 16
RB_DEV = 16
ELEMS = 262144
HW = 256
CB_DEV = 128
RB = 1024
RC_DEV = 2048
OCELLS = 131072
PIECE = 32
OCAP = 48
CAP_A = 32
N_GRP = 4
N_BLK = 64
DEVICES = 256


def draw_neighbours(key, part):
    key = jax.random.fold_in(key, 31)
    offsets = jax.random.randint(key, (4, ELEMS), -HW, HW + 1)
    element_at = jnp.arange(ELEMS)
    offsets = offsets.at[0].set(jnp.where(element_at % EDEV == 0, -HW, offsets[0]))
    offsets = offsets.at[1].set(jnp.where(element_at % EDEV == EDEV - 1, HW, offsets[1]))
    return jnp.mod(element_at[None, :] + offsets, ELEMS).astype(jnp.int32)


def remap_pattern(key):
    count_key = jax.random.fold_in(key, 11)
    base_key = jax.random.fold_in(key, 12)
    stray_key = jax.random.fold_in(key, 13)
    local_key = jax.random.fold_in(key, 14)
    stack_key = jax.random.fold_in(key, 15)
    pick_key = jax.random.fold_in(key, 16)
    counts = jax.random.randint(count_key, (RB,), 5 * NNZB // 8, NNZB + 1)
    leading = jnp.arange(RB) % RB_DEV == 0
    counts = jnp.where(leading, NNZB, counts).astype(jnp.int32)
    is_live = (jnp.arange(NNZB)[None, :] < counts[:, None]).reshape(N_BLK, RB_DEV * NNZB)
    live_rank = jnp.cumsum(is_live.astype(jnp.int32), axis=1) - 1
    step_index = jnp.maximum(live_rank, 0) // CAP_A
    base_dev = jax.random.randint(base_key, (N_BLK, 1), 0, DEVICES)
    base_grp = base_dev // N_BLK
    base_lane = base_dev % N_BLK
    spread = jnp.mod(base_dev + step_index, DEVICES)
    piled = jnp.mod(base_grp + step_index, N_GRP) * N_BLK + jnp.mod(base_lane + step_index // N_GRP, N_BLK)
    stacked = jax.random.randint(stack_key, (N_BLK, 1), 0, 2)
    forced = jax.random.randint(pick_key, (), 0, N_BLK)
    stacked = jnp.where(jnp.arange(N_BLK)[:, None] == forced, 1, stacked)
    source = jnp.where(stacked == 1, piled, spread)
    stray = jax.random.randint(stray_key, (N_BLK, RB_DEV * NNZB), 0, DEVICES)
    source = jnp.where(is_live, source, stray)
    local_block = jax.random.randint(local_key, (N_BLK, RB_DEV * NNZB), 0, CB_DEV)
    block_ids = (source * CB_DEV + local_block).reshape(RB, NNZB).astype(jnp.int32)
    return (counts, block_ids)


def draw_block_ids(key, part):
    pattern = remap_pattern(key)
    return pattern[1]


def draw_block_counts(key, part):
    pattern = remap_pattern(key)
    return pattern[0]


def draw_ocean_cells(key, part):
    key = jax.random.fold_in(key, 21)
    first_key, second_key, third_key, fourth_key = jax.random.split(key, 4)
    lower = jax.random.randint(first_key, (N_BLK // 2,), PIECE // 2, OCAP + 1)
    lower = lower.at[0].set(OCAP)
    sizes = jnp.stack([lower, 2 * PIECE - lower], axis=1).reshape(N_BLK)
    piece_ends = jnp.cumsum(sizes)
    slots_at = jnp.arange(RC_DEV)
    piece = jnp.sum((slots_at[:, None] >= piece_ends[None, :]).astype(jnp.int32), axis=1)
    offsets = jax.random.permutation(second_key, N_BLK)
    shuffles = jax.vmap(jax.random.permutation, in_axes=(0, None))(jax.random.split(third_key, N_BLK), RC_DEV)
    owners = jnp.arange(N_BLK)[:, None]
    coupler = jnp.mod(owners - offsets[piece][None, :], N_BLK)
    cells = coupler * RC_DEV + shuffles[coupler, slots_at[None, :]]
    arrange = jax.vmap(jax.random.permutation, in_axes=(0, None))(jax.random.split(fourth_key, N_BLK), RC_DEV)
    cells = jnp.take_along_axis(cells, arrange, axis=1)
    return cells.reshape(OCELLS).astype(jnp.int32)


def level_of(own_key, extent, cuts, least, high):
    level, own = 1.0, jax.random.fold_in(own_key, 6)
    for dim, blocks in cuts:
        heights = jnp.exp(jax.random.uniform(jax.random.fold_in(own, dim), (blocks,), jnp.float32, least / len(cuts), high / len(cuts)))
        level = level * jnp.repeat(heights, extent[dim] // blocks).reshape([-1 if axis == dim else 1 for axis in range(len(extent))])
    return level


def gaussian(own_key, shape, scale, reach, cuts=(), kind=jnp.bfloat16):
    values = scale * jax.random.normal(own_key, shape, jnp.float32)
    if cuts:
        values = values * level_of(own_key, shape, cuts, -0.22, 0.18)
    return jnp.clip(values, -reach, reach).astype(kind)


def setup_inputs(seed: int = 0) -> dict:
    splits = jax.random.split(jax.random.key(seed), 8)
    return {
        "atmos_state": gaussian(splits[0], (NVAR, LEV, 16, ELEMS), 1.0, 6.0, ((3, 256),), jnp.float32),
        "neighbours": draw_neighbours(jax.random.fold_in(splits[7], 71), 0),
        "flux_weight": gaussian(splits[2], (FIELDS, NVAR), NVAR ** -0.5, 3.0, (), jnp.float32),
        "block_weights": gaussian(splits[3], (RB, NNZB, BLOCK, BLOCK), (BLOCK * NNZB) ** -0.5, 0.125, ((0, 64),)),
        "block_ids": draw_block_ids(jax.random.fold_in(splits[7], 71), 0),
        "block_counts": draw_block_counts(jax.random.fold_in(splits[7], 71), 0),
        "ocean_cells": draw_ocean_cells(jax.random.fold_in(splits[7], 71), 0),
    }


time_step = 0.02
viscosity = 0.05

def derivative_matrix():
    gll_nodes = np.array([-1.0, -1.0 / np.sqrt(5.0), 1.0 / np.sqrt(5.0), 1.0])
    weights = np.array([np.prod([gll_nodes[anchor] - gll_nodes[partner] for partner in range(4) if partner != anchor]) for anchor in range(4)])
    matrix = np.zeros((4, 4))
    for anchor in range(4):
        for target in range(4):
            if anchor != target:
                matrix[anchor, target] = weights[anchor] / weights[target] / (gll_nodes[anchor] - gll_nodes[target])
            else:
                matrix[anchor, anchor] = sum((1.0 / (gll_nodes[anchor] - gll_nodes[partner]) for partner in range(4) if partner != anchor))
    return jnp.asarray(matrix, jnp.float32)

def along_east(derivative, values):
    return jnp.einsum('jk,vlike->vlije', derivative, values, precision=lax.Precision.HIGHEST)

def along_north(derivative, values):
    return jnp.einsum('ik,vlkje->vlije', derivative, values, precision=lax.Precision.HIGHEST)

def advance(fields, derivative):
    shaped = fields.reshape(fields.shape[0], fields.shape[1], 4, 4, fields.shape[3])
    slope_east = along_east(derivative, shaped)
    slope_north = along_north(derivative, shaped)
    bend = along_east(derivative, slope_east) + along_north(derivative, slope_north)
    change = -(shaped[0:1] * slope_east + shaped[1:2] * slope_north) + viscosity * bend
    return (shaped + time_step * change).reshape(fields.shape)

def edge_update(stepped, across):
    dims = (stepped.shape[0], stepped.shape[1], 4, 4, stepped.shape[3])
    shaped = stepped.reshape(dims)
    from_west = across[0].reshape(dims)
    from_east = across[1].reshape(dims)
    from_south = across[2].reshape(dims)
    from_north = across[3].reshape(dims)
    correction = jnp.zeros(dims, jnp.float32)
    correction = correction.at[:, :, :, 0, :].add(from_west[:, :, :, 3, :] - shaped[:, :, :, 0, :])
    correction = correction.at[:, :, :, 3, :].add(from_east[:, :, :, 0, :] - shaped[:, :, :, 3, :])
    correction = correction.at[:, :, 0, :, :].add(from_south[:, :, 3, :, :] - shaped[:, :, 0, :, :])
    correction = correction.at[:, :, 3, :, :].add(from_north[:, :, 0, :, :] - shaped[:, :, 3, :, :])
    return (shaped + 0.5 * correction).reshape(stepped.shape)

def reference(atmos_state, neighbours, flux_weight, block_weights, block_ids, block_counts, ocean_cells):
    derivative = derivative_matrix()
    stepped = advance(atmos_state, derivative)
    across = tuple((jnp.take(stepped, neighbours[border], axis=3) for border in range(4)))
    new_state = edge_update(stepped, across)
    bottom = new_state[:, LEV - 1]
    wind_speed = jnp.sqrt(1.0 + bottom[0] * bottom[0] + bottom[1] * bottom[1])
    combined = jnp.einsum('jv,vpe->jpe', flux_weight, bottom, precision=lax.Precision.HIGHEST)
    surface = (combined * wind_speed[None]).astype(jnp.bfloat16)
    blocks = surface.reshape(FIELDS, 16, ELEMS // BLOCK, BLOCK).transpose(2, 1, 0, 3).reshape(16 * (ELEMS // BLOCK), FIELDS, BLOCK)

    def one_row(inputs):
        row_weights, row_ids, row_count = inputs
        picked = jnp.take(blocks, row_ids, axis=0).astype(jnp.float32)
        is_live = jnp.arange(NNZB) < row_count
        picked = jnp.where(is_live[:, None, None], picked, jnp.zeros((), jnp.float32))
        return jnp.einsum('bfm,bim->fi', picked, row_weights.astype(jnp.float32), precision=lax.Precision.HIGHEST)
    remapped = lax.map(one_row, (block_weights, block_ids, block_counts))
    remapped = remapped.transpose(1, 0, 2).reshape(FIELDS, OCELLS)
    ocean_flux = jnp.take(remapped, ocean_cells, axis=1)
    return (new_state, ocean_flux)
```

```python
import functools

import jax
import jax.numpy as jnp
import ml_dtypes
import numpy as np
from jax import lax
from jax.experimental import pallas as pl
from jax.experimental.pallas import tpu as pltpu
from jax.sharding import PartitionSpec as P

time_step = 0.02
viscosity = 0.05
LANES = 128
REACH = 256
f32 = jnp.float32
bf16 = jnp.bfloat16
i32 = jnp.int32
both = ("grp", "blk")
vmem_bytes = 48 * 1024 * 1024


def params():
    return pltpu.CompilerParams(vmem_limit_bytes=vmem_bytes)


def cost(flops, moved):
    return pl.CostEstimate(flops=flops, bytes_accessed=moved, transcendentals=0)


def whole(shape):
    return pl.BlockSpec(shape, lambda *_: (0,) * len(shape))


def derivative_matrix():
    nodes = np.array([-1.0, -1.0 / np.sqrt(5.0), 1.0 / np.sqrt(5.0), 1.0])
    others = [[k for k in range(4) if k != n] for n in range(4)]
    weights = [np.prod([nodes[n] - nodes[k] for k in others[n]]) for n in range(4)]
    matrix = np.zeros((4, 4))
    for a in range(4):
        for c in range(4):
            if a != c:
                matrix[a, c] = weights[a] / weights[c] / (nodes[a] - nodes[c])
            else:
                matrix[a, a] = sum(1.0 / (nodes[a] - nodes[k]) for k in others[a])
    return matrix


def operators(copies):
    d = derivative_matrix().astype(np.float32).astype(np.float64)
    east, north = np.kron(np.eye(4), d), np.kron(d, np.eye(4))
    bend = east @ east + north @ north
    parts = [-time_step * east, -time_step * north, time_step * viscosity * bend]
    stacked = np.concatenate([np.kron(np.eye(copies), part) for part in parts])
    high = stacked.astype(ml_dtypes.bfloat16)
    low = (stacked - high.astype(np.float64)).astype(ml_dtypes.bfloat16)
    return jnp.asarray(high), jnp.asarray(low)


def split_two(x):
    high = x.astype(bf16)
    return high, (x - high.astype(f32)).astype(bf16)


def split_three(x):
    high = x.astype(bf16)
    rest = x - high.astype(f32)
    mid = rest.astype(bf16)
    return high, mid, (rest - mid.astype(f32)).astype(bf16)


def dot(a, b):
    return jnp.dot(a, b, preferred_element_type=f32)


def dot_nt(a, b):
    return lax.dot_general(a, b, (((1,), (1,)), ((), ())), preferred_element_type=f32)


def apply_operators(high, low, x):
    xh, xl = split_two(x)
    return dot(high, xh) + dot(high, xl) + dot(low, xh)


def iota(shape, dim):
    return lax.broadcasted_iota(i32, shape, dim)


def bottom_step(x_ref, high_ref, low_ref, out_ref, first_ref, last_ref):
    x = x_ref[:, 0].reshape(64, -1)
    op = apply_operators(high_ref[...], low_ref[...], x)
    size = x.shape[1]
    for v in range(4):
        rows = slice(16 * v, 16 * v + 16)
        stepped = (
            x[rows] + x[0:16] * op[rows] + x[16:32] * op[64:128][rows] + op[128:192][rows]
        )
        out_ref[v] = stepped
        first_ref[v] = stepped[:, :REACH]
        last_ref[v] = stepped[:, size - REACH :]


def bottom_stepped(state):
    nvar, levels, points, size = state.shape
    high, low = operators(nvar)
    shape = (nvar, points, size)
    rim = (nvar, points, REACH)
    return pl.pallas_call(
        bottom_step,
        grid=(1,),
        in_specs=[
            pl.BlockSpec((nvar, 1, points, size), lambda i: (0, levels - 1, 0, 0)),
            whole(high.shape),
            whole(low.shape),
        ],
        out_specs=[whole(shape), whole(rim), whole(rim)],
        out_shape=[jax.ShapeDtypeStruct(s, f32) for s in (shape, rim, rim)],
        compiler_params=params(),
        name="bottom_step",
    )(state, high, low)


def full_step(x_ref, high_ref, low_ref, out_ref, first_ref, last_ref):
    step = pl.program_id(0)
    high, low = high_ref[...], low_ref[...]
    xs = [x_ref[v].reshape(256, REACH) for v in range(4)]
    for v in range(4):
        op = apply_operators(high, low, xs[v])
        stepped = xs[v] + xs[0] * op[0:256] + xs[1] * op[256:512] + op[512:768]
        stepped = stepped.reshape(x_ref.shape[1:])
        out_ref[v] = stepped

        @pl.when(step == 0)
        def _():
            first_ref[v] = stepped.astype(bf16)

        @pl.when(step == pl.num_programs(0) - 1)
        def _():
            last_ref[v] = stepped.astype(bf16)


def full_stepped(state):
    nvar, levels, points, size = state.shape
    high, low = operators(levels)
    block = (nvar, levels, points, REACH)
    return pl.pallas_call(
        full_step,
        grid=(size // REACH,),
        in_specs=[
            pl.BlockSpec(block, lambda i: (0, 0, 0, i)),
            whole(high.shape),
            whole(low.shape),
        ],
        out_specs=[pl.BlockSpec(block, lambda i: (0, 0, 0, i)), whole(block), whole(block)],
        out_shape=[
            jax.ShapeDtypeStruct(state.shape, f32),
            jax.ShapeDtypeStruct(block, bf16),
            jax.ShapeDtypeStruct(block, bf16),
        ],
        compiler_params=params(),
        cost_estimate=cost(3 * 2 * 768 * 256 * 4096, 9 << 20),
        name="full_step",
    )(state, high, low)


def local_columns(nb_ref, first, elements):
    place = nb_ref[...] - first + REACH
    place = jnp.where(place < 0, place + elements, place)
    return jnp.where(place >= elements, place - elements, place)


def side_indices(place, rows, eb):
    cols = slice(eb * LANES, (eb + 1) * LANES)
    part = [jnp.broadcast_to(place[s : s + 1, cols], (rows, LANES)) for s in range(4)]
    point = iota((rows, LANES), 0) % 16
    we = jnp.where(point % 4 == 3, part[0], part[1])
    ns = jnp.where(point < 4, part[3], part[2])
    return we, ns


def edge_update(columns, we, ns, eb):
    own = columns[2]
    rows = own.shape[0]
    gathered = []
    for index in (we, ns):
        lane = index & (LANES - 1)
        column = (index >> 7) - eb
        value = jnp.take_along_axis(columns[0], lane, axis=1)
        for c in range(1, 5):
            value = jnp.where(
                column == c, jnp.take_along_axis(columns[c], lane, axis=1), value
            )
        gathered.append(value)
    point = iota(own.shape, 0) % 16
    b, a = point % 4, point // 4
    from_we, from_ns = gathered
    zero = jnp.zeros_like(own)
    total = jnp.where(b == 0, pltpu.roll(from_we, rows - 3, 0) - own, zero)
    total += jnp.where(b == 3, pltpu.roll(from_we, 3, 0) - own, zero)
    total += jnp.where(a == 0, pltpu.roll(from_ns, rows - 12, 0) - own, zero)
    total += jnp.where(a == 3, pltpu.roll(from_ns, 12, 0) - own, zero)
    return own + 0.5 * total


def window(own, before, after, eb):
    count = own.shape[-1] // LANES
    pieces = []
    for c in range(eb, eb + 5):
        if c < 2:
            piece = before[..., c * LANES : (c + 1) * LANES]
        elif c < 2 + count:
            piece = own[..., (c - 2) * LANES : (c - 1) * LANES]
        else:
            piece = after[..., (c - 2 - count) * LANES : (c - 1 - count) * LANES]
        pieces.append(piece)
    return pieces


def bottom_edges(elements, first_ref, s_ref, before_ref, after_ref, nb_ref, out_ref):
    place = local_columns(nb_ref, first_ref[0], elements)
    own = s_ref[...].reshape(64, -1)
    before = before_ref[...].reshape(64, -1)
    after = after_ref[...].reshape(64, -1)
    count = own.shape[1] // LANES
    new = []
    for eb in range(count):
        we, ns = side_indices(place, 64, eb)
        new.append(edge_update(window(own, before, after, eb), we, ns, eb))
    for v in range(4):
        blocks = jnp.concatenate([piece[16 * v : 16 * v + 16] for piece in new], axis=0)
        turned = blocks.T
        out_ref[64 * v : 64 * v + 64, :LANES] = turned[:64]
        out_ref[64 * v : 64 * v + 64, LANES:] = turned[64:]


def bottom_slices(stepped, before, after, neighbours, first, elements):
    shape = (256, 2 * LANES)
    return pl.pallas_call(
        functools.partial(bottom_edges, elements),
        in_specs=[
            pl.BlockSpec(memory_space=pltpu.SMEM),
            pl.BlockSpec(memory_space=pltpu.VMEM),
            pl.BlockSpec(memory_space=pltpu.VMEM),
            pl.BlockSpec(memory_space=pltpu.VMEM),
            pl.BlockSpec(memory_space=pltpu.VMEM),
        ],
        out_shape=jax.ShapeDtypeStruct(shape, f32),
        compiler_params=params(),
        name="bottom_edges",
    )(first, stepped, before, after, neighbours)


def full_edges(elements, first_ref, s_ref, before_ref, after_ref, nb_ref, out_ref):
    place = local_columns(nb_ref, first_ref[0], elements)
    levels, size = s_ref.shape[1], s_ref.shape[3]
    for eb in range(size // LANES):
        we, ns = side_indices(place, 16, eb)

        def one(level, carry):
            own = s_ref.at[0, level]
            before = before_ref.at[0, level]
            after = after_ref.at[0, level]
            columns = [p[...].astype(f32) for p in window_refs(own, before, after, eb)]
            out_ref[0, level, :, eb * LANES : (eb + 1) * LANES] = edge_update(
                columns, we, ns, eb
            )
            return carry

        lax.fori_loop(0, levels, one, 0, unroll=4)


def window_refs(own, before, after, eb):
    count = own.shape[-1] // LANES
    pieces = []
    for c in range(eb, eb + 5):
        if c < 2:
            ref, at = before, c
        elif c < 2 + count:
            ref, at = own, c - 2
        else:
            ref, at = after, c - 2 - count
        pieces.append(ref.at[:, at * LANES : (at + 1) * LANES])
    return pieces


def full_new_state(stepped, before, after, neighbours, first, elements):
    nvar, levels, points, size = stepped.shape
    block = (1, levels, points, size)
    rim = (1, levels, points, REACH)
    along = lambda v: (v, 0, 0, 0)
    return pl.pallas_call(
        functools.partial(full_edges, elements),
        grid=(nvar,),
        in_specs=[
            pl.BlockSpec(memory_space=pltpu.SMEM),
            pl.BlockSpec(block, along),
            pl.BlockSpec(rim, along),
            pl.BlockSpec(rim, along),
            whole(neighbours.shape),
        ],
        out_specs=pl.BlockSpec(block, along),
        out_shape=jax.ShapeDtypeStruct(stepped.shape, f32),
        compiler_params=params(),
        cost_estimate=cost(10**9, 10 << 20),
        name="full_edges",
    )(first, stepped, before, after, neighbours)


def request_table(cells_ref, ids_ref, out_ref, rank_ref):
    chunks = cells_ref.shape[0]
    owner_at = iota((64, LANES), 0)
    strict = (iota((LANES, LANES), 0) < iota((LANES, LANES), 1)).astype(bf16)
    counted = jnp.zeros((64, 1), f32)
    high = jnp.zeros((64, 64), f32)
    low = jnp.zeros((64, 64), f32)
    for c in range(chunks):
        cell = cells_ref[c : c + 1, :]
        mine = owner_at == (cell >> 11)
        onehot = jnp.where(mine, 1.0, 0.0)
        earlier = dot(onehot.astype(bf16), strict) + counted
        counted = counted + jnp.sum(onehot, axis=1, keepdims=True)
        rank = jnp.sum(onehot * earlier, axis=0, keepdims=True).astype(i32)
        rank_ref[c : c + 1, :] = rank
        slot = jnp.where(iota((64, LANES), 0) == rank, 1.0, 0.0).astype(bf16)
        row = cell & 2047
        high += dot_nt((onehot * (row >> 7).astype(f32)).astype(bf16), slot)
        low += dot_nt((onehot * (row & 127).astype(f32)).astype(bf16), slot)
    wanted = (high * 128.0 + low).astype(i32)
    out_ref[:, 0, :] = jnp.broadcast_to(ids_ref[0:1, :], (64, LANES))
    out_ref[:, 1, :] = jnp.broadcast_to(ids_ref[1:2, :], (64, LANES))
    out_ref[:, 2, :] = jnp.concatenate([wanted, wanted], axis=1)


def requests(ocean_cells, ids):
    chunks = ocean_cells.shape[0] // LANES
    return pl.pallas_call(
        request_table,
        out_shape=[
            jax.ShapeDtypeStruct((64, 3, LANES), i32),
            jax.ShapeDtypeStruct((chunks, LANES), i32),
        ],
        compiler_params=params(),
        name="request_table",
    )(ocean_cells.reshape(chunks, LANES), ids)


def pick_values(table_ref, index_ref, out_ref, turned_ref, found_ref):
    turned = table_ref[...].T
    high, low = split_two(turned)
    turned_ref[0] = high
    turned_ref[1] = low
    device_at = iota((256, 4 * LANES), 0)
    block_at = iota((LANES, 4 * LANES), 0)

    def some(step, carry):
        rows = [index_ref[2 * step + k, y : y + 1, :] for k in range(2) for y in range(2)]
        ids = jnp.concatenate(rows, axis=1)
        onehot = jnp.where(device_at == (ids >> 7), 1.0, 0.0).astype(bf16)
        value = dot(turned_ref[0], onehot) + dot(turned_ref[1], onehot)
        hit = block_at == (ids & 127)
        for half in range(2):
            part = value[half * LANES : (half + 1) * LANES]
            found = jnp.sum(jnp.where(hit, part, 0.0), axis=0, keepdims=True)
            for k in range(2):
                for y in range(2):
                    at = (2 * k + y) * LANES
                    found_ref[half, y, pl.ds(2 * step + k, 1), :] = found[:, at : at + LANES]
        return carry

    lax.fori_loop(0, 32, some, 0)
    lane = iota((64, LANES), 1)
    for y in range(2):
        first, second = found_ref[0, y], found_ref[1, y]
        out_ref[64 * y : 64 * y + 64, :] = jnp.where(
            lane < 64, first, pltpu.roll(second, 64, 1)
        )
        out_ref[64 * y + 128 : 64 * y + 192, :] = jnp.where(
            lane < 64, pltpu.roll(first, 64, 1), second
        )


def picked(table, index):
    return pl.pallas_call(
        pick_values,
        out_shape=jax.ShapeDtypeStruct((256, LANES), f32),
        scratch_shapes=[
            pltpu.VMEM((2, 256, 256), bf16),
            pltpu.VMEM((2, 2, 64, LANES), f32),
        ],
        compiler_params=params(),
        name="pick_values",
    )(table, index)


def remap_rows(
    grp_ref, fw_ref, got_ref, index_ref, w_ref, out_ref, field_ref, mapped_ref, sent_ref
):
    step = pl.program_id(0)

    @pl.when(step == 0)
    def _():
        values = []
        for v in range(4):
            turned = got_ref[64 * v : 64 * v + 64, :].T
            values.append(jnp.concatenate([turned[:64], turned[64:]], axis=1))
        wind = jnp.sqrt(1.0 + values[0] * values[0] + values[1] * values[1])
        for f in range(16):
            if f < 12:
                total = fw_ref[f, 0] * values[0]
                for v in range(1, 4):
                    total += fw_ref[f, v] * values[v]
                total = (total * wind).astype(bf16).astype(f32)
            else:
                total = jnp.zeros((64, LANES), f32)
            field_ref[pl.ds(f, 64, stride=16), :] = total

    total = jnp.zeros((16, LANES), f32)
    for b in range(16):
        at = pl.multiple_of((step * 16 + b) * 16, 16)
        total += dot_nt(field_ref[pl.ds(at, 16), :].astype(bf16), w_ref[0, b])
    mapped_ref[:, pl.ds(pl.multiple_of(step * LANES, LANES), LANES)] = total

    @pl.when(step == pl.num_programs(0) - 1)
    def _():
        parts = jnp.concatenate(split_three(mapped_ref[...]), axis=0)
        lane = iota((1, LANES), 1)
        row_at = iota((512, 4 * LANES), 0) + grp_ref[0] * 512

        def some(at, carry):
            rows = [
                jnp.where(
                    lane < 64,
                    index_ref[4 * at + k, 2:3, :],
                    index_ref[4 * at + k + 32, 2:3, :],
                )
                for k in range(4)
            ]
            onehot = jnp.where(row_at == jnp.concatenate(rows, axis=1), 1.0, 0.0).astype(bf16)
            value = dot(parts, onehot)
            value = value[0:16] + value[16:32] + value[32:48]
            for k in range(4):
                sent_ref[pl.ds(4 * at + k, 16, stride=32), :] = value[
                    :, k * LANES : (k + 1) * LANES
                ]
            return carry

        lax.fori_loop(0, 8, some, 0)
        lane = iota((32, LANES), 1)
        for y in range(4):
            a, b, c = [sent_ref[(3 * y + f) * 32 : (3 * y + f) * 32 + 32, :] for f in range(3)]
            base = 64 * y
            out_ref[base : base + 32, :LANES] = jnp.where(lane < 64, a, pltpu.roll(b, 64, 1))
            out_ref[base : base + 32, LANES:] = c
            out_ref[base + 32 : base + 64, :LANES] = jnp.where(
                lane < 64, pltpu.roll(a, 64, 1), b
            )
            out_ref[base + 32 : base + 64, LANES:] = pltpu.roll(c, 64, 1)


def remapped_cells(grp, flux_weight, got, index, block_weights):
    slots, block = block_weights.shape[1], block_weights.shape[2]
    grid_spec = pltpu.PrefetchScalarGridSpec(
        num_scalar_prefetch=1,
        grid=(4,),
        in_specs=[
            pl.BlockSpec(memory_space=pltpu.SMEM),
            pl.BlockSpec(got.shape, lambda i, g: (0, 0)),
            pl.BlockSpec(index.shape, lambda i, g: (0, 0, 0)),
            pl.BlockSpec((1, slots, block, block), lambda i, g: (4 * g[0] + i, 0, 0, 0)),
        ],
        out_specs=pl.BlockSpec((256, 2 * LANES), lambda i, g: (0, 0)),
        scratch_shapes=[
            pltpu.VMEM((64 * 16, LANES), f32),
            pltpu.VMEM((16, 512), f32),
            pltpu.VMEM((16 * 32, LANES), f32),
        ],
    )
    return pl.pallas_call(
        remap_rows,
        grid_spec=grid_spec,
        out_shape=jax.ShapeDtypeStruct((256, 2 * LANES), f32),
        compiler_params=params(),
        name="remap_rows",
    )(grp, flux_weight, got, index, block_weights)


def place_cells(got_ref, cells_ref, rank_ref, out_ref):
    table = got_ref[0:64] + got_ref[64:128] + got_ref[128:192] + got_ref[192:256]
    parts = jnp.concatenate(split_three(table[:, :192].T), axis=1)
    owner_at = iota((64, 4 * LANES), 0)
    for c in range(4):
        rows = range(4 * c, 4 * c + 4)
        cell = jnp.concatenate([cells_ref[r : r + 1, :] for r in rows], axis=1)
        rank = jnp.concatenate([rank_ref[r : r + 1, :] for r in rows], axis=1)
        onehot = jnp.where(owner_at == (cell >> 11), 1.0, 0.0).astype(bf16)
        value = dot(parts, jnp.concatenate([onehot] * 3, axis=0))
        hit = owner_at == rank
        for f in range(3):
            out_ref[f : f + 1, c * 4 * LANES : (c + 1) * 4 * LANES] = jnp.sum(
                jnp.where(hit, value[64 * f : 64 * f + 64], 0.0), axis=0, keepdims=True
            )


def placed(got, ocean_cells, rank):
    count = ocean_cells.shape[0]
    return pl.pallas_call(
        place_cells,
        out_shape=jax.ShapeDtypeStruct((3, count), f32),
        compiler_params=params(),
        name="place_cells",
    )(got, ocean_cells.reshape(count // LANES, LANES), rank)


def around(first, last):
    count = lax.axis_size(both)
    up = [(i, (i + 1) % count) for i in range(count)]
    down = [(j, i) for i, j in up]
    return lax.ppermute(last, both, up), lax.ppermute(first, both, down)


def exchange(x, axis):
    return lax.all_to_all(x, axis, split_axis=0, concat_axis=0, tiled=True)


def body(atmos_state, neighbours, flux_weight, block_weights, block_ids, block_counts, ocean_cells):
    size = atmos_state.shape[3]
    elements = size * lax.axis_size(both)
    grp = lax.axis_index("grp").astype(i32).reshape(1)
    first = (lax.axis_index(both) * size).astype(i32).reshape(1)

    stepped, low_rim, high_rim = bottom_stepped(atmos_state)
    before, after = around(low_rim, high_rim)

    live = jnp.arange(block_ids.shape[1])[None, :] < block_counts[:, None]
    ids = jnp.where(live, block_ids, -1).reshape(2, 2, 64)
    ids = ids.transpose(1, 0, 2).reshape(2, LANES)
    request, rank = requests(ocean_cells, ids)

    slices = bottom_slices(stepped, before, after, neighbours, first, elements)
    table = exchange(slices, both)
    index = exchange(request, "blk")

    all_stepped, all_low, all_high = full_stepped(atmos_state)
    all_before, all_after = around(all_low, all_high)
    new_state = full_new_state(all_stepped, all_before, all_after, neighbours, first, elements)

    got = exchange(picked(table, index), both)
    sent = remapped_cells(grp, flux_weight, got, index, block_weights)
    ocean_flux = placed(exchange(sent, both), ocean_cells, rank)
    return new_state, ocean_flux


def solution(mesh):
    in_specs = (
        P(None, None, None, both),
        P(None, both),
        P(),
        P("blk", None, None, None),
        P("blk", None),
        P("blk"),
        P("blk"),
    )
    out_specs = (P(None, None, None, both), P("grp", "blk"))
    return jax.shard_map(body, mesh=mesh, in_specs=in_specs, out_specs=out_specs, check_vma=False)
```

```python
import functools

import jax
import jax.numpy as jnp
import ml_dtypes
import numpy as np
from jax import lax
from jax.experimental import pallas as pl
from jax.experimental.pallas import tpu as pltpu
from jax.sharding import PartitionSpec as P

time_step = 0.02
viscosity = 0.05
LANES = 128
REACH = 256
f32 = jnp.float32
bf16 = jnp.bfloat16
i32 = jnp.int32
both = ("grp", "blk")
vmem_bytes = 48 * 1024 * 1024


def params():
    return pltpu.CompilerParams(vmem_limit_bytes=vmem_bytes)


def cost(flops, moved):
    return pl.CostEstimate(flops=flops, bytes_accessed=moved, transcendentals=0)


def whole(shape):
    return pl.BlockSpec(shape, lambda *_: (0,) * len(shape))


def derivative_matrix():
    nodes = np.array([-1.0, -1.0 / np.sqrt(5.0), 1.0 / np.sqrt(5.0), 1.0])
    others = [[k for k in range(4) if k != n] for n in range(4)]
    weights = [np.prod([nodes[n] - nodes[k] for k in others[n]]) for n in range(4)]
    matrix = np.zeros((4, 4))
    for a in range(4):
        for c in range(4):
            if a != c:
                matrix[a, c] = weights[a] / weights[c] / (nodes[a] - nodes[c])
            else:
                matrix[a, a] = sum(1.0 / (nodes[a] - nodes[k]) for k in others[a])
    return matrix


def operators(copies):
    d = derivative_matrix().astype(np.float32).astype(np.float64)
    east, north = np.kron(np.eye(4), d), np.kron(d, np.eye(4))
    bend = east @ east + north @ north
    parts = [-time_step * east, -time_step * north, time_step * viscosity * bend]
    stacked = np.concatenate([np.kron(np.eye(copies), part) for part in parts])
    high = stacked.astype(ml_dtypes.bfloat16)
    low = (stacked - high.astype(np.float64)).astype(ml_dtypes.bfloat16)
    return jnp.asarray(high), jnp.asarray(low)


def split_two(x):
    high = x.astype(bf16)
    return high, (x - high.astype(f32)).astype(bf16)


def split_three(x):
    high = x.astype(bf16)
    rest = x - high.astype(f32)
    mid = rest.astype(bf16)
    return high, mid, (rest - mid.astype(f32)).astype(bf16)


def dot(a, b):
    return jnp.dot(a, b, preferred_element_type=f32)


def dot_nt(a, b):
    return lax.dot_general(a, b, (((1,), (1,)), ((), ())), preferred_element_type=f32)


def apply_operators(high, low, x):
    xh, xl = split_two(x)
    return dot(high, xh) + dot(high, xl) + dot(low, xh)


def iota(shape, dim):
    return lax.broadcasted_iota(i32, shape, dim)


def bottom_step(x_ref, high_ref, low_ref, out_ref, first_ref, last_ref):
    x = x_ref[:, 0].reshape(64, -1)
    op = apply_operators(high_ref[...], low_ref[...], x)
    size = x.shape[1]
    for v in range(4):
        rows = slice(16 * v, 16 * v + 16)
        stepped = (
            x[rows] + x[0:16] * op[rows] + x[16:32] * op[64:128][rows] + op[128:192][rows]
        )
        out_ref[v] = stepped
        first_ref[v] = stepped[:, :REACH]
        last_ref[v] = stepped[:, size - REACH :]


def bottom_stepped(state):
    nvar, levels, points, size = state.shape
    high, low = operators(nvar)
    shape = (nvar, points, size)
    rim = (nvar, points, REACH)
    return pl.pallas_call(
        bottom_step,
        grid=(1,),
        in_specs=[
            pl.BlockSpec((nvar, 1, points, size), lambda i: (0, levels - 1, 0, 0)),
            whole(high.shape),
            whole(low.shape),
        ],
        out_specs=[whole(shape), whole(rim), whole(rim)],
        out_shape=[jax.ShapeDtypeStruct(s, f32) for s in (shape, rim, rim)],
        compiler_params=pltpu.CompilerParams(vmem_limit_bytes=63 * 1024 * 1024),
        name="bottom_step",
    )(state, high, low)


def line_operators():
    d = derivative_matrix()
    d2 = d @ d
    slope = [
        (
            0.5 * (d[i, 0] - d[i, 3]),
            0.5 * (d[i, 1] - d[i, 2]),
            0.5 * (d[i, 0] + d[i, 3]),
        )
        for i in range(2)
    ]
    bend = [
        (
            0.5 * (d2[i, 0] - d2[i, 3]),
            0.5 * (d2[i, 1] - d2[i, 2]),
            0.5 * (d2[i, 0] + d2[i, 3]),
        )
        for i in range(2)
    ]
    return slope, bend


def along_line(x, slope, bend):
    t0, t1 = x[0] - x[3], x[1] - x[2]
    mean = (x[0] + x[3]) - (x[1] + x[2])
    first, second = [None] * 4, [None] * 4
    for i in range(2):
        a, b, c = [np.float32(-time_step * k) for k in slope[i]]
        even, odd = a * t0 + b * t1, c * mean
        first[i], first[3 - i] = even + odd, even - odd
        a, b, c = [np.float32(time_step * viscosity * k) for k in bend[i]]
        odd, even = a * t0 + b * t1, c * mean
        second[i], second[3 - i] = even + odd, even - odd
    return first, second


edge_points = (0, 1, 2, 3, 4, 7, 8, 11, 12, 13, 14, 15)


def full_step(x_ref, out_ref, first_ref, last_ref):
    step = pl.program_id(0)
    count = pl.num_programs(0)
    slope, bend = line_operators()

    def points(v, half):
        start = (v * 16 + half * 8) * 16
        return [x_ref[pl.ds(start + p, 8, stride=16), :] for p in range(16)]

    for half in range(2):
        u, w = points(0, half), points(1, half)
        for v in range(4):
            x = u if v == 0 else w if v == 1 else points(v, half)
            total = list(x)
            for a in range(4):
                at = [4 * a + b for b in range(4)]
                first, second = along_line([x[p] for p in at], slope, bend)
                for p, one, two in zip(at, first, second):
                    total[p] = total[p] + (u[p] * one + two)
            for b in range(4):
                at = [4 * a + b for a in range(4)]
                first, second = along_line([x[p] for p in at], slope, bend)
                for p, one, two in zip(at, first, second):
                    total[p] = total[p] + (w[p] * one + two)
            for p in range(16):
                out_ref[p, v * 16 + half * 8 : v * 16 + half * 8 + 8, :] = total[p]

    for part in range(2):
        cols = slice(part * LANES, (part + 1) * LANES)

        @pl.when(step == part)
        def _():
            for k, p in enumerate(edge_points):
                first_ref[k, :, cols] = out_ref[p].astype(bf16)

        @pl.when(step == count - 2 + part)
        def _():
            for k, p in enumerate(edge_points):
                last_ref[k, :, cols] = out_ref[p].astype(bf16)


def full_stepped(state):
    nvar, levels, points, size = state.shape
    rows = nvar * levels
    rim = (len(edge_points), rows, REACH)
    return pl.pallas_call(
        full_step,
        grid=(size // LANES,),
        in_specs=[pl.BlockSpec((rows * points, LANES), lambda i: (0, i))],
        out_specs=[
            pl.BlockSpec((points, rows, LANES), lambda i: (0, 0, i)),
            whole(rim),
            whole(rim),
        ],
        out_shape=[
            jax.ShapeDtypeStruct((points, rows, size), f32),
            jax.ShapeDtypeStruct(rim, bf16),
            jax.ShapeDtypeStruct(rim, bf16),
        ],
        compiler_params=params(),
        cost_estimate=cost(4 * 10**7, 9 << 20),
        name="full_step",
    )(state.reshape(rows * points, size))


def local_columns(nb_ref, first, elements):
    place = nb_ref[...] - first + REACH
    place = jnp.where(place < 0, place + elements, place)
    return jnp.where(place >= elements, place - elements, place)


def side_indices(place, rows, eb):
    cols = slice(eb * LANES, (eb + 1) * LANES)
    part = [jnp.broadcast_to(place[s : s + 1, cols], (rows, LANES)) for s in range(4)]
    point = iota((rows, LANES), 0) % 16
    we = jnp.where(point % 4 == 3, part[0], part[1])
    ns = jnp.where(point < 4, part[3], part[2])
    return we, ns


def edge_update(columns, we, ns, eb):
    own = columns[2]
    rows = own.shape[0]
    gathered = []
    for index in (we, ns):
        lane = index & (LANES - 1)
        column = (index >> 7) - eb
        value = jnp.take_along_axis(columns[0], lane, axis=1)
        for c in range(1, 5):
            value = jnp.where(
                column == c, jnp.take_along_axis(columns[c], lane, axis=1), value
            )
        gathered.append(value)
    point = iota(own.shape, 0) % 16
    b, a = point % 4, point // 4
    from_we, from_ns = gathered
    zero = jnp.zeros_like(own)
    total = jnp.where(b == 0, pltpu.roll(from_we, rows - 3, 0) - own, zero)
    total += jnp.where(b == 3, pltpu.roll(from_we, 3, 0) - own, zero)
    total += jnp.where(a == 0, pltpu.roll(from_ns, rows - 12, 0) - own, zero)
    total += jnp.where(a == 3, pltpu.roll(from_ns, 12, 0) - own, zero)
    return own + 0.5 * total


def window(own, before, after, eb):
    count = own.shape[-1] // LANES
    pieces = []
    for c in range(eb, eb + 5):
        if c < 2:
            piece = before[..., c * LANES : (c + 1) * LANES]
        elif c < 2 + count:
            piece = own[..., (c - 2) * LANES : (c - 1) * LANES]
        else:
            piece = after[..., (c - 2 - count) * LANES : (c - 1 - count) * LANES]
        pieces.append(piece)
    return pieces


def bottom_edges(
    elements, first_ref, s_ref, before_ref, after_ref, nb_ref, request_ref, out_ref
):
    out_ref[:, 0, 2 * LANES :] = request_ref[...]
    place = local_columns(nb_ref, first_ref[0], elements)
    own = s_ref[...].reshape(64, -1)
    before = before_ref[...].reshape(64, -1)
    after = after_ref[...].reshape(64, -1)
    count = own.shape[1] // LANES
    new = []
    for eb in range(count):
        we, ns = side_indices(place, 64, eb)
        new.append(edge_update(window(own, before, after, eb), we, ns, eb))
    for v in range(4):
        blocks = jnp.concatenate([piece[16 * v : 16 * v + 16] for piece in new], axis=0)
        turned = blocks.T
        out_ref[64 * v : 64 * v + 64, 0, :LANES] = turned[:64]
        out_ref[64 * v : 64 * v + 64, 0, LANES : 2 * LANES] = turned[64:]


def bottom_slices(stepped, before, after, neighbours, request, first, elements):
    shape = (256, 1, 3 * LANES)
    return pl.pallas_call(
        functools.partial(bottom_edges, elements),
        in_specs=[
            pl.BlockSpec(memory_space=pltpu.SMEM),
            pl.BlockSpec(memory_space=pltpu.VMEM),
            pl.BlockSpec(memory_space=pltpu.VMEM),
            pl.BlockSpec(memory_space=pltpu.VMEM),
            pl.BlockSpec(memory_space=pltpu.VMEM),
            pl.BlockSpec(memory_space=pltpu.VMEM),
        ],
        out_shape=jax.ShapeDtypeStruct(shape, f32),
        compiler_params=params(),
        name="bottom_edges",
    )(first, stepped, before, after, neighbours, request)


sides = (
    ((3, 7, 11, 15), (0, 4, 8, 12)),
    ((0, 4, 8, 12), (3, 7, 11, 15)),
    ((12, 13, 14, 15), (0, 1, 2, 3)),
    ((0, 1, 2, 3), (12, 13, 14, 15)),
)


def full_edges(
    elements, first_ref, s_ref, before_ref, after_ref, nb_ref, out_ref, split_ref, turn_ref
):
    step = pl.program_id(0)
    size = s_ref.shape[2]
    rows = s_ref.shape[1]

    @pl.when(step == 0)
    def _():
        for k, p in enumerate(edge_points):
            split_ref[0, p, :, :REACH] = before_ref[k]
            split_ref[1, p, :, :REACH] = jnp.zeros((rows, REACH), bf16)
            high, low = split_two(s_ref[p])
            split_ref[0, p, :, REACH : REACH + size] = high
            split_ref[1, p, :, REACH : REACH + size] = low
            split_ref[0, p, :, REACH + size :] = after_ref[k]
            split_ref[1, p, :, REACH + size :] = jnp.zeros((rows, REACH), bf16)

    place = local_columns(nb_ref, first_ref[0], elements) - step * REACH
    start = pl.multiple_of(step * REACH, REACH)
    own = [s_ref[p, :, pl.ds(start, REACH)] for p in range(16)]
    change = [None] * 16
    for side, (source, target) in enumerate(sides):
        onehot = jnp.where(
            iota((3 * REACH, REACH), 0) == place[side : side + 1, :], 1.0, 0.0
        ).astype(bf16)
        pieces = [
            split_ref[part, p, :, pl.ds(start, 3 * REACH)] for part in range(2) for p in source
        ]
        value = dot(jnp.concatenate(pieces, axis=0), onehot)
        for k, p in enumerate(target):
            there = value[k * rows : (k + 1) * rows] + value[(4 + k) * rows : (5 + k) * rows]
            part = there - own[p]
            change[p] = part if change[p] is None else change[p] + part
    for p in range(16):
        new = own[p] if change[p] is None else own[p] + 0.5 * change[p]
        for h in range(2):
            turn_ref[h, pl.ds(p, rows, stride=16), :] = new[:, h * LANES : (h + 1) * LANES]
    for h in range(2):
        out_ref[:, h * LANES : (h + 1) * LANES] = turn_ref[h]


def full_new_state(shape, stepped, before, after, neighbours, first, elements):
    points, rows, size = stepped.shape
    out = pl.pallas_call(
        functools.partial(full_edges, elements),
        grid=(size // REACH,),
        in_specs=[
            pl.BlockSpec(memory_space=pltpu.SMEM),
            whole(stepped.shape),
            whole(before.shape),
            whole(after.shape),
            pl.BlockSpec((4, REACH), lambda i: (0, i)),
        ],
        out_specs=pl.BlockSpec((rows * points, REACH), lambda i: (0, i)),
        out_shape=jax.ShapeDtypeStruct((rows * points, size), f32),
        scratch_shapes=[
            pltpu.VMEM((2, 16, rows, size + 2 * REACH), bf16),
            pltpu.VMEM((2, rows * points, LANES), f32),
        ],
        compiler_params=params(),
        cost_estimate=cost(4 * 10**9, 10 << 20),
        name="full_edges",
    )(first, stepped, before, after, neighbours)
    return out.reshape(shape)


def request_table(grp_ref, cells_ref, ids_ref, out_ref, rank_ref):
    chunks = cells_ref.shape[0]
    owner_at = iota((64, LANES), 0)
    strict = (iota((LANES, LANES), 0) < iota((LANES, LANES), 1)).astype(bf16)
    counted = jnp.zeros((64, 1), f32)
    high = jnp.zeros((64, 64), f32)
    low = jnp.zeros((64, 64), f32)
    for c in range(chunks):
        cell = cells_ref[c : c + 1, :]
        onehot = jnp.where(owner_at == (cell >> 11), 1.0, 0.0)
        earlier = dot(onehot.astype(bf16), strict) + counted
        counted = counted + jnp.sum(onehot, axis=1, keepdims=True)
        rank = jnp.sum(onehot * earlier, axis=0, keepdims=True).astype(i32)
        rank_ref[c : c + 1, :] = rank
        slot = jnp.where(owner_at == rank, 1.0, 0.0).astype(bf16)
        row = cell & 2047
        high += dot_nt((onehot * (row >> 7).astype(f32)).astype(bf16), slot)
        low += dot_nt((onehot * (row & 127).astype(f32)).astype(bf16), slot)
    wanted = high * 128.0 + low
    wanted = jnp.concatenate([wanted, wanted], axis=1)
    share = pltpu.roll(wanted, 64 - 12 * grp_ref[0], 1)
    message = jnp.where(iota((64, LANES), 1) < 64, ids_ref[...].astype(f32), share)
    for y in range(4):
        out_ref[64 * y : 64 * y + 64, :] = message


def requests(grp, ocean_cells, ids):
    chunks = ocean_cells.shape[0] // LANES
    vmem = pl.BlockSpec(memory_space=pltpu.VMEM)
    return pl.pallas_call(
        request_table,
        in_specs=[pl.BlockSpec(memory_space=pltpu.SMEM), vmem, vmem],
        out_shape=[
            jax.ShapeDtypeStruct((256, LANES), f32),
            jax.ShapeDtypeStruct((chunks, LANES), i32),
        ],
        compiler_params=params(),
        name="request_table",
    )(grp, ocean_cells.reshape(chunks, LANES), ids)


QUERIES = 512


def pick_values(table_ref, out_ref, cells_ref, turned_ref, ids_ref, found_ref):
    lane = iota((LANES, LANES), 1)
    asked = table_ref[:, 0, 2 * LANES :]
    ids = jnp.where(lane < 64, asked[:LANES], pltpu.roll(asked[LANES:], 64, 1))
    ids_ref[...] = ids.astype(i32)
    lane = iota((64, LANES), 1)
    wanted = jnp.zeros((64, LANES), f32)
    for y in range(4):
        part = pltpu.roll(asked[64 * y : 64 * y + 64], 64 + 12 * y, 1)
        wanted = jnp.where((lane >= 12 * y) & (lane < 12 * y + 12), part, wanted)
    lane = iota((32, LANES), 1)
    cells_ref[...] = jnp.where(lane < 64, wanted[:32], pltpu.roll(wanted[32:], 64, 1)).astype(i32)

    high, low = split_two(table_ref[:, 0, : 2 * LANES].T)
    turned_ref[:256] = high
    turned_ref[256:] = low
    groups = QUERIES // LANES
    device_at = iota((256, QUERIES), 0)
    block_at = iota((LANES, QUERIES), 0)

    def some(step, carry):
        rows = [ids_ref[pl.ds(groups * step + k, 1), :] for k in range(groups)]
        asked = jnp.concatenate(rows, axis=1)
        onehot = jnp.where(device_at == (asked >> 7), 1.0, 0.0).astype(bf16)
        value = dot(turned_ref[...], onehot)
        hit = block_at == (asked & 127)
        for half in range(2):
            at = half * LANES
            part = value[at : at + LANES] + value[256 + at : 256 + at + LANES]
            found = jnp.sum(jnp.where(hit, part, 0.0), axis=0, keepdims=True)
            for k in range(groups):
                found_ref[half, pl.ds(groups * step + k, 1), :] = found[
                    :, k * LANES : (k + 1) * LANES
                ]
        return carry

    lax.fori_loop(0, LANES // groups, some, 0, unroll=8)
    lane = iota((LANES, LANES), 1)
    first, second = found_ref[0], found_ref[1]
    out_ref[:LANES, 0, :] = jnp.where(lane < 64, first, pltpu.roll(second, 64, 1))
    out_ref[LANES:, 0, :] = jnp.where(lane < 64, pltpu.roll(first, 64, 1), second)


def picked(table):
    return pl.pallas_call(
        pick_values,
        out_shape=[
            jax.ShapeDtypeStruct((256, 1, LANES), f32),
            jax.ShapeDtypeStruct((32, LANES), i32),
        ],
        scratch_shapes=[
            pltpu.VMEM((512, 256), bf16),
            pltpu.VMEM((LANES, LANES), i32),
            pltpu.VMEM((2, LANES, LANES), f32),
        ],
        compiler_params=params(),
        name="pick_values",
    )(table)


def remap_rows(
    grp_ref, fw_ref, got_ref, index_ref, w_ref, out_ref, field_ref, mapped_ref, sent_ref
):
    step = pl.program_id(0)

    @pl.when(step == 0)
    def _():
        values = []
        for v in range(4):
            turned = got_ref[64 * v : 64 * v + 64, 0, :].T
            values.append(jnp.concatenate([turned[:64], turned[64:]], axis=1))
        wind = jnp.sqrt(1.0 + values[0] * values[0] + values[1] * values[1])
        for f in range(16):
            if f < 12:
                total = fw_ref[f, 0] * values[0]
                for v in range(1, 4):
                    total += fw_ref[f, v] * values[v]
                total = (total * wind).astype(bf16).astype(f32)
            else:
                total = jnp.zeros((64, LANES), f32)
            field_ref[pl.ds(f, 64, stride=16), :] = total

    total = jnp.zeros((16, LANES), f32)
    for b in range(0, 16, 2):
        at = pl.multiple_of((step * 16 + b) * 16, 32)
        pair = field_ref[pl.ds(at, 32), :].astype(bf16)
        pair = jnp.concatenate([pair[:16], pair[16:]], axis=1)
        weights = jnp.concatenate([w_ref[0, b], w_ref[0, b + 1]], axis=1)
        total += dot_nt(pair, weights)
    mapped_ref[:, pl.ds(pl.multiple_of(step * LANES, LANES), LANES)] = total

    @pl.when(step == pl.num_programs(0) - 1)
    def _():
        parts = jnp.concatenate(split_three(mapped_ref[...]), axis=0)
        row_at = iota((512, 4 * LANES), 0) + grp_ref[0] * 512

        def some(at, carry):
            rows = [index_ref[pl.ds(4 * at + k, 1), :] for k in range(4)]
            onehot = jnp.where(row_at == jnp.concatenate(rows, axis=1), 1.0, 0.0).astype(bf16)
            value = dot(parts, onehot)
            value = value[0:16] + value[16:32] + value[32:48]
            for k in range(4):
                sent_ref[pl.ds(4 * at + k, 16, stride=32), :] = value[
                    :, k * LANES : (k + 1) * LANES
                ]
            return carry

        lax.fori_loop(0, 8, some, 0, unroll=True)
        lane = iota((32, LANES), 1)
        for y in range(4):
            a, b, c = [sent_ref[(3 * y + f) * 32 : (3 * y + f) * 32 + 32, :] for f in range(3)]
            base = 64 * y
            low, high = slice(base, base + 32), slice(base + 32, base + 64)
            out_ref[low, 0, :LANES] = jnp.where(lane < 64, a, pltpu.roll(b, 64, 1))
            out_ref[low, 0, LANES:] = c
            out_ref[high, 0, :LANES] = jnp.where(lane < 64, pltpu.roll(a, 64, 1), b)
            out_ref[high, 0, LANES:] = pltpu.roll(c, 64, 1)


def remapped_cells(grp, flux_weight, got, index, block_weights):
    slots, block = block_weights.shape[1], block_weights.shape[2]
    grid_spec = pltpu.PrefetchScalarGridSpec(
        num_scalar_prefetch=1,
        grid=(4,),
        in_specs=[
            pl.BlockSpec(memory_space=pltpu.SMEM),
            whole(got.shape),
            whole(index.shape),
            pl.BlockSpec((1, slots, block, block), lambda i, g: (4 * g[0] + i, 0, 0, 0)),
        ],
        out_specs=whole((256, 1, 2 * LANES)),
        scratch_shapes=[
            pltpu.VMEM((64 * 16, LANES), f32),
            pltpu.VMEM((16, 512), f32),
            pltpu.VMEM((16 * 32, LANES), f32),
        ],
    )
    return pl.pallas_call(
        remap_rows,
        grid_spec=grid_spec,
        out_shape=jax.ShapeDtypeStruct((256, 1, 2 * LANES), f32),
        compiler_params=params(),
        name="remap_rows",
    )(grp, flux_weight, got, index, block_weights)


def place_cells(got_ref, cells_ref, rank_ref, out_ref):
    got = got_ref[:, 0, :]
    table = got[0:64] + got[64:128] + got[128:192] + got[192:256]
    parts = jnp.concatenate(split_three(table[:, :192].T), axis=1)
    owner_at = iota((64, 4 * LANES), 0)
    for c in range(4):
        rows = range(4 * c, 4 * c + 4)
        cell = jnp.concatenate([cells_ref[r : r + 1, :] for r in rows], axis=1)
        rank = jnp.concatenate([rank_ref[r : r + 1, :] for r in rows], axis=1)
        onehot = jnp.where(owner_at == (cell >> 11), 1.0, 0.0).astype(bf16)
        value = dot(parts, jnp.concatenate([onehot] * 3, axis=0))
        hit = owner_at == rank
        for f in range(3):
            out_ref[f : f + 1, c * 4 * LANES : (c + 1) * 4 * LANES] = jnp.sum(
                jnp.where(hit, value[64 * f : 64 * f + 64], 0.0), axis=0, keepdims=True
            )


def placed(got, ocean_cells, rank):
    count = ocean_cells.shape[0]
    return pl.pallas_call(
        place_cells,
        out_shape=jax.ShapeDtypeStruct((3, count), f32),
        compiler_params=params(),
        name="place_cells",
    )(got, ocean_cells.reshape(count // LANES, LANES), rank)


def around(first, last):
    count = lax.axis_size(both)
    up = [(i, (i + 1) % count) for i in range(count)]
    down = [(j, i) for i, j in up]
    return lax.ppermute(last, both, up), lax.ppermute(first, both, down)


def exchange(x, axis):
    return lax.all_to_all(x, axis, split_axis=0, concat_axis=0, tiled=True)


def body(atmos_state, neighbours, flux_weight, block_weights, block_ids, block_counts, ocean_cells):
    size = atmos_state.shape[3]
    elements = size * lax.axis_size(both)
    grp = lax.axis_index("grp").astype(i32).reshape(1)
    first = (lax.axis_index(both) * size).astype(i32).reshape(1)

    stepped, low_rim, high_rim = bottom_stepped(atmos_state)
    before, after = around(low_rim, high_rim)

    live = jnp.arange(block_ids.shape[1])[None, :] < block_counts[:, None]
    ids = jnp.where(live, block_ids, -1).reshape(4, 64)
    ids = lax.dynamic_slice_in_dim(ids, lax.axis_index("grp"), 1, 0)
    ids = jnp.concatenate([ids, ids], axis=1)
    request, rank = requests(grp, ocean_cells, ids)

    slices = bottom_slices(stepped, before, after, neighbours, request, first, elements)
    table = exchange(slices, both)

    all_stepped, all_low, all_high = full_stepped(atmos_state)
    all_before, all_after = around(all_low, all_high)
    new_state = full_new_state(
        atmos_state.shape, all_stepped, all_before, all_after, neighbours, first, elements
    )

    answer, wanted = picked(table)
    got = exchange(answer, both)
    sent = remapped_cells(grp, flux_weight, got, wanted, block_weights)
    ocean_flux = placed(exchange(sent, both), ocean_cells, rank)
    return new_state, ocean_flux


def solution(mesh):
    in_specs = (
        P(None, None, None, both),
        P(None, both),
        P(),
        P("blk", None, None, None),
        P("blk", None),
        P("blk"),
        P("blk"),
    )
    out_specs = (P(None, None, None, both), P("grp", "blk"))
    return jax.shard_map(body, mesh=mesh, in_specs=in_specs, out_specs=out_specs, check_vma=False)
```

```python
import functools

import jax
import jax.numpy as jnp
import ml_dtypes
import numpy as np
from jax import lax
from jax.experimental import pallas as pl
from jax.experimental.pallas import tpu as pltpu
from jax.sharding import PartitionSpec as P

time_step = 0.02
viscosity = 0.05
LANES = 128
REACH = 256
f32 = jnp.float32
bf16 = jnp.bfloat16
i32 = jnp.int32
both = ("grp", "blk")


def params(mebibytes=16):
    return pltpu.CompilerParams(vmem_limit_bytes=mebibytes * 1024 * 1024)


def in_hbm(x):
    return pltpu.with_memory_space_constraint(x, pltpu.HBM)


def cost(flops, moved):
    return pl.CostEstimate(flops=flops, bytes_accessed=moved, transcendentals=0)


def whole(shape):
    return pl.BlockSpec(shape, lambda *_: (0,) * len(shape))


def derivative_matrix():
    nodes = np.array([-1.0, -1.0 / np.sqrt(5.0), 1.0 / np.sqrt(5.0), 1.0])
    others = [[k for k in range(4) if k != n] for n in range(4)]
    weights = [np.prod([nodes[n] - nodes[k] for k in others[n]]) for n in range(4)]
    matrix = np.zeros((4, 4))
    for a in range(4):
        for c in range(4):
            if a != c:
                matrix[a, c] = weights[a] / weights[c] / (nodes[a] - nodes[c])
            else:
                matrix[a, a] = sum(1.0 / (nodes[a] - nodes[k]) for k in others[a])
    return matrix


def operators(copies):
    d = derivative_matrix().astype(np.float32).astype(np.float64)
    east, north = np.kron(np.eye(4), d), np.kron(d, np.eye(4))
    bend = east @ east + north @ north
    parts = [-time_step * east, -time_step * north, time_step * viscosity * bend]
    stacked = np.concatenate([np.kron(np.eye(copies), part) for part in parts])
    high = stacked.astype(ml_dtypes.bfloat16)
    low = (stacked - high.astype(np.float64)).astype(ml_dtypes.bfloat16)
    return jnp.asarray(high), jnp.asarray(low)


def split_two(x):
    high = x.astype(bf16)
    return high, (x - high.astype(f32)).astype(bf16)


def dot(a, b):
    return jnp.dot(a, b, preferred_element_type=f32)


def dot_nt(a, b):
    return lax.dot_general(a, b, (((1,), (1,)), ((), ())), preferred_element_type=f32)


def apply_operators(high, low, x):
    xh, xl = split_two(x)
    return dot(high, xh) + dot(high, xl) + dot(low, xh)


def iota(shape, dim):
    return lax.broadcasted_iota(i32, shape, dim)


def bottom_step(x_ref, high_ref, low_ref, out_ref, first_ref, last_ref):
    x = x_ref[:, 0].reshape(64, -1)
    op = apply_operators(high_ref[...], low_ref[...], x)
    size = x.shape[1]
    for v in range(4):
        rows = slice(16 * v, 16 * v + 16)
        stepped = (
            x[rows] + x[0:16] * op[rows] + x[16:32] * op[64:128][rows] + op[128:192][rows]
        )
        out_ref[v] = stepped
        first_ref[v] = stepped[:, :REACH]
        last_ref[v] = stepped[:, size - REACH :]


def bottom_stepped(state):
    nvar, levels, points, size = state.shape
    high, low = operators(nvar)
    shape = (nvar, points, size)
    rim = (nvar, points, REACH)
    return pl.pallas_call(
        bottom_step,
        grid=(1,),
        in_specs=[
            pl.BlockSpec((nvar, 1, points, size), lambda i: (0, levels - 1, 0, 0)),
            whole(high.shape),
            whole(low.shape),
        ],
        out_specs=[pl.BlockSpec(memory_space=pltpu.VMEM), whole(rim), whole(rim)],
        out_shape=[
            pltpu.VMEM(shape, f32),
            jax.ShapeDtypeStruct(rim, f32),
            jax.ShapeDtypeStruct(rim, f32),
        ],
        compiler_params=params(),
        name="bottom_step",
    )(in_hbm(state), in_hbm(high), in_hbm(low))


def line_operators():
    d = derivative_matrix()
    d2 = d @ d
    slope = [
        (
            0.5 * (d[i, 0] - d[i, 3]),
            0.5 * (d[i, 1] - d[i, 2]),
            0.5 * (d[i, 0] + d[i, 3]),
        )
        for i in range(2)
    ]
    bend = [
        (
            0.5 * (d2[i, 0] - d2[i, 3]),
            0.5 * (d2[i, 1] - d2[i, 2]),
            0.5 * (d2[i, 0] + d2[i, 3]),
        )
        for i in range(2)
    ]
    return slope, bend


def along_line(x, slope, bend):
    t0, t1 = x[0] - x[3], x[1] - x[2]
    mean = (x[0] + x[3]) - (x[1] + x[2])
    first, second = [None] * 4, [None] * 4
    for i in range(2):
        a, b, c = [np.float32(-time_step * k) for k in slope[i]]
        even, odd = a * t0 + b * t1, c * mean
        first[i], first[3 - i] = even + odd, even - odd
        a, b, c = [np.float32(time_step * viscosity * k) for k in bend[i]]
        odd, even = a * t0 + b * t1, c * mean
        second[i], second[3 - i] = even + odd, even - odd
    return first, second


edge_points = (0, 1, 2, 3, 4, 7, 8, 11, 12, 13, 14, 15)


def full_step(x_ref, out_ref, first_ref, last_ref):
    step = pl.program_id(0)
    count = pl.num_programs(0)
    slope, bend = line_operators()

    def points(v, half):
        start = (v * 16 + half * 8) * 16
        return [x_ref[pl.ds(start + p, 8, stride=16), :] for p in range(16)]

    for half in range(2):
        u, w = points(0, half), points(1, half)
        for v in range(4):
            x = u if v == 0 else w if v == 1 else points(v, half)
            total = list(x)
            for a in range(4):
                at = [4 * a + b for b in range(4)]
                first, second = along_line([x[p] for p in at], slope, bend)
                for p, one, two in zip(at, first, second):
                    total[p] = total[p] + (u[p] * one + two)
            for b in range(4):
                at = [4 * a + b for a in range(4)]
                first, second = along_line([x[p] for p in at], slope, bend)
                for p, one, two in zip(at, first, second):
                    total[p] = total[p] + (w[p] * one + two)
            for p in range(16):
                out_ref[p, v * 16 + half * 8 : v * 16 + half * 8 + 8, :] = total[p]

    for part in range(2):
        cols = slice(part * LANES, (part + 1) * LANES)

        @pl.when(step == part)
        def _():
            for k, p in enumerate(edge_points):
                first_ref[k, :, cols] = out_ref[p].astype(bf16)

        @pl.when(step == count - 2 + part)
        def _():
            for k, p in enumerate(edge_points):
                last_ref[k, :, cols] = out_ref[p].astype(bf16)


def full_stepped(state):
    nvar, levels, points, size = state.shape
    rows = nvar * levels
    rim = (len(edge_points), rows, REACH)
    return pl.pallas_call(
        full_step,
        grid=(size // LANES,),
        in_specs=[pl.BlockSpec((rows * points, LANES), lambda i: (0, i))],
        out_specs=[
            pl.BlockSpec((points, rows, LANES), lambda i: (0, 0, i)),
            whole(rim),
            whole(rim),
        ],
        out_shape=[
            pltpu.HBM((points, rows, size), f32),
            jax.ShapeDtypeStruct(rim, bf16),
            jax.ShapeDtypeStruct(rim, bf16),
        ],
        compiler_params=params(24),
        cost_estimate=cost(4 * 10**7, 9 << 20),
        name="full_step",
    )(in_hbm(state.reshape(rows * points, size)))


def local_columns(nb_ref, first, elements):
    place = nb_ref[...] - first + REACH
    place = jnp.where(place < 0, place + elements, place)
    return jnp.where(place >= elements, place - elements, place)


def side_indices(place, rows, eb):
    cols = slice(eb * LANES, (eb + 1) * LANES)
    part = [jnp.broadcast_to(place[s : s + 1, cols], (rows, LANES)) for s in range(4)]
    point = iota((rows, LANES), 0) % 8
    we = jnp.where(point % 4 == 3, part[0], part[1])
    ns = jnp.where(point < 4, part[3], part[2])
    return we, ns


def look_up(columns, index, eb):
    lane = index & (LANES - 1)
    column = (index >> 7) - eb
    value = jnp.take_along_axis(columns[0], lane, axis=1)
    for c in range(1, 5):
        value = jnp.where(column == c, jnp.take_along_axis(columns[c], lane, axis=1), value)
    return value


def halves(x):
    grouped = x.reshape(x.shape[0] // 16, 2, 8, x.shape[1])
    shape = (x.shape[0] // 2, x.shape[1])
    return grouped[:, 0].reshape(shape), grouped[:, 1].reshape(shape)


def edge_update(columns, we, ns, eb):
    pairs = [halves(column) for column in columns]
    rows = pairs[0][0].shape[0]
    point = iota(pairs[0][0].shape, 0) % 8
    first = point < 4
    across = look_up([jnp.where(first, low, high) for low, high in pairs], ns, eb)
    zero = jnp.zeros(first.shape, f32)
    done = []
    for side in range(2):
        own = pairs[2][side]
        beside = look_up([pair[side] for pair in pairs], we, eb)
        total = jnp.where(point % 4 == 0, pltpu.roll(beside, rows - 3, 0) - own, zero)
        total += jnp.where(point % 4 == 3, pltpu.roll(beside, 3, 0) - own, zero)
        if side == 0:
            total += jnp.where(first, pltpu.roll(across, rows - 4, 0) - own, zero)
        else:
            total += jnp.where(first, zero, pltpu.roll(across, 4, 0) - own)
        done.append((own + 0.5 * total).reshape(-1, 1, 8, own.shape[1]))
    return jnp.concatenate(done, axis=1).reshape(columns[0].shape)


def window(own, before, after, eb):
    count = own.shape[-1] // LANES
    pieces = []
    for c in range(eb, eb + 5):
        if c < 2:
            piece = before[..., c * LANES : (c + 1) * LANES]
        elif c < 2 + count:
            piece = own[..., (c - 2) * LANES : (c - 1) * LANES]
        else:
            piece = after[..., (c - 2 - count) * LANES : (c - 1 - count) * LANES]
        pieces.append(piece)
    return pieces


def bottom_edges(
    elements, first_ref, s_ref, before_ref, after_ref, nb_ref, request_ref, out_ref
):
    out_ref[:, 0, 2 * LANES :] = request_ref[...]
    place = local_columns(nb_ref, first_ref[0], elements)
    own = s_ref[...].reshape(64, -1)
    before = before_ref[...].reshape(64, -1)
    after = after_ref[...].reshape(64, -1)
    count = own.shape[1] // LANES
    new = []
    for eb in range(count):
        we, ns = side_indices(place, 32, eb)
        new.append(edge_update(window(own, before, after, eb), we, ns, eb))
    for v in range(4):
        blocks = jnp.concatenate([piece[16 * v : 16 * v + 16] for piece in new], axis=0)
        turned = blocks.T
        out_ref[64 * v : 64 * v + 64, 0, :LANES] = turned[:64]
        out_ref[64 * v : 64 * v + 64, 0, LANES : 2 * LANES] = turned[64:]


def bottom_slices(stepped, before, after, neighbours, request, first, elements):
    shape = (256, 1, 3 * LANES)
    return pl.pallas_call(
        functools.partial(bottom_edges, elements),
        in_specs=[
            pl.BlockSpec(memory_space=pltpu.SMEM),
            pl.BlockSpec(memory_space=pltpu.VMEM),
            pl.BlockSpec(memory_space=pltpu.VMEM),
            pl.BlockSpec(memory_space=pltpu.VMEM),
            pl.BlockSpec(memory_space=pltpu.VMEM),
            pl.BlockSpec(memory_space=pltpu.VMEM),
        ],
        out_shape=jax.ShapeDtypeStruct(shape, f32),
        compiler_params=params(),
        name="bottom_edges",
    )(first, stepped, before, after, neighbours, request)


sides = (
    ((3, 7, 11, 15), (0, 4, 8, 12)),
    ((0, 4, 8, 12), (3, 7, 11, 15)),
    ((12, 13, 14, 15), (0, 1, 2, 3)),
    ((0, 1, 2, 3), (12, 13, 14, 15)),
)


def full_edges(
    elements,
    first_ref,
    ahead_ref,
    own_ref,
    before_ref,
    after_ref,
    nb_ref,
    out_ref,
    split_ref,
    turn_ref,
):
    step = pl.program_id(0)
    tiles = pl.num_programs(0) - 1
    rows = own_ref.shape[1]
    empty = jnp.zeros((rows, REACH), bf16)

    @pl.when(step == 0)
    def _():
        for k, p in enumerate(edge_points):
            split_ref[0, p, :, :REACH] = before_ref[k]
            split_ref[1, p, :, :REACH] = empty

    place_at = pl.multiple_of((step + 1) * REACH, REACH)

    @pl.when(step < tiles)
    def _():
        for p in edge_points:
            high, low = split_two(ahead_ref[p])
            split_ref[0, p, :, pl.ds(place_at, REACH)] = high
            split_ref[1, p, :, pl.ds(place_at, REACH)] = low

    @pl.when(step == tiles)
    def _():
        for k, p in enumerate(edge_points):
            split_ref[0, p, :, pl.ds(place_at, REACH)] = after_ref[k]
            split_ref[1, p, :, pl.ds(place_at, REACH)] = empty

    @pl.when(step > 0)
    def _():
        place = local_columns(nb_ref, first_ref[0], elements) - (step - 1) * REACH
        start = pl.multiple_of((step - 1) * REACH, REACH)
        change = [None] * 16
        for side, (source, target) in enumerate(sides):
            onehot = jnp.where(
                iota((3 * REACH, REACH), 0) == place[side : side + 1, :], 1.0, 0.0
            ).astype(bf16)
            pieces = [
                split_ref[part, p, :, pl.ds(start, 3 * REACH)]
                for part in range(2)
                for p in source
            ]
            value = dot(jnp.concatenate(pieces, axis=0), onehot)
            for k, p in enumerate(target):
                there = value[k * rows : (k + 1) * rows] + value[(4 + k) * rows : (5 + k) * rows]
                part = there - own_ref[p]
                change[p] = part if change[p] is None else change[p] + part
        for p in range(16):
            new = own_ref[p] if change[p] is None else own_ref[p] + 0.5 * change[p]
            for h in range(2):
                turn_ref[h, pl.ds(p, rows, stride=16), :] = new[:, h * LANES : (h + 1) * LANES]
        for h in range(2):
            out_ref[:, h * LANES : (h + 1) * LANES] = turn_ref[h]


def full_new_state(shape, stepped, before, after, neighbours, first, elements):
    points, rows, size = stepped.shape
    tiles = size // REACH
    tile = (points, rows, REACH)
    out = pl.pallas_call(
        functools.partial(full_edges, elements),
        grid=(tiles + 1,),
        in_specs=[
            pl.BlockSpec(memory_space=pltpu.SMEM),
            pl.BlockSpec(tile, lambda i: (0, 0, jnp.minimum(i, tiles - 1))),
            pl.BlockSpec(tile, lambda i: (0, 0, jnp.maximum(i - 1, 0))),
            whole(before.shape),
            whole(after.shape),
            pl.BlockSpec((4, REACH), lambda i: (0, jnp.maximum(i - 1, 0))),
        ],
        out_specs=pl.BlockSpec((rows * points, REACH), lambda i: (0, jnp.maximum(i - 1, 0))),
        out_shape=jax.ShapeDtypeStruct((rows * points, size), f32),
        scratch_shapes=[
            pltpu.VMEM((2, 16, rows, size + 2 * REACH), bf16),
            pltpu.VMEM((2, rows * points, LANES), f32),
        ],
        compiler_params=params(24),
        cost_estimate=cost(4 * 10**9, 10 << 20),
        name="full_edges",
    )(first, in_hbm(stepped), in_hbm(stepped), before, after, neighbours)
    return out.reshape(shape)


def request_table(grp_ref, cells_ref, ids_ref, out_ref, rank_ref):
    chunks = cells_ref.shape[0]
    owner_at = iota((64, LANES), 0)
    cells = [cells_ref[c : c + 1, :] for c in range(chunks)]
    mine = [jnp.where(owner_at == (cell >> 11), 1.0, 0.0) for cell in cells]
    before = jnp.where(iota((LANES, 2 * LANES), 0) < iota((LANES, 2 * LANES), 1), 1.0, 0.0)
    counts = dot(jnp.concatenate(mine, axis=0).astype(bf16), before.astype(bf16))
    carried = jnp.zeros((64, LANES), f32)
    slots, high, low = [], [], []
    for c, cell in enumerate(cells):
        count = counts[64 * c : 64 * c + 64]
        rank = jnp.sum(mine[c] * (count[:, :LANES] + carried), axis=0, keepdims=True).astype(i32)
        carried = carried + count[:, LANES:]
        rank_ref[c : c + 1, :] = rank
        slots.append(jnp.where(owner_at == rank, 1.0, 0.0).astype(bf16))
        row = cell & 2047
        high.append((mine[c] * (row >> 7).astype(f32)).astype(bf16))
        low.append((mine[c] * (row & 127).astype(f32)).astype(bf16))
    parts = jnp.concatenate([jnp.concatenate(p, axis=1) for p in (high, low)], axis=0)
    wanted = dot_nt(parts, jnp.concatenate(slots, axis=1))
    wanted = wanted[:64] * 128.0 + wanted[64:]
    wanted = jnp.concatenate([wanted, wanted], axis=1)
    share = pltpu.roll(wanted, 64 - 12 * grp_ref[0], 1)
    message = jnp.where(iota((64, LANES), 1) < 64, ids_ref[...].astype(f32), share)
    for y in range(4):
        out_ref[64 * y : 64 * y + 64, :] = message


def requests(grp, ocean_cells, ids):
    chunks = ocean_cells.shape[0] // LANES
    vmem = pl.BlockSpec(memory_space=pltpu.VMEM)
    return pl.pallas_call(
        request_table,
        in_specs=[pl.BlockSpec(memory_space=pltpu.SMEM), vmem, vmem],
        out_shape=[
            jax.ShapeDtypeStruct((256, LANES), f32),
            jax.ShapeDtypeStruct((chunks, LANES), i32),
        ],
        compiler_params=params(),
        name="request_table",
    )(grp, ocean_cells.reshape(chunks, LANES), ids)


QUERIES = 512


def pick_values(table_ref, out_ref, cells_ref, turned_ref, ids_ref, found_ref):
    lane = iota((LANES, LANES), 1)
    asked = table_ref[:, 0, 2 * LANES :]
    ids = jnp.where(lane < 64, asked[:LANES], pltpu.roll(asked[LANES:], 64, 1))
    ids_ref[...] = ids.astype(i32)
    lane = iota((64, LANES), 1)
    wanted = jnp.zeros((64, LANES), f32)
    for y in range(4):
        part = pltpu.roll(asked[64 * y : 64 * y + 64], 64 + 12 * y, 1)
        wanted = jnp.where((lane >= 12 * y) & (lane < 12 * y + 12), part, wanted)
    lane = iota((32, LANES), 1)
    cells_ref[...] = jnp.where(lane < 64, wanted[:32], pltpu.roll(wanted[32:], 64, 1)).astype(i32)

    high, low = split_two(table_ref[:, 0, : 2 * LANES].T)
    turned_ref[:256] = high
    turned_ref[256:] = low
    groups = QUERIES // LANES
    device_at = iota((256, QUERIES), 0)
    block_at = iota((LANES, QUERIES), 0)

    def some(step, carry):
        rows = [ids_ref[pl.ds(groups * step + k, 1), :] for k in range(groups)]
        asked = jnp.concatenate(rows, axis=1)
        onehot = jnp.where(device_at == (asked >> 7), 1.0, 0.0).astype(bf16)
        value = dot(turned_ref[...], onehot)
        hit = block_at == (asked & 127)
        for half in range(2):
            at = half * LANES
            part = value[at : at + LANES] + value[256 + at : 256 + at + LANES]
            found = jnp.sum(jnp.where(hit, part, 0.0), axis=0, keepdims=True)
            for k in range(groups):
                found_ref[half, pl.ds(groups * step + k, 1), :] = found[
                    :, k * LANES : (k + 1) * LANES
                ]
        return carry

    lax.fori_loop(0, LANES // groups, some, 0, unroll=16)
    lane = iota((LANES, LANES), 1)
    first, second = found_ref[0], found_ref[1]
    out_ref[:LANES, 0, :] = jnp.where(lane < 64, first, pltpu.roll(second, 64, 1))
    out_ref[LANES:, 0, :] = jnp.where(lane < 64, pltpu.roll(first, 64, 1), second)


def picked(table):
    return pl.pallas_call(
        pick_values,
        out_shape=[
            pltpu.HBM((256, 1, LANES), f32),
            jax.ShapeDtypeStruct((32, LANES), i32),
        ],
        scratch_shapes=[
            pltpu.VMEM((512, 256), bf16),
            pltpu.VMEM((LANES, LANES), i32),
            pltpu.VMEM((2, LANES, LANES), f32),
        ],
        compiler_params=params(24),
        name="pick_values",
    )(table)


def remap_rows(
    grp_ref,
    fw_ref,
    got_ref,
    index_ref,
    w_ref,
    out_ref,
    field_ref,
    mapped_ref,
    sent_ref,
    pair_ref,
):
    step = pl.program_id(0)

    @pl.when(step == 0)
    def _():
        values = []
        for v in range(4):
            turned = got_ref[64 * v : 64 * v + 64, 0, :].T
            values.append(jnp.concatenate([turned[:64], turned[64:]], axis=1))
        wind = jnp.sqrt(1.0 + values[0] * values[0] + values[1] * values[1])
        for f in range(16):
            if f < 12:
                total = fw_ref[f, 0] * values[0]
                for v in range(1, 4):
                    total += fw_ref[f, v] * values[v]
                total = (total * wind).astype(bf16).astype(f32)
            else:
                total = jnp.zeros((64, LANES), f32)
            field_ref[pl.ds(f, 64, stride=16), :] = total

    total = jnp.zeros((16, LANES), f32)
    for b in range(0, 16, 2):
        at = pl.multiple_of((step * 16 + b) * 16, 32)
        pair = field_ref[pl.ds(at, 32), :].astype(bf16)
        pair = jnp.concatenate([pair[:16], pair[16:]], axis=1)
        weights = jnp.concatenate([w_ref[0, b], w_ref[0, b + 1]], axis=1)
        total += dot_nt(pair, weights)
    mapped_ref[pl.ds(pl.multiple_of(step * 16, 16), 16), :] = total

    @pl.when(step == pl.num_programs(0) - 1)
    def _():
        parts = jnp.concatenate(split_two(mapped_ref[...]), axis=0)
        row_at = iota((LANES, 4 * LANES), 0)

        def some(at, carry):
            rows = [index_ref[pl.ds(4 * at + k, 1), :] for k in range(4)]
            asked = jnp.concatenate(rows, axis=1)
            onehot = jnp.where(row_at == (asked & 127), 1.0, 0.0).astype(bf16)
            value = dot(parts, onehot)
            value = value[:64] + value[64:]
            block = (asked >> 7) - 4 * grp_ref[0]
            found = jnp.where(block == 0, value[:16], 0.0)
            for r in range(1, 4):
                found = jnp.where(block == r, value[16 * r : 16 * r + 16], found)
            for k in range(4):
                sent_ref[pl.ds(4 * at + k, 16, stride=32), :] = found[
                    :, k * LANES : (k + 1) * LANES
                ]
            return carry

        lax.fori_loop(0, 8, some, 0, unroll=True)
        lane = iota((32, LANES), 1)
        for y in range(4):
            a, b, c = [sent_ref[(3 * y + f) * 32 : (3 * y + f) * 32 + 32, :] for f in range(3)]
            base = 64 * y
            low, high = slice(base, base + 32), slice(base + 32, base + 64)
            pair_ref[low, 0, :] = jnp.where(lane < 64, a, pltpu.roll(b, 64, 1))
            pair_ref[low, 1, :] = c
            pair_ref[high, 0, :] = jnp.where(lane < 64, pltpu.roll(a, 64, 1), b)
            pair_ref[high, 1, :] = pltpu.roll(c, 64, 1)
        out_ref[...] = pair_ref[...].astype(bf16)


def remapped_cells(grp, flux_weight, got, index, block_weights):
    count, slots, block = block_weights.shape[:3]
    smem = pl.BlockSpec(memory_space=pltpu.SMEM)
    return pl.pallas_call(
        remap_rows,
        grid=(count,),
        in_specs=[
            smem,
            smem,
            whole(got.shape),
            whole(index.shape),
            pl.BlockSpec((1, slots, block, block), lambda i: (i, 0, 0, 0)),
        ],
        out_specs=whole((256, 2, LANES)),
        out_shape=jax.ShapeDtypeStruct((256, 2, LANES), bf16),
        scratch_shapes=[
            pltpu.VMEM((64 * 16, LANES), f32),
            pltpu.VMEM((64, LANES), f32),
            pltpu.VMEM((16 * 32, LANES), f32),
            pltpu.VMEM((256, 2, LANES), f32),
        ],
        compiler_params=params(),
        name="remap_rows",
    )(grp, flux_weight, got, index, block_weights)


def place_cells(got_ref, cells_ref, rank_ref, out_ref):
    got = got_ref[...].astype(f32)
    got = got[0:64] + got[64:128] + got[128:192] + got[192:256]
    pair, last = got[:, 0, :].T, got[:, 1, :].T
    parts = jnp.concatenate([pair, last[:64]], axis=0).astype(bf16)
    owner_at = iota((64, 4 * LANES), 0)
    for c in range(4):
        rows = range(4 * c, 4 * c + 4)
        cell = jnp.concatenate([cells_ref[r : r + 1, :] for r in rows], axis=1)
        rank = jnp.concatenate([rank_ref[r : r + 1, :] for r in rows], axis=1)
        onehot = jnp.where(owner_at == (cell >> 11), 1.0, 0.0).astype(bf16)
        value = dot(parts, onehot)
        hit = owner_at == rank
        for f in range(3):
            out_ref[f : f + 1, c * 4 * LANES : (c + 1) * 4 * LANES] = jnp.sum(
                jnp.where(hit, value[64 * f : 64 * f + 64], 0.0), axis=0, keepdims=True
            )


def placed(got, ocean_cells, rank):
    count = ocean_cells.shape[0]
    return pl.pallas_call(
        place_cells,
        out_shape=jax.ShapeDtypeStruct((3, count), f32),
        compiler_params=params(),
        name="place_cells",
    )(got, ocean_cells.reshape(count // LANES, LANES), rank)


def around(first, last):
    count = lax.axis_size(both)
    up = [(i, (i + 1) % count) for i in range(count)]
    down = [(j, i) for i, j in up]
    return lax.ppermute(last, both, up), lax.ppermute(first, both, down)


def exchange(x, axis):
    return lax.all_to_all(x, axis, split_axis=0, concat_axis=0, tiled=True)


def body(atmos_state, neighbours, flux_weight, block_weights, block_ids, block_counts, ocean_cells):
    size = atmos_state.shape[3]
    elements = size * lax.axis_size(both)
    grp = lax.axis_index("grp").astype(i32).reshape(1)
    first = (lax.axis_index(both) * size).astype(i32).reshape(1)

    stepped, low_rim, high_rim = bottom_stepped(atmos_state)
    before, after = around(low_rim, high_rim)

    live = jnp.arange(block_ids.shape[1])[None, :] < block_counts[:, None]
    ids = jnp.where(live, block_ids, -1).reshape(4, 64)
    ids = lax.dynamic_slice_in_dim(ids, lax.axis_index("grp"), 1, 0)
    ids = jnp.concatenate([ids, ids], axis=1)
    request, rank = requests(grp, ocean_cells, ids)

    slices = bottom_slices(stepped, before, after, neighbours, request, first, elements)
    table = exchange(slices, both)
    all_stepped, all_low, all_high = full_stepped(atmos_state)
    all_before, all_after = around(all_low, all_high)
    new_state = full_new_state(
        atmos_state.shape, all_stepped, all_before, all_after, neighbours, first, elements
    )

    answer, wanted = picked(table)
    answer, block_weights = lax.optimization_barrier((answer, block_weights))
    weights = lax.dynamic_slice_in_dim(block_weights, 4 * grp[0], 4, 0)
    got = exchange(answer, both)
    sent = remapped_cells(grp, flux_weight, got, wanted, weights)
    ocean_flux = placed(exchange(sent, both), ocean_cells, rank)
    return new_state, ocean_flux


def solution(mesh):
    in_specs = (
        P(None, None, None, both),
        P(None, both),
        P(),
        P("blk", None, None, None),
        P("blk", None),
        P("blk"),
        P("blk"),
    )
    out_specs = (P(None, None, None, both), P("grp", "blk"))
    return jax.shard_map(body, mesh=mesh, in_specs=in_specs, out_specs=out_specs, check_vma=False)
```

```python
import functools

import jax
import jax.numpy as jnp
import ml_dtypes
import numpy as np
from jax import lax
from jax.experimental import pallas as pl
from jax.experimental.pallas import tpu as pltpu
from jax.sharding import PartitionSpec as P

time_step = 0.02
viscosity = 0.05
LANES = 128
REACH = 256
f32 = jnp.float32
bf16 = jnp.bfloat16
i32 = jnp.int32
both = ("grp", "blk")


def params(mebibytes=16):
    return pltpu.CompilerParams(vmem_limit_bytes=mebibytes * 1024 * 1024)


def in_hbm(x):
    return pltpu.with_memory_space_constraint(x, pltpu.HBM)


def cost(flops, moved):
    return pl.CostEstimate(flops=flops, bytes_accessed=moved, transcendentals=0)


def whole(shape):
    return pl.BlockSpec(shape, lambda *_: (0,) * len(shape))


def derivative_matrix():
    nodes = np.array([-1.0, -1.0 / np.sqrt(5.0), 1.0 / np.sqrt(5.0), 1.0])
    others = [[k for k in range(4) if k != n] for n in range(4)]
    weights = [np.prod([nodes[n] - nodes[k] for k in others[n]]) for n in range(4)]
    matrix = np.zeros((4, 4))
    for a in range(4):
        for c in range(4):
            if a != c:
                matrix[a, c] = weights[a] / weights[c] / (nodes[a] - nodes[c])
            else:
                matrix[a, a] = sum(1.0 / (nodes[a] - nodes[k]) for k in others[a])
    return matrix


def operators(copies):
    d = derivative_matrix().astype(np.float32).astype(np.float64)
    east, north = np.kron(np.eye(4), d), np.kron(d, np.eye(4))
    bend = east @ east + north @ north
    parts = [-time_step * east, -time_step * north, time_step * viscosity * bend]
    stacked = np.concatenate([np.kron(np.eye(copies), part) for part in parts])
    high = stacked.astype(ml_dtypes.bfloat16)
    low = (stacked - high.astype(np.float64)).astype(ml_dtypes.bfloat16)
    return jnp.asarray(high), jnp.asarray(low)


def split_two(x):
    high = x.astype(bf16)
    return high, (x - high.astype(f32)).astype(bf16)


def dot(a, b):
    return jnp.dot(a, b, preferred_element_type=f32)


def dot_nt(a, b):
    return lax.dot_general(a, b, (((1,), (1,)), ((), ())), preferred_element_type=f32)


def apply_operators(high, low, x):
    xh, xl = split_two(x)
    return dot(high, xh) + dot(high, xl) + dot(low, xh)


def iota(shape, dim):
    return lax.broadcasted_iota(i32, shape, dim)


def bottom_step(x_ref, high_ref, low_ref, out_ref, first_ref, last_ref):
    x = x_ref[:, 0].reshape(64, -1)
    op = apply_operators(high_ref[...], low_ref[...], x)
    size = x.shape[1]
    for v in range(4):
        rows = slice(16 * v, 16 * v + 16)
        stepped = (
            x[rows] + x[0:16] * op[rows] + x[16:32] * op[64:128][rows] + op[128:192][rows]
        )
        out_ref[v] = stepped
        first_ref[v] = stepped[:, :REACH]
        last_ref[v] = stepped[:, size - REACH :]


def bottom_stepped(state):
    nvar, levels, points, size = state.shape
    high, low = operators(nvar)
    shape = (nvar, points, size)
    rim = (nvar, points, REACH)
    return pl.pallas_call(
        bottom_step,
        grid=(1,),
        in_specs=[
            pl.BlockSpec((nvar, 1, points, size), lambda i: (0, levels - 1, 0, 0)),
            whole(high.shape),
            whole(low.shape),
        ],
        out_specs=[pl.BlockSpec(memory_space=pltpu.VMEM), whole(rim), whole(rim)],
        out_shape=[
            pltpu.VMEM(shape, f32),
            jax.ShapeDtypeStruct(rim, f32),
            jax.ShapeDtypeStruct(rim, f32),
        ],
        compiler_params=params(),
        name="bottom_step",
    )(in_hbm(state), in_hbm(high), in_hbm(low))


def line_operators():
    d = derivative_matrix()
    d2 = d @ d
    slope = [
        (
            0.5 * (d[i, 0] - d[i, 3]),
            0.5 * (d[i, 1] - d[i, 2]),
            0.5 * (d[i, 0] + d[i, 3]),
        )
        for i in range(2)
    ]
    bend = [
        (
            0.5 * (d2[i, 0] - d2[i, 3]),
            0.5 * (d2[i, 1] - d2[i, 2]),
            0.5 * (d2[i, 0] + d2[i, 3]),
        )
        for i in range(2)
    ]
    return slope, bend


def along_line(x, slope, bend):
    t0, t1 = x[0] - x[3], x[1] - x[2]
    mean = (x[0] + x[3]) - (x[1] + x[2])
    first, second = [None] * 4, [None] * 4
    for i in range(2):
        a, b, c = [np.float32(-time_step * k) for k in slope[i]]
        even, odd = a * t0 + b * t1, c * mean
        first[i], first[3 - i] = even + odd, even - odd
        a, b, c = [np.float32(time_step * viscosity * k) for k in bend[i]]
        odd, even = a * t0 + b * t1, c * mean
        second[i], second[3 - i] = even + odd, even - odd
    return first, second


edge_points = (0, 1, 2, 3, 4, 7, 8, 11, 12, 13, 14, 15)


def full_step(x_ref, out_ref, first_ref, last_ref):
    step = pl.program_id(0)
    count = pl.num_programs(0)
    slope, bend = line_operators()

    def points(v, half):
        start = (v * 16 + half * 8) * 16
        return [x_ref[pl.ds(start + p, 8, stride=16), :] for p in range(16)]

    for half in range(2):
        u, w = points(0, half), points(1, half)
        for v in range(4):
            x = u if v == 0 else w if v == 1 else points(v, half)
            total = list(x)
            for a in range(4):
                at = [4 * a + b for b in range(4)]
                first, second = along_line([x[p] for p in at], slope, bend)
                for p, one, two in zip(at, first, second):
                    total[p] = total[p] + (u[p] * one + two)
            for b in range(4):
                at = [4 * a + b for a in range(4)]
                first, second = along_line([x[p] for p in at], slope, bend)
                for p, one, two in zip(at, first, second):
                    total[p] = total[p] + (w[p] * one + two)
            for p in range(16):
                out_ref[p, v * 16 + half * 8 : v * 16 + half * 8 + 8, :] = total[p]

    for part in range(2):
        cols = slice(part * LANES, (part + 1) * LANES)

        @pl.when(step == part)
        def _():
            for k, p in enumerate(edge_points):
                first_ref[k, :, cols] = out_ref[p].astype(bf16)

        @pl.when(step == count - 2 + part)
        def _():
            for k, p in enumerate(edge_points):
                last_ref[k, :, cols] = out_ref[p].astype(bf16)


def full_stepped(state):
    nvar, levels, points, size = state.shape
    rows = nvar * levels
    rim = (len(edge_points), rows, REACH)
    return pl.pallas_call(
        full_step,
        grid=(size // LANES,),
        in_specs=[pl.BlockSpec((rows * points, LANES), lambda i: (0, i))],
        out_specs=[
            pl.BlockSpec((points, rows, LANES), lambda i: (0, 0, i)),
            whole(rim),
            whole(rim),
        ],
        out_shape=[
            pltpu.HBM((points, rows, size), f32),
            jax.ShapeDtypeStruct(rim, bf16),
            jax.ShapeDtypeStruct(rim, bf16),
        ],
        compiler_params=params(24),
        cost_estimate=cost(4 * 10**7, 9 << 20),
        name="full_step",
    )(in_hbm(state.reshape(rows * points, size)))


def local_columns(nb_ref, first, elements):
    place = nb_ref[...] - first + REACH
    place = jnp.where(place < 0, place + elements, place)
    return jnp.where(place >= elements, place - elements, place)


def side_indices(place, rows, eb):
    cols = slice(eb * LANES, (eb + 1) * LANES)
    part = [jnp.broadcast_to(place[s : s + 1, cols], (rows, LANES)) for s in range(4)]
    point = iota((rows, LANES), 0) % 8
    we = jnp.where(point % 4 == 3, part[0], part[1])
    ns = jnp.where(point < 4, part[3], part[2])
    return we, ns


def look_up(columns, index, eb):
    lane = index & (LANES - 1)
    column = (index >> 7) - eb
    value = jnp.take_along_axis(columns[0], lane, axis=1)
    for c in range(1, 5):
        value = jnp.where(column == c, jnp.take_along_axis(columns[c], lane, axis=1), value)
    return value


def halves(x):
    grouped = x.reshape(x.shape[0] // 16, 2, 8, x.shape[1])
    shape = (x.shape[0] // 2, x.shape[1])
    return grouped[:, 0].reshape(shape), grouped[:, 1].reshape(shape)


def edge_update(columns, we, ns, eb):
    pairs = [halves(column) for column in columns]
    rows = pairs[0][0].shape[0]
    point = iota(pairs[0][0].shape, 0) % 8
    first = point < 4
    across = look_up([jnp.where(first, low, high) for low, high in pairs], ns, eb)
    zero = jnp.zeros(first.shape, f32)
    done = []
    for side in range(2):
        own = pairs[2][side]
        beside = look_up([pair[side] for pair in pairs], we, eb)
        total = jnp.where(point % 4 == 0, pltpu.roll(beside, rows - 3, 0) - own, zero)
        total += jnp.where(point % 4 == 3, pltpu.roll(beside, 3, 0) - own, zero)
        if side == 0:
            total += jnp.where(first, pltpu.roll(across, rows - 4, 0) - own, zero)
        else:
            total += jnp.where(first, zero, pltpu.roll(across, 4, 0) - own)
        done.append((own + 0.5 * total).reshape(-1, 1, 8, own.shape[1]))
    return jnp.concatenate(done, axis=1).reshape(columns[0].shape)


def window(own, before, after, eb):
    count = own.shape[-1] // LANES
    pieces = []
    for c in range(eb, eb + 5):
        if c < 2:
            piece = before[..., c * LANES : (c + 1) * LANES]
        elif c < 2 + count:
            piece = own[..., (c - 2) * LANES : (c - 1) * LANES]
        else:
            piece = after[..., (c - 2 - count) * LANES : (c - 1 - count) * LANES]
        pieces.append(piece)
    return pieces


def bottom_edges(
    elements, first_ref, s_ref, before_ref, after_ref, nb_ref, request_ref, out_ref
):
    out_ref[:, 0, 2 * LANES :] = request_ref[...]
    place = local_columns(nb_ref, first_ref[0], elements)
    own = s_ref[...].reshape(64, -1)
    before = before_ref[...].reshape(64, -1)
    after = after_ref[...].reshape(64, -1)
    count = own.shape[1] // LANES
    new = []
    for eb in range(count):
        we, ns = side_indices(place, 32, eb)
        new.append(edge_update(window(own, before, after, eb), we, ns, eb))
    for v in range(4):
        blocks = jnp.concatenate([piece[16 * v : 16 * v + 16] for piece in new], axis=0)
        turned = blocks.T
        out_ref[64 * v : 64 * v + 64, 0, :LANES] = turned[:64]
        out_ref[64 * v : 64 * v + 64, 0, LANES : 2 * LANES] = turned[64:]


def bottom_slices(stepped, before, after, neighbours, request, first, elements):
    shape = (256, 1, 3 * LANES)
    return pl.pallas_call(
        functools.partial(bottom_edges, elements),
        in_specs=[
            pl.BlockSpec(memory_space=pltpu.SMEM),
            pl.BlockSpec(memory_space=pltpu.VMEM),
            pl.BlockSpec(memory_space=pltpu.VMEM),
            pl.BlockSpec(memory_space=pltpu.VMEM),
            pl.BlockSpec(memory_space=pltpu.VMEM),
            pl.BlockSpec(memory_space=pltpu.VMEM),
        ],
        out_shape=jax.ShapeDtypeStruct(shape, f32),
        compiler_params=params(),
        name="bottom_edges",
    )(first, stepped, before, after, neighbours, request)


sides = (
    ((3, 7, 11, 15), (0, 4, 8, 12)),
    ((0, 4, 8, 12), (3, 7, 11, 15)),
    ((12, 13, 14, 15), (0, 1, 2, 3)),
    ((0, 1, 2, 3), (12, 13, 14, 15)),
)


def full_edges(
    elements,
    first_ref,
    ahead_ref,
    own_ref,
    before_ref,
    after_ref,
    nb_ref,
    out_ref,
    split_ref,
    turn_ref,
):
    step = pl.program_id(0)
    tiles = pl.num_programs(0) - 1
    rows = own_ref.shape[1]
    empty = jnp.zeros((rows, REACH), bf16)

    @pl.when(step == 0)
    def _():
        for k, p in enumerate(edge_points):
            split_ref[0, p, :, :REACH] = before_ref[k]
            split_ref[1, p, :, :REACH] = empty

    place_at = pl.multiple_of((step + 1) * REACH, REACH)

    @pl.when(step < tiles)
    def _():
        for p in edge_points:
            high, low = split_two(ahead_ref[p])
            split_ref[0, p, :, pl.ds(place_at, REACH)] = high
            split_ref[1, p, :, pl.ds(place_at, REACH)] = low

    @pl.when(step == tiles)
    def _():
        for k, p in enumerate(edge_points):
            split_ref[0, p, :, pl.ds(place_at, REACH)] = after_ref[k]
            split_ref[1, p, :, pl.ds(place_at, REACH)] = empty

    @pl.when(step > 0)
    def _():
        place = local_columns(nb_ref, first_ref[0], elements) - (step - 1) * REACH
        start = pl.multiple_of((step - 1) * REACH, REACH)
        change = [None] * 16
        for side, (source, target) in enumerate(sides):
            onehot = jnp.where(
                iota((3 * REACH, REACH), 0) == place[side : side + 1, :], 1.0, 0.0
            ).astype(bf16)
            pieces = [
                split_ref[part, p, :, pl.ds(start, 3 * REACH)]
                for part in range(2)
                for p in source
            ]
            value = dot(jnp.concatenate(pieces, axis=0), onehot)
            for k, p in enumerate(target):
                there = value[k * rows : (k + 1) * rows] + value[(4 + k) * rows : (5 + k) * rows]
                part = there - own_ref[p]
                change[p] = part if change[p] is None else change[p] + part
        for p in range(16):
            new = own_ref[p] if change[p] is None else own_ref[p] + 0.5 * change[p]
            for h in range(2):
                turn_ref[h, pl.ds(p, rows, stride=16), :] = new[:, h * LANES : (h + 1) * LANES]
        for h in range(2):
            out_ref[:, h * LANES : (h + 1) * LANES] = turn_ref[h]


def full_new_state(shape, stepped, before, after, neighbours, first, elements):
    points, rows, size = stepped.shape
    tiles = size // REACH
    tile = (points, rows, REACH)
    out = pl.pallas_call(
        functools.partial(full_edges, elements),
        grid=(tiles + 1,),
        in_specs=[
            pl.BlockSpec(memory_space=pltpu.SMEM),
            pl.BlockSpec(tile, lambda i: (0, 0, jnp.minimum(i, tiles - 1))),
            pl.BlockSpec(tile, lambda i: (0, 0, jnp.maximum(i - 1, 0))),
            whole(before.shape),
            whole(after.shape),
            pl.BlockSpec((4, REACH), lambda i: (0, jnp.maximum(i - 1, 0))),
        ],
        out_specs=pl.BlockSpec((rows * points, REACH), lambda i: (0, jnp.maximum(i - 1, 0))),
        out_shape=jax.ShapeDtypeStruct((rows * points, size), f32),
        scratch_shapes=[
            pltpu.VMEM((2, 16, rows, size + 2 * REACH), bf16),
            pltpu.VMEM((2, rows * points, LANES), f32),
        ],
        compiler_params=params(24),
        cost_estimate=cost(4 * 10**9, 10 << 20),
        name="full_edges",
    )(first, in_hbm(stepped), in_hbm(stepped), before, after, neighbours)
    return out.reshape(shape)


def request_table(grp_ref, cells_ref, ids_ref, out_ref, rank_ref):
    chunks = cells_ref.shape[0]
    owner_at = iota((64, LANES), 0)
    cells = [cells_ref[c : c + 1, :] for c in range(chunks)]
    mine = [jnp.where(owner_at == (cell >> 11), 1.0, 0.0) for cell in cells]
    before = jnp.where(iota((LANES, 2 * LANES), 0) < iota((LANES, 2 * LANES), 1), 1.0, 0.0)
    counts = dot(jnp.concatenate(mine, axis=0).astype(bf16), before.astype(bf16))
    carried = jnp.zeros((64, LANES), f32)
    slots, high, low = [], [], []
    for c, cell in enumerate(cells):
        count = counts[64 * c : 64 * c + 64]
        rank = jnp.sum(mine[c] * (count[:, :LANES] + carried), axis=0, keepdims=True).astype(i32)
        carried = carried + count[:, LANES:]
        rank_ref[c : c + 1, :] = rank
        slots.append(jnp.where(owner_at == rank, 1.0, 0.0).astype(bf16))
        row = cell & 2047
        high.append((mine[c] * (row >> 7).astype(f32)).astype(bf16))
        low.append((mine[c] * (row & 127).astype(f32)).astype(bf16))
    parts = jnp.concatenate([jnp.concatenate(p, axis=1) for p in (high, low)], axis=0)
    wanted = dot_nt(parts, jnp.concatenate(slots, axis=1))
    wanted = wanted[:64] * 128.0 + wanted[64:]
    wanted = jnp.concatenate([wanted, wanted], axis=1)
    share = pltpu.roll(wanted, 64 - 12 * grp_ref[0], 1)
    message = jnp.where(iota((64, LANES), 1) < 64, ids_ref[...].astype(f32), share)
    for y in range(4):
        out_ref[64 * y : 64 * y + 64, :] = message


def requests(grp, ocean_cells, ids):
    chunks = ocean_cells.shape[0] // LANES
    vmem = pl.BlockSpec(memory_space=pltpu.VMEM)
    return pl.pallas_call(
        request_table,
        in_specs=[pl.BlockSpec(memory_space=pltpu.SMEM), vmem, vmem],
        out_shape=[
            jax.ShapeDtypeStruct((256, LANES), f32),
            jax.ShapeDtypeStruct((chunks, LANES), i32),
        ],
        compiler_params=params(),
        name="request_table",
    )(grp, ocean_cells.reshape(chunks, LANES), ids)


QUERIES = 256


def pick_values(table_ref, out_ref, cells_ref, turned_ref, ids_ref, found_ref):
    lane = iota((LANES, LANES), 1)
    asked = table_ref[:, 0, 2 * LANES :]
    ids = jnp.where(lane < 64, asked[:LANES], pltpu.roll(asked[LANES:], 64, 1))
    ids_ref[...] = ids.astype(i32)
    lane = iota((64, LANES), 1)
    wanted = jnp.zeros((64, LANES), f32)
    for y in range(4):
        part = pltpu.roll(asked[64 * y : 64 * y + 64], 64 + 12 * y, 1)
        wanted = jnp.where((lane >= 12 * y) & (lane < 12 * y + 12), part, wanted)
    lane = iota((32, LANES), 1)
    cells_ref[...] = jnp.where(lane < 64, wanted[:32], pltpu.roll(wanted[32:], 64, 1)).astype(i32)

    high, low = split_two(table_ref[:, 0, : 2 * LANES].T)
    for half in range(2):
        turned_ref[half, :LANES] = high[half * LANES : (half + 1) * LANES]
        turned_ref[half, LANES:] = low[half * LANES : (half + 1) * LANES]
    groups = QUERIES // LANES
    device_at = iota((256, QUERIES), 0)
    block_at = iota((LANES, QUERIES), 0)

    def some(step, carry):
        rows = [ids_ref[pl.ds(groups * step + k, 1), :] for k in range(groups)]
        asked = jnp.concatenate(rows, axis=1)
        onehot = jnp.where(device_at == (asked >> 7), 1.0, 0.0).astype(bf16)
        hit = block_at == (asked & 127)
        for half in range(2):
            value = dot(turned_ref[half], onehot)
            part = value[:LANES] + value[LANES:]
            found = jnp.sum(jnp.where(hit, part, 0.0), axis=0, keepdims=True)
            for k in range(groups):
                found_ref[half, pl.ds(groups * step + k, 1), :] = found[
                    :, k * LANES : (k + 1) * LANES
                ]
        return carry

    lax.fori_loop(0, LANES // groups, some, 0, unroll=32)
    lane = iota((LANES, LANES), 1)
    first, second = found_ref[0], found_ref[1]
    out_ref[:LANES, 0, :] = jnp.where(lane < 64, first, pltpu.roll(second, 64, 1))
    out_ref[LANES:, 0, :] = jnp.where(lane < 64, pltpu.roll(first, 64, 1), second)


def picked(table):
    return pl.pallas_call(
        pick_values,
        out_shape=[
            pltpu.HBM((256, 1, LANES), f32),
            jax.ShapeDtypeStruct((32, LANES), i32),
        ],
        scratch_shapes=[
            pltpu.VMEM((2, 256, 256), bf16),
            pltpu.VMEM((LANES, LANES), i32),
            pltpu.VMEM((2, LANES, LANES), f32),
        ],
        compiler_params=params(24),
        name="pick_values",
    )(table)


def remap_rows(
    grp_ref, fw_ref, got_ref, index_ref, w_ref, out_ref, field_ref, mapped_ref, sent_ref, pair_ref
):
    values = []
    for v in range(4):
        turned = got_ref[64 * v : 64 * v + 64, 0, :].T
        values.append(jnp.concatenate([turned[:64], turned[64:]], axis=1))
    wind = jnp.sqrt(1.0 + values[0] * values[0] + values[1] * values[1])
    for f in range(16):
        if f < 12:
            total = fw_ref[f, 0] * values[0]
            for v in range(1, 4):
                total += fw_ref[f, v] * values[v]
            total = (total * wind).astype(bf16).astype(f32)
        else:
            total = jnp.zeros((64, LANES), f32)
        field_ref[pl.ds(f, 64, stride=16), :] = total

    for r in range(4):
        total = jnp.zeros((16, LANES), f32)
        for b in range(0, 16, 2):
            at = (r * 16 + b) * 16
            pair = field_ref[at : at + 32, :].astype(bf16)
            pair = jnp.concatenate([pair[:16], pair[16:]], axis=1)
            weights = jnp.concatenate([w_ref[r, b], w_ref[r, b + 1]], axis=1)
            total += dot_nt(pair, weights)
        mapped_ref[16 * r : 16 * r + 16, :] = total

    parts = jnp.concatenate(split_two(mapped_ref[...]), axis=0)
    row_at = iota((LANES, 4 * LANES), 0)

    def some(at, carry):
        rows = [index_ref[pl.ds(4 * at + k, 1), :] for k in range(4)]
        asked = jnp.concatenate(rows, axis=1)
        onehot = jnp.where(row_at == (asked & 127), 1.0, 0.0).astype(bf16)
        value = dot(parts, onehot)
        value = value[:64] + value[64:]
        block = (asked >> 7) - 4 * grp_ref[0]
        found = jnp.where(block == 0, value[:16], 0.0)
        for r in range(1, 4):
            found = jnp.where(block == r, value[16 * r : 16 * r + 16], found)
        for k in range(4):
            sent_ref[pl.ds(4 * at + k, 16, stride=32), :] = found[
                :, k * LANES : (k + 1) * LANES
            ]
        return carry

    lax.fori_loop(0, 8, some, 0, unroll=True)
    lane = iota((32, LANES), 1)
    for y in range(4):
        a, b, c = [sent_ref[(3 * y + f) * 32 : (3 * y + f) * 32 + 32, :] for f in range(3)]
        base = 64 * y
        low, high = slice(base, base + 32), slice(base + 32, base + 64)
        pair_ref[low, 0, :] = jnp.where(lane < 64, a, pltpu.roll(b, 64, 1))
        pair_ref[low, 1, :] = c
        pair_ref[high, 0, :] = jnp.where(lane < 64, pltpu.roll(a, 64, 1), b)
        pair_ref[high, 1, :] = pltpu.roll(c, 64, 1)
    out_ref[...] = pair_ref[...].astype(bf16)


def remapped_cells(grp, flux_weight, got, index, block_weights):
    smem = pl.BlockSpec(memory_space=pltpu.SMEM)
    vmem = pl.BlockSpec(memory_space=pltpu.VMEM)
    return pl.pallas_call(
        remap_rows,
        in_specs=[smem, smem, vmem, vmem, vmem],
        out_shape=jax.ShapeDtypeStruct((256, 2, LANES), bf16),
        scratch_shapes=[
            pltpu.VMEM((64 * 16, LANES), f32),
            pltpu.VMEM((64, LANES), f32),
            pltpu.VMEM((16 * 32, LANES), f32),
            pltpu.VMEM((256, 2, LANES), f32),
        ],
        compiler_params=params(),
        name="remap_rows",
    )(grp, flux_weight, got, index, block_weights)


def place_cells(got_ref, cells_ref, rank_ref, out_ref):
    got = got_ref[...].astype(f32)
    got = got[0:64] + got[64:128] + got[128:192] + got[192:256]
    pair, last = got[:, 0, :].T, got[:, 1, :].T
    parts = jnp.concatenate([pair, last[:64]], axis=0).astype(bf16)
    owner_at = iota((64, 4 * LANES), 0)
    for c in range(4):
        rows = range(4 * c, 4 * c + 4)
        cell = jnp.concatenate([cells_ref[r : r + 1, :] for r in rows], axis=1)
        rank = jnp.concatenate([rank_ref[r : r + 1, :] for r in rows], axis=1)
        onehot = jnp.where(owner_at == (cell >> 11), 1.0, 0.0).astype(bf16)
        value = dot(parts, onehot)
        hit = owner_at == rank
        for f in range(3):
            out_ref[f : f + 1, c * 4 * LANES : (c + 1) * 4 * LANES] = jnp.sum(
                jnp.where(hit, value[64 * f : 64 * f + 64], 0.0), axis=0, keepdims=True
            )


def placed(got, ocean_cells, rank):
    count = ocean_cells.shape[0]
    return pl.pallas_call(
        place_cells,
        out_shape=jax.ShapeDtypeStruct((3, count), f32),
        compiler_params=params(),
        name="place_cells",
    )(got, ocean_cells.reshape(count // LANES, LANES), rank)


def around(first, last):
    count = lax.axis_size(both)
    up = [(i, (i + 1) % count) for i in range(count)]
    down = [(j, i) for i, j in up]
    return lax.ppermute(last, both, up), lax.ppermute(first, both, down)


def exchange(x, axis):
    return lax.all_to_all(x, axis, split_axis=0, concat_axis=0, tiled=True)


def body(atmos_state, neighbours, flux_weight, block_weights, block_ids, block_counts, ocean_cells):
    size = atmos_state.shape[3]
    elements = size * lax.axis_size(both)
    grp = lax.axis_index("grp").astype(i32).reshape(1)
    first = (lax.axis_index(both) * size).astype(i32).reshape(1)

    stepped, low_rim, high_rim = bottom_stepped(atmos_state)
    before, after = around(low_rim, high_rim)

    live = jnp.arange(block_ids.shape[1])[None, :] < block_counts[:, None]
    ids = jnp.where(live, block_ids, -1).reshape(4, 64)
    ids = lax.dynamic_slice_in_dim(ids, lax.axis_index("grp"), 1, 0)
    ids = jnp.concatenate([ids, ids], axis=1)
    request, rank = requests(grp, ocean_cells, ids)

    slices = bottom_slices(stepped, before, after, neighbours, request, first, elements)
    table = exchange(slices, both)
    all_stepped, all_low, all_high = full_stepped(atmos_state)
    all_before, all_after = around(all_low, all_high)
    new_state = full_new_state(
        atmos_state.shape, all_stepped, all_before, all_after, neighbours, first, elements
    )

    answer, wanted = picked(table)
    answer, block_weights = lax.optimization_barrier((answer, block_weights))
    weights = lax.dynamic_slice_in_dim(block_weights, 4 * grp[0], 4, 0)
    got = exchange(answer, both)
    sent = remapped_cells(grp, flux_weight, got, wanted, weights)
    ocean_flux = placed(exchange(sent, both), ocean_cells, rank)
    return new_state, ocean_flux


def solution(mesh):
    in_specs = (
        P(None, None, None, both),
        P(None, both),
        P(),
        P("blk", None, None, None),
        P("blk", None),
        P("blk"),
        P("blk"),
    )
    out_specs = (P(None, None, None, both), P("grp", "blk"))
    return jax.shard_map(body, mesh=mesh, in_specs=in_specs, out_specs=out_specs, check_vma=False)
```

```python
import functools

import jax
import jax.numpy as jnp
import ml_dtypes
import numpy as np
from jax import lax
from jax.experimental import pallas as pl
from jax.experimental.pallas import tpu as pltpu
from jax.sharding import PartitionSpec as P

time_step = 0.02
viscosity = 0.05
LANES = 128
REACH = 256
f32 = jnp.float32
bf16 = jnp.bfloat16
i32 = jnp.int32
both = ("grp", "blk")


def params(mebibytes=16):
    return pltpu.CompilerParams(vmem_limit_bytes=mebibytes * 1024 * 1024)


def in_hbm(x):
    return pltpu.with_memory_space_constraint(x, pltpu.HBM)


def cost(flops, moved):
    return pl.CostEstimate(flops=flops, bytes_accessed=moved, transcendentals=0)


def whole(shape):
    return pl.BlockSpec(shape, lambda *_: (0,) * len(shape))


def derivative_matrix():
    nodes = np.array([-1.0, -1.0 / np.sqrt(5.0), 1.0 / np.sqrt(5.0), 1.0])
    others = [[k for k in range(4) if k != n] for n in range(4)]
    weights = [np.prod([nodes[n] - nodes[k] for k in others[n]]) for n in range(4)]
    matrix = np.zeros((4, 4))
    for a in range(4):
        for c in range(4):
            if a != c:
                matrix[a, c] = weights[a] / weights[c] / (nodes[a] - nodes[c])
            else:
                matrix[a, a] = sum(1.0 / (nodes[a] - nodes[k]) for k in others[a])
    return matrix


def operators(copies):
    d = derivative_matrix().astype(np.float32).astype(np.float64)
    east, north = np.kron(np.eye(4), d), np.kron(d, np.eye(4))
    bend = east @ east + north @ north
    parts = [-time_step * east, -time_step * north, time_step * viscosity * bend]
    stacked = np.concatenate([np.kron(np.eye(copies), part) for part in parts])
    high = stacked.astype(ml_dtypes.bfloat16)
    low = (stacked - high.astype(np.float64)).astype(ml_dtypes.bfloat16)
    return jnp.asarray(high), jnp.asarray(low)


def split_two(x):
    high = x.astype(bf16)
    return high, (x - high.astype(f32)).astype(bf16)


def dot(a, b):
    return jnp.dot(a, b, preferred_element_type=f32)


def dot_nt(a, b):
    return lax.dot_general(a, b, (((1,), (1,)), ((), ())), preferred_element_type=f32)


def apply_operators(high, low, x):
    xh, xl = split_two(x)
    return dot(high, xh) + dot(high, xl) + dot(low, xh)


def iota(shape, dim):
    return lax.broadcasted_iota(i32, shape, dim)


def bottom_step(x_ref, nb_ref, high_ref, low_ref, out_ref, rim_ref):
    x = x_ref[:, 0].reshape(64, -1)
    op = apply_operators(high_ref[...], low_ref[...], x)
    size = x.shape[1]
    for v in range(4):
        rows = slice(16 * v, 16 * v + 16)
        stepped = (
            x[rows] + x[0:16] * op[rows] + x[16:32] * op[64:128][rows] + op[128:192][rows]
        )
        out_ref[rows] = stepped
        rim_ref[rows] = stepped[:, size - 2 * REACH :]
        rim_ref[16 * v + 5 : 16 * v + 6, :REACH] = nb_ref[v : v + 1].astype(f32)


def bottom_stepped(state, neighbours):
    nvar, levels, points, size = state.shape
    high, low = operators(nvar)
    rim = (nvar * points, 2 * REACH)
    return pl.pallas_call(
        bottom_step,
        grid=(1,),
        in_specs=[
            pl.BlockSpec((nvar, 1, points, size), lambda i: (0, levels - 1, 0, 0)),
            pl.BlockSpec((4, REACH), lambda i: (0, size // REACH - 1)),
            whole(high.shape),
            whole(low.shape),
        ],
        out_specs=[pl.BlockSpec(memory_space=pltpu.VMEM), whole(rim)],
        out_shape=[pltpu.VMEM((nvar * points, size), f32), jax.ShapeDtypeStruct(rim, f32)],
        compiler_params=params(),
        name="bottom_step",
    )(in_hbm(state), in_hbm(neighbours), in_hbm(high), in_hbm(low))


def line_operators():
    d = derivative_matrix()
    d2 = d @ d
    slope = [
        (
            0.5 * (d[i, 0] - d[i, 3]),
            0.5 * (d[i, 1] - d[i, 2]),
            0.5 * (d[i, 0] + d[i, 3]),
        )
        for i in range(2)
    ]
    bend = [
        (
            0.5 * (d2[i, 0] - d2[i, 3]),
            0.5 * (d2[i, 1] - d2[i, 2]),
            0.5 * (d2[i, 0] + d2[i, 3]),
        )
        for i in range(2)
    ]
    return slope, bend


def along_line(x, slope, bend):
    t0, t1 = x[0] - x[3], x[1] - x[2]
    mean = (x[0] + x[3]) - (x[1] + x[2])
    first, second = [None] * 4, [None] * 4
    for i in range(2):
        a, b, c = [np.float32(-time_step * k) for k in slope[i]]
        even, odd = a * t0 + b * t1, c * mean
        first[i], first[3 - i] = even + odd, even - odd
        a, b, c = [np.float32(time_step * viscosity * k) for k in bend[i]]
        odd, even = a * t0 + b * t1, c * mean
        second[i], second[3 - i] = even + odd, even - odd
    return first, second


edge_points = (0, 1, 2, 3, 4, 7, 8, 11, 12, 13, 14, 15)


def full_step(x_ref, out_ref, first_ref, last_ref):
    step = pl.program_id(0)
    count = pl.num_programs(0)
    slope, bend = line_operators()

    def points(v, half):
        start = (v * 16 + half * 8) * 16
        return [x_ref[pl.ds(start + p, 8, stride=16), :] for p in range(16)]

    for half in range(2):
        u, w = points(0, half), points(1, half)
        for v in range(4):
            x = u if v == 0 else w if v == 1 else points(v, half)
            total = list(x)
            for a in range(4):
                at = [4 * a + b for b in range(4)]
                first, second = along_line([x[p] for p in at], slope, bend)
                for p, one, two in zip(at, first, second):
                    total[p] = total[p] + (u[p] * one + two)
            for b in range(4):
                at = [4 * a + b for a in range(4)]
                first, second = along_line([x[p] for p in at], slope, bend)
                for p, one, two in zip(at, first, second):
                    total[p] = total[p] + (w[p] * one + two)
            for p in range(16):
                out_ref[p, v * 16 + half * 8 : v * 16 + half * 8 + 8, :] = total[p]

    for part in range(2):
        cols = slice(part * LANES, (part + 1) * LANES)

        @pl.when(step == part)
        def _():
            for k, p in enumerate(edge_points):
                first_ref[k, :, cols] = out_ref[p].astype(bf16)

        @pl.when(step == count - 2 + part)
        def _():
            for k, p in enumerate(edge_points):
                last_ref[k, :, cols] = out_ref[p].astype(bf16)


def full_stepped(state):
    nvar, levels, points, size = state.shape
    rows = nvar * levels
    rim = (len(edge_points), rows, REACH)
    return pl.pallas_call(
        full_step,
        grid=(size // LANES,),
        in_specs=[pl.BlockSpec((rows * points, LANES), lambda i: (0, i))],
        out_specs=[
            pl.BlockSpec((points, rows, LANES), lambda i: (0, 0, i)),
            whole(rim),
            whole(rim),
        ],
        out_shape=[
            pltpu.HBM((points, rows, size), f32),
            jax.ShapeDtypeStruct(rim, bf16),
            jax.ShapeDtypeStruct(rim, bf16),
        ],
        compiler_params=params(24),
        cost_estimate=cost(4 * 10**7, 9 << 20),
        name="full_step",
    )(in_hbm(state.reshape(rows * points, size)))


def local_columns(neighbours, start, elements):
    place = neighbours - start
    place = jnp.where(place < 0, place + elements, place)
    return jnp.where(place >= elements, place - elements, place)


def side_indices(place, rows):
    part = [jnp.broadcast_to(place[s : s + 1], (rows, LANES)) for s in range(4)]
    point = iota((rows, LANES), 0) % 8
    we = jnp.where(point % 4 == 3, part[0], part[1])
    ns = jnp.where(point < 4, part[3], part[2])
    return we, ns


def look_up(columns, index, eb):
    lane = index & (LANES - 1)
    column = (index >> 7) - eb
    value = jnp.take_along_axis(columns[0], lane, axis=1)
    for c in range(1, 5):
        value = jnp.where(column == c, jnp.take_along_axis(columns[c], lane, axis=1), value)
    return value


def halves(x):
    grouped = x.reshape(x.shape[0] // 16, 2, 8, x.shape[1])
    shape = (x.shape[0] // 2, x.shape[1])
    return grouped[:, 0].reshape(shape), grouped[:, 1].reshape(shape)


def edge_update(columns, we, ns, eb):
    pairs = [halves(column) for column in columns]
    rows = pairs[0][0].shape[0]
    point = iota(pairs[0][0].shape, 0) % 8
    first = point < 4
    across = look_up([jnp.where(first, low, high) for low, high in pairs], ns, eb)
    zero = jnp.zeros(first.shape, f32)
    done = []
    for side in range(2):
        own = pairs[2][side]
        beside = look_up([pair[side] for pair in pairs], we, eb)
        total = jnp.where(point % 4 == 0, pltpu.roll(beside, rows - 3, 0) - own, zero)
        total += jnp.where(point % 4 == 3, pltpu.roll(beside, 3, 0) - own, zero)
        if side == 0:
            total += jnp.where(first, pltpu.roll(across, rows - 4, 0) - own, zero)
        else:
            total += jnp.where(first, zero, pltpu.roll(across, 4, 0) - own)
        done.append((own + 0.5 * total).reshape(-1, 1, 8, own.shape[1]))
    return jnp.concatenate(done, axis=1).reshape(columns[0].shape)


def lane_tiles(ref, count):
    return [ref[:, c * LANES : (c + 1) * LANES] for c in range(count)]


def inner_edges(elements, first_ref, s_ref, nb_ref, out_ref):
    size = s_ref.shape[1]
    place = local_columns(nb_ref[...], first_ref[0], elements)
    tiles = lane_tiles(s_ref, size // LANES)
    for eb in range(size // LANES - 4):
        cols = slice(eb * LANES + REACH, eb * LANES + REACH + LANES)
        we, ns = side_indices(place[:, cols], 32)
        out_ref[:, eb * LANES : (eb + 1) * LANES] = edge_update(tiles[eb : eb + 5], we, ns, eb)


def bottom_inner(stepped, neighbours, first, elements):
    rows, size = stepped.shape
    vmem = pl.BlockSpec(memory_space=pltpu.VMEM)
    return pl.pallas_call(
        functools.partial(inner_edges, elements),
        in_specs=[pl.BlockSpec(memory_space=pltpu.SMEM), vmem, vmem],
        out_specs=vmem,
        out_shape=pltpu.VMEM((rows, size - 2 * REACH), f32),
        compiler_params=params(),
        name="bottom_inner",
    )(first, stepped, neighbours)


def bottom_edges(elements, first_ref, s_ref, prev_ref, nb_ref, inner_ref, request_ref, out_ref):
    out_ref[:, 0, 2 * LANES :] = request_ref[...]
    edge = 2 * REACH // LANES
    carried = [prev_ref[16 * v + 5 : 16 * v + 6, :REACH] for v in range(4)]
    neighbours = jnp.concatenate(
        [jnp.concatenate(carried, axis=0).astype(i32), nb_ref[:, :REACH]], axis=1
    )
    place = local_columns(neighbours, first_ref[0] - 2 * REACH, elements)
    tiles = lane_tiles(prev_ref, edge) + lane_tiles(s_ref, edge)
    new = []
    for eb in range(edge):
        we, ns = side_indices(place[:, eb * LANES : (eb + 1) * LANES], 32)
        new.append(edge_update(tiles[eb : eb + 5], we, ns, eb))
    new += lane_tiles(inner_ref, inner_ref.shape[1] // LANES)
    for v in range(4):
        blocks = jnp.concatenate([piece[16 * v : 16 * v + 16] for piece in new], axis=0)
        turned = blocks.T
        out_ref[64 * v : 64 * v + 64, 0, :LANES] = turned[:64]
        out_ref[64 * v : 64 * v + 64, 0, LANES : 2 * LANES] = turned[64:]


def bottom_slices(stepped, prev, neighbours, inner, request, first, elements):
    vmem = pl.BlockSpec(memory_space=pltpu.VMEM)
    return pl.pallas_call(
        functools.partial(bottom_edges, elements),
        in_specs=[pl.BlockSpec(memory_space=pltpu.SMEM)] + [vmem] * 5,
        out_shape=jax.ShapeDtypeStruct((256, 1, 3 * LANES), f32),
        compiler_params=params(),
        name="bottom_edges",
    )(first, stepped, prev, neighbours, inner, request)


sides = (
    ((3, 7, 11, 15), (0, 4, 8, 12)),
    ((0, 4, 8, 12), (3, 7, 11, 15)),
    ((12, 13, 14, 15), (0, 1, 2, 3)),
    ((0, 1, 2, 3), (12, 13, 14, 15)),
)


def full_edges(
    elements,
    first_ref,
    ahead_ref,
    own_ref,
    before_ref,
    after_ref,
    nb_ref,
    out_ref,
    split_ref,
    turn_ref,
):
    step = pl.program_id(0)
    tiles = pl.num_programs(0) - 1
    rows = own_ref.shape[1]
    empty = jnp.zeros((rows, REACH), bf16)

    @pl.when(step == 0)
    def _():
        for k, p in enumerate(edge_points):
            split_ref[0, p, :, :REACH] = before_ref[k]
            split_ref[1, p, :, :REACH] = empty

    place_at = pl.multiple_of((step + 1) * REACH, REACH)

    @pl.when(step < tiles)
    def _():
        for p in edge_points:
            high, low = split_two(ahead_ref[p])
            split_ref[0, p, :, pl.ds(place_at, REACH)] = high
            split_ref[1, p, :, pl.ds(place_at, REACH)] = low

    @pl.when(step == tiles)
    def _():
        for k, p in enumerate(edge_points):
            split_ref[0, p, :, pl.ds(place_at, REACH)] = after_ref[k]
            split_ref[1, p, :, pl.ds(place_at, REACH)] = empty

    @pl.when(step > 0)
    def _():
        place = local_columns(nb_ref[...], first_ref[0] - REACH, elements) - (step - 1) * REACH
        start = pl.multiple_of((step - 1) * REACH, REACH)
        change = [None] * 16
        for side, (source, target) in enumerate(sides):
            onehot = jnp.where(
                iota((3 * REACH, REACH), 0) == place[side : side + 1, :], 1.0, 0.0
            ).astype(bf16)
            pieces = [
                split_ref[part, p, :, pl.ds(start, 3 * REACH)]
                for part in range(2)
                for p in source
            ]
            value = dot(jnp.concatenate(pieces, axis=0), onehot)
            for k, p in enumerate(target):
                there = value[k * rows : (k + 1) * rows] + value[(4 + k) * rows : (5 + k) * rows]
                part = there - own_ref[p]
                change[p] = part if change[p] is None else change[p] + part
        for p in range(16):
            new = own_ref[p] if change[p] is None else own_ref[p] + 0.5 * change[p]
            for h in range(2):
                turn_ref[h, pl.ds(p, rows, stride=16), :] = new[:, h * LANES : (h + 1) * LANES]
        for h in range(2):
            out_ref[:, h * LANES : (h + 1) * LANES] = turn_ref[h]


def full_new_state(shape, stepped, before, after, neighbours, first, elements):
    points, rows, size = stepped.shape
    tiles = size // REACH
    tile = (points, rows, REACH)
    out = pl.pallas_call(
        functools.partial(full_edges, elements),
        grid=(tiles + 1,),
        in_specs=[
            pl.BlockSpec(memory_space=pltpu.SMEM),
            pl.BlockSpec(tile, lambda i: (0, 0, jnp.minimum(i, tiles - 1))),
            pl.BlockSpec(tile, lambda i: (0, 0, jnp.maximum(i - 1, 0))),
            whole(before.shape),
            whole(after.shape),
            pl.BlockSpec((4, REACH), lambda i: (0, jnp.maximum(i - 1, 0))),
        ],
        out_specs=pl.BlockSpec((rows * points, REACH), lambda i: (0, jnp.maximum(i - 1, 0))),
        out_shape=jax.ShapeDtypeStruct((rows * points, size), f32),
        scratch_shapes=[
            pltpu.VMEM((2, 16, rows, size + 2 * REACH), bf16),
            pltpu.VMEM((2, rows * points, LANES), f32),
        ],
        compiler_params=params(24),
        cost_estimate=cost(4 * 10**9, 10 << 20),
        name="full_edges",
    )(first, in_hbm(stepped), in_hbm(stepped), before, after, neighbours)
    return out.reshape(shape)


def request_table(grp_ref, cells_ref, ids_ref, out_ref, rank_ref):
    chunks = cells_ref.shape[0]
    owner_at = iota((64, LANES), 0)
    cells = [cells_ref[c : c + 1, :] for c in range(chunks)]
    mine = [jnp.where(owner_at == (cell >> 11), 1.0, 0.0) for cell in cells]
    before = jnp.where(iota((LANES, 2 * LANES), 0) < iota((LANES, 2 * LANES), 1), 1.0, 0.0)
    counts = dot(jnp.concatenate(mine, axis=0).astype(bf16), before.astype(bf16))
    carried = jnp.zeros((64, LANES), f32)
    slots, high, low = [], [], []
    for c, cell in enumerate(cells):
        count = counts[64 * c : 64 * c + 64]
        rank = jnp.sum(mine[c] * (count[:, :LANES] + carried), axis=0, keepdims=True).astype(i32)
        carried = carried + count[:, LANES:]
        rank_ref[c : c + 1, :] = rank
        slots.append(jnp.where(owner_at == rank, 1.0, 0.0).astype(bf16))
        row = cell & 2047
        high.append((mine[c] * (row >> 7).astype(f32)).astype(bf16))
        low.append((mine[c] * (row & 127).astype(f32)).astype(bf16))
    parts = jnp.concatenate([jnp.concatenate(p, axis=1) for p in (high, low)], axis=0)
    wanted = dot_nt(parts, jnp.concatenate(slots, axis=1))
    wanted = wanted[:64] * 128.0 + wanted[64:]
    wanted = jnp.concatenate([wanted, wanted], axis=1)
    share = pltpu.roll(wanted, 64 - 12 * grp_ref[0], 1)
    message = jnp.where(iota((64, LANES), 1) < 64, ids_ref[...].astype(f32), share)
    for y in range(4):
        out_ref[64 * y : 64 * y + 64, :] = message


def requests(grp, ocean_cells, ids):
    chunks = ocean_cells.shape[0] // LANES
    vmem = pl.BlockSpec(memory_space=pltpu.VMEM)
    return pl.pallas_call(
        request_table,
        in_specs=[pl.BlockSpec(memory_space=pltpu.SMEM), vmem, vmem],
        out_shape=[
            jax.ShapeDtypeStruct((256, LANES), f32),
            jax.ShapeDtypeStruct((chunks, LANES), i32),
        ],
        compiler_params=params(),
        name="request_table",
    )(grp, ocean_cells.reshape(chunks, LANES), ids)


QUERIES = 256


def pick_values(table_ref, out_ref, cells_ref, turned_ref, ids_ref, found_ref):
    lane = iota((LANES, LANES), 1)
    asked = table_ref[:, 0, 2 * LANES :]
    ids = jnp.where(lane < 64, asked[:LANES], pltpu.roll(asked[LANES:], 64, 1))
    ids_ref[...] = ids.astype(i32)
    lane = iota((64, LANES), 1)
    wanted = jnp.zeros((64, LANES), f32)
    for y in range(4):
        part = pltpu.roll(asked[64 * y : 64 * y + 64], 64 + 12 * y, 1)
        wanted = jnp.where((lane >= 12 * y) & (lane < 12 * y + 12), part, wanted)
    lane = iota((32, LANES), 1)
    cells_ref[...] = jnp.where(lane < 64, wanted[:32], pltpu.roll(wanted[32:], 64, 1)).astype(i32)

    high, low = split_two(table_ref[:, 0, : 2 * LANES].T)
    for half in range(2):
        turned_ref[half, :LANES] = high[half * LANES : (half + 1) * LANES]
        turned_ref[half, LANES:] = low[half * LANES : (half + 1) * LANES]
    groups = QUERIES // LANES
    device_at = iota((256, QUERIES), 0)
    block_at = iota((LANES, QUERIES), 0)

    def some(step, carry):
        rows = [ids_ref[pl.ds(groups * step + k, 1), :] for k in range(groups)]
        asked = jnp.concatenate(rows, axis=1)
        onehot = jnp.where(device_at == (asked >> 7), 1.0, 0.0).astype(bf16)
        hit = block_at == (asked & 127)
        for half in range(2):
            value = dot(turned_ref[half], onehot)
            part = value[:LANES] + value[LANES:]
            found = jnp.sum(jnp.where(hit, part, 0.0), axis=0, keepdims=True)
            for k in range(groups):
                found_ref[half, pl.ds(groups * step + k, 1), :] = found[
                    :, k * LANES : (k + 1) * LANES
                ]
        return carry

    lax.fori_loop(0, LANES // groups, some, 0, unroll=32)
    lane = iota((LANES, LANES), 1)
    first, second = found_ref[0], found_ref[1]
    out_ref[:LANES, 0, :] = jnp.where(lane < 64, first, pltpu.roll(second, 64, 1))
    out_ref[LANES:, 0, :] = jnp.where(lane < 64, pltpu.roll(first, 64, 1), second)


def picked(table):
    return pl.pallas_call(
        pick_values,
        out_shape=[
            pltpu.HBM((256, 1, LANES), f32),
            jax.ShapeDtypeStruct((32, LANES), i32),
        ],
        scratch_shapes=[
            pltpu.VMEM((2, 256, 256), bf16),
            pltpu.VMEM((LANES, LANES), i32),
            pltpu.VMEM((2, LANES, LANES), f32),
        ],
        compiler_params=params(24),
        name="pick_values",
    )(table)


def remap_rows(
    grp_ref, fw_ref, got_ref, index_ref, w_ref, out_ref, field_ref, mapped_ref, sent_ref, pair_ref
):
    values = []
    for v in range(4):
        turned = got_ref[64 * v : 64 * v + 64, 0, :].T
        values.append(jnp.concatenate([turned[:64], turned[64:]], axis=1))
    wind = jnp.sqrt(1.0 + values[0] * values[0] + values[1] * values[1])
    for f in range(16):
        if f < 12:
            total = fw_ref[f, 0] * values[0]
            for v in range(1, 4):
                total += fw_ref[f, v] * values[v]
            total = (total * wind).astype(bf16).astype(f32)
        else:
            total = jnp.zeros((64, LANES), f32)
        field_ref[pl.ds(f, 64, stride=16), :] = total

    for r in range(4):
        total = jnp.zeros((16, LANES), f32)
        for b in range(0, 16, 2):
            at = (r * 16 + b) * 16
            pair = field_ref[at : at + 32, :].astype(bf16)
            pair = jnp.concatenate([pair[:16], pair[16:]], axis=1)
            weights = jnp.concatenate([w_ref[r, b], w_ref[r, b + 1]], axis=1)
            total += dot_nt(pair, weights)
        mapped_ref[16 * r : 16 * r + 16, :] = total

    parts = jnp.concatenate(split_two(mapped_ref[...]), axis=0)
    row_at = iota((LANES, 4 * LANES), 0)

    def some(at, carry):
        rows = [index_ref[pl.ds(4 * at + k, 1), :] for k in range(4)]
        asked = jnp.concatenate(rows, axis=1)
        onehot = jnp.where(row_at == (asked & 127), 1.0, 0.0).astype(bf16)
        value = dot(parts, onehot)
        value = value[:64] + value[64:]
        block = (asked >> 7) - 4 * grp_ref[0]
        found = jnp.where(block == 0, value[:16], 0.0)
        for r in range(1, 4):
            found = jnp.where(block == r, value[16 * r : 16 * r + 16], found)
        for k in range(4):
            sent_ref[pl.ds(4 * at + k, 16, stride=32), :] = found[
                :, k * LANES : (k + 1) * LANES
            ]
        return carry

    lax.fori_loop(0, 8, some, 0, unroll=True)
    lane = iota((32, LANES), 1)
    for y in range(4):
        a, b, c = [sent_ref[(3 * y + f) * 32 : (3 * y + f) * 32 + 32, :] for f in range(3)]
        base = 64 * y
        low, high = slice(base, base + 32), slice(base + 32, base + 64)
        pair_ref[low, 0, :] = jnp.where(lane < 64, a, pltpu.roll(b, 64, 1))
        pair_ref[low, 1, :] = c
        pair_ref[high, 0, :] = jnp.where(lane < 64, pltpu.roll(a, 64, 1), b)
        pair_ref[high, 1, :] = pltpu.roll(c, 64, 1)
    out_ref[...] = pair_ref[...].astype(bf16)


def remapped_cells(grp, flux_weight, got, index, block_weights):
    smem = pl.BlockSpec(memory_space=pltpu.SMEM)
    vmem = pl.BlockSpec(memory_space=pltpu.VMEM)
    return pl.pallas_call(
        remap_rows,
        in_specs=[smem, smem, vmem, vmem, vmem],
        out_shape=jax.ShapeDtypeStruct((256, 2, LANES), bf16),
        scratch_shapes=[
            pltpu.VMEM((64 * 16, LANES), f32),
            pltpu.VMEM((64, LANES), f32),
            pltpu.VMEM((16 * 32, LANES), f32),
            pltpu.VMEM((256, 2, LANES), f32),
        ],
        compiler_params=params(),
        name="remap_rows",
    )(grp, flux_weight, got, index, block_weights)


def place_cells(got_ref, cells_ref, rank_ref, out_ref):
    got = got_ref[...].astype(f32)
    got = got[0:64] + got[64:128] + got[128:192] + got[192:256]
    pair, last = got[:, 0, :].T, got[:, 1, :].T
    parts = jnp.concatenate([pair, last[:64]], axis=0).astype(bf16)
    owner_at = iota((64, 4 * LANES), 0)
    for c in range(4):
        rows = range(4 * c, 4 * c + 4)
        cell = jnp.concatenate([cells_ref[r : r + 1, :] for r in rows], axis=1)
        rank = jnp.concatenate([rank_ref[r : r + 1, :] for r in rows], axis=1)
        onehot = jnp.where(owner_at == (cell >> 11), 1.0, 0.0).astype(bf16)
        value = dot(parts, onehot)
        hit = owner_at == rank
        for f in range(3):
            out_ref[f : f + 1, c * 4 * LANES : (c + 1) * 4 * LANES] = jnp.sum(
                jnp.where(hit, value[64 * f : 64 * f + 64], 0.0), axis=0, keepdims=True
            )


def placed(got, ocean_cells, rank):
    count = ocean_cells.shape[0]
    return pl.pallas_call(
        place_cells,
        out_shape=jax.ShapeDtypeStruct((3, count), f32),
        compiler_params=params(),
        name="place_cells",
    )(got, ocean_cells.reshape(count // LANES, LANES), rank)


def upward():
    count = lax.axis_size(both)
    return [(i, (i + 1) % count) for i in range(count)]


def around(first, last):
    up = upward()
    down = [(j, i) for i, j in up]
    return lax.ppermute(last, both, up), lax.ppermute(first, both, down)


def exchange(x, axis):
    return lax.all_to_all(x, axis, split_axis=0, concat_axis=0, tiled=True)


def body(atmos_state, neighbours, flux_weight, block_weights, block_ids, block_counts, ocean_cells):
    size = atmos_state.shape[3]
    elements = size * lax.axis_size(both)
    grp = lax.axis_index("grp").astype(i32).reshape(1)
    first = (lax.axis_index(both) * size).astype(i32).reshape(1)

    stepped, rim = bottom_stepped(atmos_state, neighbours)
    prev = lax.ppermute(rim, both, upward())

    shift = REACH // LANES * 16
    blocks = elements // LANES * 16
    live = jnp.arange(block_ids.shape[1])[None, :] < block_counts[:, None]
    ids = jnp.where(live, (block_ids + shift) % blocks, -1).reshape(4, 64)
    ids = lax.dynamic_slice_in_dim(ids, lax.axis_index("grp"), 1, 0)
    ids = jnp.concatenate([ids, ids], axis=1)
    request, rank = requests(grp, ocean_cells, ids)

    inner = bottom_inner(stepped, neighbours, first, elements)
    slices = bottom_slices(stepped, prev, neighbours, inner, request, first, elements)
    table = exchange(slices, both)
    all_stepped, all_low, all_high = full_stepped(atmos_state)
    all_before, all_after = around(all_low, all_high)
    new_state = full_new_state(
        atmos_state.shape, all_stepped, all_before, all_after, neighbours, first, elements
    )

    answer, wanted = picked(table)
    answer, block_weights = lax.optimization_barrier((answer, block_weights))
    weights = lax.dynamic_slice_in_dim(block_weights, 4 * grp[0], 4, 0)
    got = exchange(answer, both)
    sent = remapped_cells(grp, flux_weight, got, wanted, weights)
    ocean_flux = placed(exchange(sent, both), ocean_cells, rank)
    return new_state, ocean_flux


def solution(mesh):
    in_specs = (
        P(None, None, None, both),
        P(None, both),
        P(),
        P("blk", None, None, None),
        P("blk", None),
        P("blk"),
        P("blk"),
    )
    out_specs = (P(None, None, None, both), P("grp", "blk"))
    return jax.shard_map(body, mesh=mesh, in_specs=in_specs, out_specs=out_specs, check_vma=False)
```

```python
import functools

import jax
import jax.numpy as jnp
import ml_dtypes
import numpy as np
from jax import lax
from jax.experimental import pallas as pl
from jax.experimental.pallas import tpu as pltpu
from jax.sharding import PartitionSpec as P

time_step = 0.02
viscosity = 0.05
LANES = 128
REACH = 256
f32 = jnp.float32
bf16 = jnp.bfloat16
i32 = jnp.int32
both = ("grp", "blk")


def params(mebibytes=16):
    return pltpu.CompilerParams(vmem_limit_bytes=mebibytes * 1024 * 1024)


def in_hbm(x):
    return pltpu.with_memory_space_constraint(x, pltpu.HBM)


def cost(flops, moved):
    return pl.CostEstimate(flops=flops, bytes_accessed=moved, transcendentals=0)


def whole(shape):
    return pl.BlockSpec(shape, lambda *_: (0,) * len(shape))


def derivative_matrix():
    nodes = np.array([-1.0, -1.0 / np.sqrt(5.0), 1.0 / np.sqrt(5.0), 1.0])
    others = [[k for k in range(4) if k != n] for n in range(4)]
    weights = [np.prod([nodes[n] - nodes[k] for k in others[n]]) for n in range(4)]
    matrix = np.zeros((4, 4))
    for a in range(4):
        for c in range(4):
            if a != c:
                matrix[a, c] = weights[a] / weights[c] / (nodes[a] - nodes[c])
            else:
                matrix[a, a] = sum(1.0 / (nodes[a] - nodes[k]) for k in others[a])
    return matrix


def operators(copies):
    d = derivative_matrix().astype(np.float32).astype(np.float64)
    east, north = np.kron(np.eye(4), d), np.kron(d, np.eye(4))
    bend = east @ east + north @ north
    parts = [-time_step * east, -time_step * north, time_step * viscosity * bend]
    stacked = np.concatenate([np.kron(np.eye(copies), part) for part in parts])
    high = stacked.astype(ml_dtypes.bfloat16)
    low = (stacked - high.astype(np.float64)).astype(ml_dtypes.bfloat16)
    return jnp.asarray(high), jnp.asarray(low)


def split_two(x):
    high = x.astype(bf16)
    return high, (x - high.astype(f32)).astype(bf16)


def dot(a, b):
    return jnp.dot(a, b, preferred_element_type=f32)


def dot_nt(a, b):
    return lax.dot_general(a, b, (((1,), (1,)), ((), ())), preferred_element_type=f32)


def apply_operators(high, low, x):
    xh, xl = split_two(x)
    return dot(high, xh) + dot(high, xl) + dot(low, xh)


def iota(shape, dim):
    return lax.broadcasted_iota(i32, shape, dim)


def bottom_step(x_ref, nb_ref, high_ref, low_ref, out_ref, rim_ref):
    x = x_ref[:, 0].reshape(64, -1)
    op = apply_operators(high_ref[...], low_ref[...], x)
    size = x.shape[1]
    for v in range(4):
        rows = slice(16 * v, 16 * v + 16)
        stepped = (
            x[rows] + x[0:16] * op[rows] + x[16:32] * op[64:128][rows] + op[128:192][rows]
        )
        out_ref[rows] = stepped
        rim_ref[rows] = stepped[:, size - 2 * REACH :]
        rim_ref[16 * v + 5 : 16 * v + 6, :REACH] = nb_ref[v : v + 1].astype(f32)


def bottom_stepped(state, neighbours):
    nvar, levels, points, size = state.shape
    high, low = operators(nvar)
    rim = (nvar * points, 2 * REACH)
    return pl.pallas_call(
        bottom_step,
        grid=(1,),
        in_specs=[
            pl.BlockSpec((nvar, 1, points, size), lambda i: (0, levels - 1, 0, 0)),
            pl.BlockSpec((4, REACH), lambda i: (0, size // REACH - 1)),
            whole(high.shape),
            whole(low.shape),
        ],
        out_specs=[pl.BlockSpec(memory_space=pltpu.VMEM), whole(rim)],
        out_shape=[pltpu.VMEM((nvar * points, size), f32), jax.ShapeDtypeStruct(rim, f32)],
        compiler_params=params(),
        name="bottom_step",
    )(in_hbm(state), in_hbm(neighbours), in_hbm(high), in_hbm(low))


def line_operators():
    d = derivative_matrix()
    d2 = d @ d
    slope = [
        (
            0.5 * (d[i, 0] - d[i, 3]),
            0.5 * (d[i, 1] - d[i, 2]),
            0.5 * (d[i, 0] + d[i, 3]),
        )
        for i in range(2)
    ]
    bend = [
        (
            0.5 * (d2[i, 0] - d2[i, 3]),
            0.5 * (d2[i, 1] - d2[i, 2]),
            0.5 * (d2[i, 0] + d2[i, 3]),
        )
        for i in range(2)
    ]
    return slope, bend


def along_line(x, slope, bend):
    t0, t1 = x[0] - x[3], x[1] - x[2]
    mean = (x[0] + x[3]) - (x[1] + x[2])
    first, second = [None] * 4, [None] * 4
    for i in range(2):
        a, b, c = [np.float32(-time_step * k) for k in slope[i]]
        even, odd = a * t0 + b * t1, c * mean
        first[i], first[3 - i] = even + odd, even - odd
        a, b, c = [np.float32(time_step * viscosity * k) for k in bend[i]]
        odd, even = a * t0 + b * t1, c * mean
        second[i], second[3 - i] = even + odd, even - odd
    return first, second


edge_points = (0, 1, 2, 3, 4, 7, 8, 11, 12, 13, 14, 15)


def full_step(x_ref, out_ref, first_ref, last_ref):
    step = pl.program_id(0)
    count = pl.num_programs(0)
    slope, bend = line_operators()

    def points(v, half):
        start = (v * 16 + half * 8) * 16
        return [x_ref[pl.ds(start + p, 8, stride=16), :] for p in range(16)]

    for half in range(2):
        u, w = points(0, half), points(1, half)
        for v in range(4):
            x = u if v == 0 else w if v == 1 else points(v, half)
            total = list(x)
            for a in range(4):
                at = [4 * a + b for b in range(4)]
                first, second = along_line([x[p] for p in at], slope, bend)
                for p, one, two in zip(at, first, second):
                    total[p] = total[p] + (u[p] * one + two)
            for b in range(4):
                at = [4 * a + b for a in range(4)]
                first, second = along_line([x[p] for p in at], slope, bend)
                for p, one, two in zip(at, first, second):
                    total[p] = total[p] + (w[p] * one + two)
            for p in range(16):
                out_ref[p, v * 16 + half * 8 : v * 16 + half * 8 + 8, :] = total[p]

    for part in range(2):
        cols = slice(part * LANES, (part + 1) * LANES)

        @pl.when(step == part)
        def _():
            for k, p in enumerate(edge_points):
                first_ref[k, :, cols] = out_ref[p].astype(bf16)

        @pl.when(step == count - 2 + part)
        def _():
            for k, p in enumerate(edge_points):
                last_ref[k, :, cols] = out_ref[p].astype(bf16)


def full_stepped(state):
    nvar, levels, points, size = state.shape
    rows = nvar * levels
    rim = (len(edge_points), rows, REACH)
    return pl.pallas_call(
        full_step,
        grid=(size // LANES,),
        in_specs=[pl.BlockSpec((rows * points, LANES), lambda i: (0, i))],
        out_specs=[
            pl.BlockSpec((points, rows, LANES), lambda i: (0, 0, i)),
            whole(rim),
            whole(rim),
        ],
        out_shape=[
            pltpu.HBM((points, rows, size), f32),
            jax.ShapeDtypeStruct(rim, bf16),
            jax.ShapeDtypeStruct(rim, bf16),
        ],
        compiler_params=params(24),
        cost_estimate=cost(4 * 10**7, 9 << 20),
        name="full_step",
    )(in_hbm(state.reshape(rows * points, size)))


def local_columns(neighbours, start, elements):
    place = neighbours - start
    place = jnp.where(place < 0, place + elements, place)
    return jnp.where(place >= elements, place - elements, place)


def side_indices(place, rows):
    part = [jnp.broadcast_to(place[s : s + 1], (rows, LANES)) for s in range(4)]
    point = iota((rows, LANES), 0) % 8
    we = jnp.where(point % 4 == 3, part[0], part[1])
    ns = jnp.where(point < 4, part[3], part[2])
    return we, ns


def look_up(columns, index, eb):
    lane = index & (LANES - 1)
    column = (index >> 7) - eb
    value = jnp.take_along_axis(columns[0], lane, axis=1)
    for c in range(1, 5):
        value = jnp.where(column == c, jnp.take_along_axis(columns[c], lane, axis=1), value)
    return value


def halves(x):
    grouped = x.reshape(x.shape[0] // 16, 2, 8, x.shape[1])
    shape = (x.shape[0] // 2, x.shape[1])
    return grouped[:, 0].reshape(shape), grouped[:, 1].reshape(shape)


def edge_update(columns, we, ns, eb):
    pairs = [halves(column) for column in columns]
    rows = pairs[0][0].shape[0]
    point = iota(pairs[0][0].shape, 0) % 8
    first = point < 4
    across = look_up([jnp.where(first, low, high) for low, high in pairs], ns, eb)
    zero = jnp.zeros(first.shape, f32)
    done = []
    for side in range(2):
        own = pairs[2][side]
        beside = look_up([pair[side] for pair in pairs], we, eb)
        total = jnp.where(point % 4 == 0, pltpu.roll(beside, rows - 3, 0) - own, zero)
        total += jnp.where(point % 4 == 3, pltpu.roll(beside, 3, 0) - own, zero)
        if side == 0:
            total += jnp.where(first, pltpu.roll(across, rows - 4, 0) - own, zero)
        else:
            total += jnp.where(first, zero, pltpu.roll(across, 4, 0) - own)
        done.append((own + 0.5 * total).reshape(-1, 1, 8, own.shape[1]))
    return jnp.concatenate(done, axis=1).reshape(columns[0].shape)


def lane_tiles(ref, count):
    return [ref[:, c * LANES : (c + 1) * LANES] for c in range(count)]


def inner_edges(elements, first_ref, s_ref, nb_ref, out_ref):
    size = s_ref.shape[1]
    place = local_columns(nb_ref[...], first_ref[0], elements)
    tiles = lane_tiles(s_ref, size // LANES)
    for eb in range(size // LANES - 4):
        cols = slice(eb * LANES + REACH, eb * LANES + REACH + LANES)
        we, ns = side_indices(place[:, cols], 32)
        out_ref[:, eb * LANES : (eb + 1) * LANES] = edge_update(tiles[eb : eb + 5], we, ns, eb)


def bottom_inner(stepped, neighbours, first, elements):
    rows, size = stepped.shape
    vmem = pl.BlockSpec(memory_space=pltpu.VMEM)
    return pl.pallas_call(
        functools.partial(inner_edges, elements),
        in_specs=[pl.BlockSpec(memory_space=pltpu.SMEM), vmem, vmem],
        out_specs=vmem,
        out_shape=pltpu.VMEM((rows, size - 2 * REACH), f32),
        compiler_params=params(),
        name="bottom_inner",
    )(first, stepped, neighbours)


def bottom_edges(elements, first_ref, s_ref, prev_ref, nb_ref, inner_ref, request_ref, out_ref):
    out_ref[:, 0, 2 * LANES :] = request_ref[...]
    edge = 2 * REACH // LANES
    carried = [prev_ref[16 * v + 5 : 16 * v + 6, :REACH] for v in range(4)]
    neighbours = jnp.concatenate(
        [jnp.concatenate(carried, axis=0).astype(i32), nb_ref[:, :REACH]], axis=1
    )
    place = local_columns(neighbours, first_ref[0] - 2 * REACH, elements)
    tiles = lane_tiles(prev_ref, edge) + lane_tiles(s_ref, edge)
    new = []
    for eb in range(edge):
        we, ns = side_indices(place[:, eb * LANES : (eb + 1) * LANES], 32)
        new.append(edge_update(tiles[eb : eb + 5], we, ns, eb))
    new += lane_tiles(inner_ref, inner_ref.shape[1] // LANES)
    for v in range(4):
        blocks = jnp.concatenate([piece[16 * v : 16 * v + 16] for piece in new], axis=0)
        turned = blocks.T
        for g in range(4):
            rows = slice(64 * g + 16 * v, 64 * g + 16 * v + 16)
            for h in range(2):
                at = 32 * g + 16 * h
                out_ref[rows, 0, h * LANES : (h + 1) * LANES] = turned[at : at + 16]


def bottom_slices(stepped, prev, neighbours, inner, request, first, elements):
    vmem = pl.BlockSpec(memory_space=pltpu.VMEM)
    return pl.pallas_call(
        functools.partial(bottom_edges, elements),
        in_specs=[pl.BlockSpec(memory_space=pltpu.SMEM)] + [vmem] * 5,
        out_shape=jax.ShapeDtypeStruct((256, 1, 3 * LANES), f32),
        compiler_params=params(),
        name="bottom_edges",
    )(first, stepped, prev, neighbours, inner, request)


sides = (
    ((3, 7, 11, 15), (0, 4, 8, 12)),
    ((0, 4, 8, 12), (3, 7, 11, 15)),
    ((12, 13, 14, 15), (0, 1, 2, 3)),
    ((0, 1, 2, 3), (12, 13, 14, 15)),
)


def full_edges(
    elements,
    first_ref,
    ahead_ref,
    own_ref,
    before_ref,
    after_ref,
    nb_ref,
    out_ref,
    split_ref,
    turn_ref,
):
    step = pl.program_id(0)
    tiles = pl.num_programs(0) - 1
    rows = own_ref.shape[1]
    empty = jnp.zeros((rows, REACH), bf16)

    @pl.when(step == 0)
    def _():
        for k, p in enumerate(edge_points):
            split_ref[0, p, :, :REACH] = before_ref[k]
            split_ref[1, p, :, :REACH] = empty

    place_at = pl.multiple_of((step + 1) * REACH, REACH)

    @pl.when(step < tiles)
    def _():
        for p in edge_points:
            high, low = split_two(ahead_ref[p])
            split_ref[0, p, :, pl.ds(place_at, REACH)] = high
            split_ref[1, p, :, pl.ds(place_at, REACH)] = low

    @pl.when(step == tiles)
    def _():
        for k, p in enumerate(edge_points):
            split_ref[0, p, :, pl.ds(place_at, REACH)] = after_ref[k]
            split_ref[1, p, :, pl.ds(place_at, REACH)] = empty

    @pl.when(step > 0)
    def _():
        place = local_columns(nb_ref[...], first_ref[0] - REACH, elements) - (step - 1) * REACH
        start = pl.multiple_of((step - 1) * REACH, REACH)
        change = [None] * 16
        for side, (source, target) in enumerate(sides):
            onehot = jnp.where(
                iota((3 * REACH, REACH), 0) == place[side : side + 1, :], 1.0, 0.0
            ).astype(bf16)
            pieces = [
                split_ref[part, p, :, pl.ds(start, 3 * REACH)]
                for part in range(2)
                for p in source
            ]
            value = dot(jnp.concatenate(pieces, axis=0), onehot)
            for k, p in enumerate(target):
                there = value[k * rows : (k + 1) * rows] + value[(4 + k) * rows : (5 + k) * rows]
                part = there - own_ref[p]
                change[p] = part if change[p] is None else change[p] + part
        for p in range(16):
            new = own_ref[p] if change[p] is None else own_ref[p] + 0.5 * change[p]
            for h in range(2):
                turn_ref[h, pl.ds(p, rows, stride=16), :] = new[:, h * LANES : (h + 1) * LANES]
        for h in range(2):
            out_ref[:, h * LANES : (h + 1) * LANES] = turn_ref[h]


def full_new_state(shape, stepped, before, after, neighbours, first, elements):
    points, rows, size = stepped.shape
    tiles = size // REACH
    tile = (points, rows, REACH)
    out = pl.pallas_call(
        functools.partial(full_edges, elements),
        grid=(tiles + 1,),
        in_specs=[
            pl.BlockSpec(memory_space=pltpu.SMEM),
            pl.BlockSpec(tile, lambda i: (0, 0, jnp.minimum(i, tiles - 1))),
            pl.BlockSpec(tile, lambda i: (0, 0, jnp.maximum(i - 1, 0))),
            whole(before.shape),
            whole(after.shape),
            pl.BlockSpec((4, REACH), lambda i: (0, jnp.maximum(i - 1, 0))),
        ],
        out_specs=pl.BlockSpec((rows * points, REACH), lambda i: (0, jnp.maximum(i - 1, 0))),
        out_shape=jax.ShapeDtypeStruct((rows * points, size), f32),
        scratch_shapes=[
            pltpu.VMEM((2, 16, rows, size + 2 * REACH), bf16),
            pltpu.VMEM((2, rows * points, LANES), f32),
        ],
        compiler_params=params(24),
        cost_estimate=cost(4 * 10**9, 10 << 20),
        name="full_edges",
    )(first, in_hbm(stepped), in_hbm(stepped), before, after, neighbours)
    return out.reshape(shape)


def request_table(grp_ref, cells_ref, ids_ref, out_ref, rank_ref):
    chunks = cells_ref.shape[0]
    owner_at = iota((64, LANES), 0)
    cells = [cells_ref[c : c + 1, :] for c in range(chunks)]
    mine = [jnp.where(owner_at == (cell >> 11), 1.0, 0.0) for cell in cells]
    before = jnp.where(iota((LANES, 2 * LANES), 0) < iota((LANES, 2 * LANES), 1), 1.0, 0.0)
    counts = dot(jnp.concatenate(mine, axis=0).astype(bf16), before.astype(bf16))
    carried = jnp.zeros((64, LANES), f32)
    slots, high, low = [], [], []
    for c, cell in enumerate(cells):
        count = counts[64 * c : 64 * c + 64]
        rank = jnp.sum(mine[c] * (count[:, :LANES] + carried), axis=0, keepdims=True).astype(i32)
        carried = carried + count[:, LANES:]
        rank_ref[c : c + 1, :] = rank
        slots.append(jnp.where(owner_at == rank, 1.0, 0.0).astype(bf16))
        row = cell & 2047
        high.append((mine[c] * (row >> 7).astype(f32)).astype(bf16))
        low.append((mine[c] * (row & 127).astype(f32)).astype(bf16))
    parts = jnp.concatenate([jnp.concatenate(p, axis=1) for p in (high, low)], axis=0)
    wanted = dot_nt(parts, jnp.concatenate(slots, axis=1))
    wanted = wanted[:64] * 128.0 + wanted[64:]
    wanted = jnp.concatenate([wanted, wanted], axis=1)
    share = pltpu.roll(wanted, 64 - 12 * grp_ref[0], 1)
    message = jnp.where(iota((64, LANES), 1) < 64, ids_ref[...].astype(f32), share)
    for y in range(4):
        out_ref[64 * y : 64 * y + 64, :] = message


def requests(grp, ocean_cells, ids):
    chunks = ocean_cells.shape[0] // LANES
    vmem = pl.BlockSpec(memory_space=pltpu.VMEM)
    return pl.pallas_call(
        request_table,
        in_specs=[pl.BlockSpec(memory_space=pltpu.SMEM), vmem, vmem],
        out_shape=[
            jax.ShapeDtypeStruct((256, LANES), f32),
            jax.ShapeDtypeStruct((chunks, LANES), i32),
        ],
        compiler_params=params(),
        name="request_table",
    )(grp, ocean_cells.reshape(chunks, LANES), ids)


QUERIES = 256


def pick_values(table_ref, out_ref, cells_ref, turned_ref, ids_ref, found_ref):
    lane = iota((LANES, LANES), 1)
    asked = table_ref[:, 0, 2 * LANES :]
    ids = jnp.where(lane < 64, asked[:LANES], pltpu.roll(asked[LANES:], 64, 1))
    ids_ref[...] = ids.astype(i32)
    lane = iota((64, LANES), 1)
    wanted = jnp.zeros((64, LANES), f32)
    for y in range(4):
        part = pltpu.roll(asked[64 * y : 64 * y + 64], 64 + 12 * y, 1)
        wanted = jnp.where((lane >= 12 * y) & (lane < 12 * y + 12), part, wanted)
    lane = iota((32, LANES), 1)
    cells_ref[...] = jnp.where(lane < 64, wanted[:32], pltpu.roll(wanted[32:], 64, 1)).astype(i32)

    high, low = split_two(table_ref[:, 0, : 2 * LANES].T)
    for half in range(2):
        turned_ref[half, :LANES] = high[half * LANES : (half + 1) * LANES]
        turned_ref[half, LANES:] = low[half * LANES : (half + 1) * LANES]
    groups = QUERIES // LANES
    device_at = iota((256, QUERIES), 0)
    block_at = iota((LANES, QUERIES), 0)

    def some(step, carry):
        rows = [ids_ref[pl.ds(groups * step + k, 1), :] for k in range(groups)]
        asked = jnp.concatenate(rows, axis=1)
        onehot = jnp.where(device_at == (asked >> 7), 1.0, 0.0).astype(bf16)
        hit = block_at == (asked & 127)
        for half in range(2):
            value = dot(turned_ref[half], onehot)
            part = value[:LANES] + value[LANES:]
            found = jnp.sum(jnp.where(hit, part, 0.0), axis=0, keepdims=True)
            for k in range(groups):
                found_ref[half, pl.ds(groups * step + k, 1), :] = found[
                    :, k * LANES : (k + 1) * LANES
                ]
        return carry

    lax.fori_loop(0, LANES // groups, some, 0, unroll=32)
    for half in range(2):
        for y in range(2):
            at = (2 * half + y) * LANES
            out_ref[:, 0, at : at + LANES] = found_ref[half, 64 * y : 64 * y + 64, :]


def picked(table):
    return pl.pallas_call(
        pick_values,
        out_shape=[
            pltpu.HBM((64, 1, 4 * LANES), f32),
            jax.ShapeDtypeStruct((32, LANES), i32),
        ],
        scratch_shapes=[
            pltpu.VMEM((2, 256, 256), bf16),
            pltpu.VMEM((LANES, LANES), i32),
            pltpu.VMEM((2, LANES, LANES), f32),
        ],
        compiler_params=params(24),
        name="pick_values",
    )(table)


def quarter_weights(grp_ref, w_ref, out_ref):
    column, lane = iota((4 * LANES, LANES), 0), iota((4 * LANES, LANES), 1)
    wanted = (column // LANES == lane // 32) & (
        column % LANES == 32 * grp_ref[0] + lane % 32
    )
    chosen = jnp.where(wanted, 1.0, 0.0).astype(bf16)
    at = [(r, b) for r in range(w_ref.shape[0]) for b in range(4)]
    rows = [
        jnp.concatenate([w_ref[r, 4 * b + q] for q in range(4)], axis=1) for r, b in at
    ]
    packed = dot(jnp.concatenate(rows, axis=0), chosen).astype(bf16)
    for k, (r, b) in enumerate(at):
        out_ref[r, b] = packed[LANES * k : LANES * (k + 1)]


def packed_weights(grp, block_weights):
    count, slots, block = block_weights.shape[:3]
    step = 8
    return pl.pallas_call(
        quarter_weights,
        grid=(count // step,),
        in_specs=[
            pl.BlockSpec(memory_space=pltpu.SMEM),
            pl.BlockSpec((step, slots, block, block), lambda i: (i, 0, 0, 0)),
        ],
        out_specs=pl.BlockSpec((step, slots // 4, block, block), lambda i: (i, 0, 0, 0)),
        out_shape=jax.ShapeDtypeStruct((count, slots // 4, block, block), bf16),
        compiler_params=params(),
        cost_estimate=cost(10**9, 10 << 20),
        name="quarter_weights",
    )(grp, in_hbm(block_weights))


def remap_rows(
    fw_ref, got_ref, index_ref, w_ref, out_ref, field_ref, mapped_ref, sent_ref, pair_ref
):
    values = []
    for v in range(4):
        rows = slice(16 * v, 16 * v + 16)
        tiles = [
            got_ref[rows, 0, (2 * h + y) * LANES : (2 * h + y + 1) * LANES]
            for y in range(2)
            for h in range(2)
        ]
        turned = jnp.concatenate(tiles, axis=0).T
        values.append(jnp.concatenate([turned[:64], turned[64:]], axis=1))
    wind = jnp.sqrt(1.0 + values[0] * values[0] + values[1] * values[1])
    for f in range(16):
        if f < 12:
            total = fw_ref[f, 0] * values[0]
            for v in range(1, 4):
                total += fw_ref[f, v] * values[v]
            total = (total * wind).astype(bf16).astype(f32)
        else:
            total = jnp.zeros((64, LANES), f32)
        field_ref[pl.ds(f, 64, stride=16), :] = total

    for r in range(16):
        total = jnp.zeros((16, LANES), f32)
        for b in range(0, 4, 2):
            at = (r * 4 + b) * 16
            pair = field_ref[at : at + 32, :].astype(bf16)
            pair = jnp.concatenate([pair[:16], pair[16:]], axis=1)
            weights = jnp.concatenate([w_ref[r, b], w_ref[r, b + 1]], axis=1)
            total += dot_nt(pair, weights)
        mapped_ref[16 * r : 16 * r + 16, :] = total

    parts = jnp.concatenate(split_two(mapped_ref[...]), axis=0)
    row_at = iota((LANES, 4 * LANES), 0)

    def some(at, carry):
        rows = [index_ref[pl.ds(4 * at + k, 1), :] for k in range(4)]
        asked = jnp.concatenate(rows, axis=1)
        onehot = jnp.where(row_at == (asked & 127), 1.0, 0.0).astype(bf16)
        value = dot(parts, onehot)
        value = value[:256] + value[256:]
        block = asked >> 7
        found = value[:16]
        for r in range(1, 16):
            found = jnp.where(block == r, value[16 * r : 16 * r + 16], found)
        for k in range(4):
            sent_ref[pl.ds(4 * at + k, 16, stride=32), :] = found[
                :, k * LANES : (k + 1) * LANES
            ]
        return carry

    lax.fori_loop(0, 8, some, 0, unroll=True)
    lane = iota((32, LANES), 1)
    for y in range(4):
        a, b, c = [sent_ref[(3 * y + f) * 32 : (3 * y + f) * 32 + 32, :] for f in range(3)]
        base = 64 * y
        low, high = slice(base, base + 32), slice(base + 32, base + 64)
        pair_ref[low, 0, :] = jnp.where(lane < 64, a, pltpu.roll(b, 64, 1))
        pair_ref[low, 1, :] = c
        pair_ref[high, 0, :] = jnp.where(lane < 64, pltpu.roll(a, 64, 1), b)
        pair_ref[high, 1, :] = pltpu.roll(c, 64, 1)
    out_ref[...] = pair_ref[...].astype(bf16)


def remapped_cells(flux_weight, got, index, block_weights):
    smem = pl.BlockSpec(memory_space=pltpu.SMEM)
    vmem = pl.BlockSpec(memory_space=pltpu.VMEM)
    return pl.pallas_call(
        remap_rows,
        in_specs=[smem, vmem, vmem, vmem],
        out_shape=jax.ShapeDtypeStruct((256, 2, LANES), bf16),
        scratch_shapes=[
            pltpu.VMEM((64 * 16, LANES), f32),
            pltpu.VMEM((256, LANES), f32),
            pltpu.VMEM((16 * 32, LANES), f32),
            pltpu.VMEM((256, 2, LANES), f32),
        ],
        compiler_params=params(),
        name="remap_rows",
    )(flux_weight, got, index, block_weights)


def place_cells(got_ref, cells_ref, rank_ref, out_ref):
    got = got_ref[...].astype(f32)
    got = got[0:64] + got[64:128] + got[128:192] + got[192:256]
    pair, last = got[:, 0, :].T, got[:, 1, :].T
    parts = jnp.concatenate([pair, last[:64]], axis=0).astype(bf16)
    owner_at = iota((64, 4 * LANES), 0)
    for c in range(4):
        rows = range(4 * c, 4 * c + 4)
        cell = jnp.concatenate([cells_ref[r : r + 1, :] for r in rows], axis=1)
        rank = jnp.concatenate([rank_ref[r : r + 1, :] for r in rows], axis=1)
        onehot = jnp.where(owner_at == (cell >> 11), 1.0, 0.0).astype(bf16)
        value = dot(parts, onehot)
        hit = owner_at == rank
        for f in range(3):
            out_ref[f : f + 1, c * 4 * LANES : (c + 1) * 4 * LANES] = jnp.sum(
                jnp.where(hit, value[64 * f : 64 * f + 64], 0.0), axis=0, keepdims=True
            )


def placed(got, ocean_cells, rank):
    count = ocean_cells.shape[0]
    return pl.pallas_call(
        place_cells,
        out_shape=jax.ShapeDtypeStruct((3, count), f32),
        compiler_params=params(),
        name="place_cells",
    )(got, ocean_cells.reshape(count // LANES, LANES), rank)


def upward():
    count = lax.axis_size(both)
    return [(i, (i + 1) % count) for i in range(count)]


def around(first, last):
    up = upward()
    down = [(j, i) for i, j in up]
    return lax.ppermute(last, both, up), lax.ppermute(first, both, down)


def exchange(x, axis):
    return lax.all_to_all(x, axis, split_axis=0, concat_axis=0, tiled=True)


def body(atmos_state, neighbours, flux_weight, block_weights, block_ids, block_counts, ocean_cells):
    size = atmos_state.shape[3]
    elements = size * lax.axis_size(both)
    grp = lax.axis_index("grp").astype(i32).reshape(1)
    first = (lax.axis_index(both) * size).astype(i32).reshape(1)

    stepped, rim = bottom_stepped(atmos_state, neighbours)
    prev = lax.ppermute(rim, both, upward())

    shift = REACH // LANES * 16
    blocks = elements // LANES * 16
    live = jnp.arange(block_ids.shape[1])[None, :] < block_counts[:, None]
    ids = jnp.where(live, (block_ids + shift) % blocks, -1)
    ids = ids.reshape(-1, 4, 4).transpose(2, 0, 1).reshape(4, 64)
    ids = lax.dynamic_slice_in_dim(ids, lax.axis_index("grp"), 1, 0)
    ids = jnp.concatenate([ids, ids], axis=1)
    request, rank = requests(grp, ocean_cells, ids)

    inner = bottom_inner(stepped, neighbours, first, elements)
    slices = bottom_slices(stepped, prev, neighbours, inner, request, first, elements)
    table = exchange(slices, both)
    all_stepped, all_low, all_high = full_stepped(atmos_state)
    all_before, all_after = around(all_low, all_high)
    new_state = full_new_state(
        atmos_state.shape, all_stepped, all_before, all_after, neighbours, first, elements
    )

    answer, wanted = picked(table)
    answer, block_weights = lax.optimization_barrier((answer, block_weights))
    weights = packed_weights(grp, block_weights)
    got = exchange(answer, "blk")
    sent = remapped_cells(flux_weight, got, wanted, weights)
    ocean_flux = placed(exchange(sent, both), ocean_cells, rank)
    return new_state, ocean_flux


def solution(mesh):
    in_specs = (
        P(None, None, None, both),
        P(None, both),
        P(),
        P("blk", None, None, None),
        P("blk", None),
        P("blk"),
        P("blk"),
    )
    out_specs = (P(None, None, None, both), P("grp", "blk"))
    return jax.shard_map(body, mesh=mesh, in_specs=in_specs, out_specs=out_specs, check_vma=False)
```

```python
import functools

import jax
import jax.numpy as jnp
import ml_dtypes
import numpy as np
from jax import lax
from jax.experimental import pallas as pl
from jax.experimental.pallas import tpu as pltpu
from jax.sharding import PartitionSpec as P

time_step = 0.02
viscosity = 0.05
LANES = 128
REACH = 256
f32 = jnp.float32
bf16 = jnp.bfloat16
i32 = jnp.int32
both = ("grp", "blk")


def params(mebibytes=16):
    return pltpu.CompilerParams(vmem_limit_bytes=mebibytes * 1024 * 1024)


def in_hbm(x):
    return pltpu.with_memory_space_constraint(x, pltpu.HBM)


def cost(flops, moved):
    return pl.CostEstimate(flops=flops, bytes_accessed=moved, transcendentals=0)


def whole(shape):
    return pl.BlockSpec(shape, lambda *_: (0,) * len(shape))


def derivative_matrix():
    nodes = np.array([-1.0, -1.0 / np.sqrt(5.0), 1.0 / np.sqrt(5.0), 1.0])
    others = [[k for k in range(4) if k != n] for n in range(4)]
    weights = [np.prod([nodes[n] - nodes[k] for k in others[n]]) for n in range(4)]
    matrix = np.zeros((4, 4))
    for a in range(4):
        for c in range(4):
            if a != c:
                matrix[a, c] = weights[a] / weights[c] / (nodes[a] - nodes[c])
            else:
                matrix[a, a] = sum(1.0 / (nodes[a] - nodes[k]) for k in others[a])
    return matrix


def operators(copies):
    d = derivative_matrix().astype(np.float32).astype(np.float64)
    east, north = np.kron(np.eye(4), d), np.kron(d, np.eye(4))
    bend = east @ east + north @ north
    parts = [-time_step * east, -time_step * north, time_step * viscosity * bend]
    stacked = np.concatenate([np.kron(np.eye(copies), part) for part in parts])
    high = stacked.astype(ml_dtypes.bfloat16)
    low = (stacked - high.astype(np.float64)).astype(ml_dtypes.bfloat16)
    return jnp.asarray(high), jnp.asarray(low)


def split_two(x):
    high = x.astype(bf16)
    return high, (x - high.astype(f32)).astype(bf16)


def dot(a, b):
    return jnp.dot(a, b, preferred_element_type=f32)


def dot_nt(a, b):
    return lax.dot_general(a, b, (((1,), (1,)), ((), ())), preferred_element_type=f32)


def apply_operators(high, low, x):
    xh, xl = split_two(x)
    return dot(high, xh) + dot(high, xl) + dot(low, xh)


def iota(shape, dim):
    return lax.broadcasted_iota(i32, shape, dim)


def bottom_step(x_ref, nb_ref, high_ref, low_ref, out_ref, rim_ref):
    x = x_ref[:, 0].reshape(64, -1)
    op = apply_operators(high_ref[...], low_ref[...], x)
    size = x.shape[1]
    for v in range(4):
        rows = slice(16 * v, 16 * v + 16)
        stepped = (
            x[rows] + x[0:16] * op[rows] + x[16:32] * op[64:128][rows] + op[128:192][rows]
        )
        out_ref[rows] = stepped
        rim_ref[rows] = stepped[:, size - 2 * REACH :]
        rim_ref[16 * v + 5 : 16 * v + 6, :REACH] = nb_ref[v : v + 1].astype(f32)


def bottom_stepped(state, neighbours):
    nvar, levels, points, size = state.shape
    high, low = operators(nvar)
    rim = (nvar * points, 2 * REACH)
    return pl.pallas_call(
        bottom_step,
        grid=(1,),
        in_specs=[
            pl.BlockSpec((nvar, 1, points, size), lambda i: (0, levels - 1, 0, 0)),
            pl.BlockSpec((4, REACH), lambda i: (0, size // REACH - 1)),
            whole(high.shape),
            whole(low.shape),
        ],
        out_specs=[pl.BlockSpec(memory_space=pltpu.VMEM), whole(rim)],
        out_shape=[pltpu.VMEM((nvar * points, size), f32), jax.ShapeDtypeStruct(rim, f32)],
        compiler_params=params(),
        name="bottom_step",
    )(in_hbm(state), in_hbm(neighbours), in_hbm(high), in_hbm(low))


def line_operators():
    d = derivative_matrix()
    d2 = d @ d
    slope = [
        (
            0.5 * (d[i, 0] - d[i, 3]),
            0.5 * (d[i, 1] - d[i, 2]),
            0.5 * (d[i, 0] + d[i, 3]),
        )
        for i in range(2)
    ]
    bend = [
        (
            0.5 * (d2[i, 0] - d2[i, 3]),
            0.5 * (d2[i, 1] - d2[i, 2]),
            0.5 * (d2[i, 0] + d2[i, 3]),
        )
        for i in range(2)
    ]
    return slope, bend


def along_line(x, slope, bend):
    t0, t1 = x[0] - x[3], x[1] - x[2]
    mean = (x[0] + x[3]) - (x[1] + x[2])
    first, second = [None] * 4, [None] * 4
    for i in range(2):
        a, b, c = [np.float32(-time_step * k) for k in slope[i]]
        even, odd = a * t0 + b * t1, c * mean
        first[i], first[3 - i] = even + odd, even - odd
        a, b, c = [np.float32(time_step * viscosity * k) for k in bend[i]]
        odd, even = a * t0 + b * t1, c * mean
        second[i], second[3 - i] = even + odd, even - odd
    return first, second


edge_points = (0, 1, 2, 3, 4, 7, 8, 11, 12, 13, 14, 15)


def full_step(left_ref, right_ref, out_ref, first_ref, last_ref):
    step = pl.program_id(0)
    slope, bend = line_operators()

    def points(x_ref, v, half):
        start = (v * 16 + half * 8) * 16
        return [x_ref[pl.ds(start + p, 8, stride=16), :] for p in range(16)]

    for part, x_ref in enumerate((left_ref, right_ref)):
        cols = slice(part * LANES, (part + 1) * LANES)
        for half in range(2):
            u, w = points(x_ref, 0, half), points(x_ref, 1, half)
            for v in range(4):
                x = u if v == 0 else w if v == 1 else points(x_ref, v, half)
                total = list(x)
                for a in range(4):
                    at = [4 * a + b for b in range(4)]
                    first, second = along_line([x[p] for p in at], slope, bend)
                    for p, one, two in zip(at, first, second):
                        total[p] = total[p] + (u[p] * one + two)
                for b in range(4):
                    at = [4 * a + b for a in range(4)]
                    first, second = along_line([x[p] for p in at], slope, bend)
                    for p, one, two in zip(at, first, second):
                        total[p] = total[p] + (w[p] * one + two)
                start = v * 16 + half * 8
                for p in range(16):
                    out_ref[p, start : start + 8, cols] = total[p]

    @pl.when(step == 0)
    def _():
        for k, p in enumerate(edge_points):
            first_ref[k] = out_ref[p].astype(bf16)

    @pl.when(step == pl.num_programs(0) - 1)
    def _():
        for k, p in enumerate(edge_points):
            last_ref[k] = out_ref[p].astype(bf16)


def full_stepped(state):
    nvar, levels, points, size = state.shape
    rows = nvar * levels
    rim = (len(edge_points), rows, REACH)
    flat = in_hbm(state.reshape(rows * points, size))
    return pl.pallas_call(
        full_step,
        grid=(size // REACH,),
        in_specs=[
            pl.BlockSpec((rows * points, LANES), lambda i: (0, 2 * i)),
            pl.BlockSpec((rows * points, LANES), lambda i: (0, 2 * i + 1)),
        ],
        out_specs=[
            pl.BlockSpec((points, rows, REACH), lambda i: (0, 0, i)),
            whole(rim),
            whole(rim),
        ],
        out_shape=[
            pltpu.HBM((points, rows, size), f32),
            jax.ShapeDtypeStruct(rim, bf16),
            jax.ShapeDtypeStruct(rim, bf16),
        ],
        compiler_params=params(24),
        cost_estimate=cost(4 * 10**7, 9 << 20),
        name="full_step",
    )(flat, flat)


def local_columns(neighbours, start, elements):
    place = neighbours - start
    place = jnp.where(place < 0, place + elements, place)
    return jnp.where(place >= elements, place - elements, place)


def side_indices(place, rows):
    part = [jnp.broadcast_to(place[s : s + 1], (rows, LANES)) for s in range(4)]
    point = iota((rows, LANES), 0) % 8
    we = jnp.where(point % 4 == 3, part[0], part[1])
    ns = jnp.where(point < 4, part[3], part[2])
    return we, ns


def look_up(columns, index, eb):
    lane = index & (LANES - 1)
    column = (index >> 7) - eb
    value = jnp.take_along_axis(columns[0], lane, axis=1)
    for c in range(1, 5):
        value = jnp.where(column == c, jnp.take_along_axis(columns[c], lane, axis=1), value)
    return value


def halves(x):
    grouped = x.reshape(x.shape[0] // 16, 2, 8, x.shape[1])
    shape = (x.shape[0] // 2, x.shape[1])
    return grouped[:, 0].reshape(shape), grouped[:, 1].reshape(shape)


def edge_update(columns, we, ns, eb):
    pairs = [halves(column) for column in columns]
    rows = pairs[0][0].shape[0]
    point = iota(pairs[0][0].shape, 0) % 8
    first = point < 4
    across = look_up([jnp.where(first, low, high) for low, high in pairs], ns, eb)
    zero = jnp.zeros(first.shape, f32)
    done = []
    for side in range(2):
        own = pairs[2][side]
        beside = look_up([pair[side] for pair in pairs], we, eb)
        total = jnp.where(point % 4 == 0, pltpu.roll(beside, rows - 3, 0) - own, zero)
        total += jnp.where(point % 4 == 3, pltpu.roll(beside, 3, 0) - own, zero)
        if side == 0:
            total += jnp.where(first, pltpu.roll(across, rows - 4, 0) - own, zero)
        else:
            total += jnp.where(first, zero, pltpu.roll(across, 4, 0) - own)
        done.append((own + 0.5 * total).reshape(-1, 1, 8, own.shape[1]))
    return jnp.concatenate(done, axis=1).reshape(columns[0].shape)


def lane_tiles(ref, count):
    return [ref[:, c * LANES : (c + 1) * LANES] for c in range(count)]


def inner_edges(elements, first_ref, s_ref, nb_ref, out_ref):
    size = s_ref.shape[1]
    place = local_columns(nb_ref[...], first_ref[0], elements)
    tiles = lane_tiles(s_ref, size // LANES)
    for eb in range(size // LANES - 4):
        cols = slice(eb * LANES + REACH, eb * LANES + REACH + LANES)
        we, ns = side_indices(place[:, cols], 32)
        out_ref[:, eb * LANES : (eb + 1) * LANES] = edge_update(tiles[eb : eb + 5], we, ns, eb)


def bottom_inner(stepped, neighbours, first, elements):
    rows, size = stepped.shape
    vmem = pl.BlockSpec(memory_space=pltpu.VMEM)
    return pl.pallas_call(
        functools.partial(inner_edges, elements),
        in_specs=[pl.BlockSpec(memory_space=pltpu.SMEM), vmem, vmem],
        out_specs=vmem,
        out_shape=pltpu.VMEM((rows, size - 2 * REACH), f32),
        compiler_params=params(),
        name="bottom_inner",
    )(first, stepped, neighbours)


def bottom_edges(elements, first_ref, s_ref, prev_ref, nb_ref, inner_ref, request_ref, out_ref):
    out_ref[:, 0, 2 * LANES :] = request_ref[...]
    edge = 2 * REACH // LANES
    carried = [prev_ref[16 * v + 5 : 16 * v + 6, :REACH] for v in range(4)]
    neighbours = jnp.concatenate(
        [jnp.concatenate(carried, axis=0).astype(i32), nb_ref[:, :REACH]], axis=1
    )
    place = local_columns(neighbours, first_ref[0] - 2 * REACH, elements)
    tiles = lane_tiles(prev_ref, edge) + lane_tiles(s_ref, edge)
    new = []
    for eb in range(edge):
        we, ns = side_indices(place[:, eb * LANES : (eb + 1) * LANES], 32)
        new.append(edge_update(tiles[eb : eb + 5], we, ns, eb))
    new += lane_tiles(inner_ref, inner_ref.shape[1] // LANES)
    for v in range(4):
        blocks = jnp.concatenate([piece[16 * v : 16 * v + 16] for piece in new], axis=0)
        turned = blocks.T
        for g in range(4):
            rows = slice(64 * g + 16 * v, 64 * g + 16 * v + 16)
            for h in range(2):
                at = 32 * g + 16 * h
                out_ref[rows, 0, h * LANES : (h + 1) * LANES] = turned[at : at + 16]


def bottom_slices(stepped, prev, neighbours, inner, request, first, elements):
    vmem = pl.BlockSpec(memory_space=pltpu.VMEM)
    return pl.pallas_call(
        functools.partial(bottom_edges, elements),
        in_specs=[pl.BlockSpec(memory_space=pltpu.SMEM)] + [vmem] * 5,
        out_shape=jax.ShapeDtypeStruct((256, 1, 3 * LANES), f32),
        compiler_params=params(),
        name="bottom_edges",
    )(first, stepped, prev, neighbours, inner, request)


sides = (
    ((3, 7, 11, 15), (0, 4, 8, 12)),
    ((0, 4, 8, 12), (3, 7, 11, 15)),
    ((12, 13, 14, 15), (0, 1, 2, 3)),
    ((0, 1, 2, 3), (12, 13, 14, 15)),
)


def full_edges(
    elements,
    first_ref,
    ahead_ref,
    before_ref,
    after_ref,
    nb_ref,
    out_ref,
    own_ref,
    split_ref,
    turn_ref,
):
    step = pl.program_id(0)
    tiles = pl.num_programs(0) - 1
    rows = own_ref.shape[1]
    empty = jnp.zeros((rows, REACH), bf16)

    @pl.when(step == 0)
    def _():
        for k, p in enumerate(edge_points):
            split_ref[0, p, :, :REACH] = before_ref[k]
            split_ref[1, p, :, :REACH] = empty

    place_at = pl.multiple_of((step + 1) * REACH, REACH)

    @pl.when(step < tiles)
    def _():
        for p in edge_points:
            high, low = split_two(ahead_ref[p])
            split_ref[0, p, :, pl.ds(place_at, REACH)] = high
            split_ref[1, p, :, pl.ds(place_at, REACH)] = low

    @pl.when(step == tiles)
    def _():
        for k, p in enumerate(edge_points):
            split_ref[0, p, :, pl.ds(place_at, REACH)] = after_ref[k]
            split_ref[1, p, :, pl.ds(place_at, REACH)] = empty

    @pl.when(step > 0)
    def _():
        place = local_columns(nb_ref[...], first_ref[0] - REACH, elements) - (step - 1) * REACH
        start = pl.multiple_of((step - 1) * REACH, REACH)
        change = [None] * 16
        for side, (source, target) in enumerate(sides):
            onehot = jnp.where(
                iota((3 * REACH, REACH), 0) == place[side : side + 1, :], 1.0, 0.0
            ).astype(bf16)
            pieces = [
                split_ref[part, p, :, pl.ds(start, 3 * REACH)]
                for part in range(2)
                for p in source
            ]
            value = dot(jnp.concatenate(pieces, axis=0), onehot)
            for k, p in enumerate(target):
                there = value[k * rows : (k + 1) * rows] + value[(4 + k) * rows : (5 + k) * rows]
                part = there - own_ref[p]
                change[p] = part if change[p] is None else change[p] + part
        for p in range(16):
            new = own_ref[p] if change[p] is None else own_ref[p] + 0.5 * change[p]
            for h in range(2):
                turn_ref[h, pl.ds(p, rows, stride=16), :] = new[:, h * LANES : (h + 1) * LANES]
        for h in range(2):
            out_ref[:, h * LANES : (h + 1) * LANES] = turn_ref[h]

    @pl.when(step < tiles)
    def _():
        own_ref[...] = ahead_ref[...]


def full_new_state(shape, stepped, before, after, neighbours, first, elements):
    points, rows, size = stepped.shape
    tiles = size // REACH
    tile = (points, rows, REACH)
    out = pl.pallas_call(
        functools.partial(full_edges, elements),
        grid=(tiles + 1,),
        in_specs=[
            pl.BlockSpec(memory_space=pltpu.SMEM),
            pl.BlockSpec(tile, lambda i: (0, 0, jnp.minimum(i, tiles - 1))),
            whole(before.shape),
            whole(after.shape),
            pl.BlockSpec((4, REACH), lambda i: (0, jnp.maximum(i - 1, 0))),
        ],
        out_specs=pl.BlockSpec((rows * points, REACH), lambda i: (0, jnp.maximum(i - 1, 0))),
        out_shape=jax.ShapeDtypeStruct((rows * points, size), f32),
        scratch_shapes=[
            pltpu.VMEM(tile, f32),
            pltpu.VMEM((2, 16, rows, size + 2 * REACH), bf16),
            pltpu.VMEM((2, rows * points, LANES), f32),
        ],
        compiler_params=params(24),
        cost_estimate=cost(4 * 10**9, 10 << 20),
        name="full_edges",
    )(first, in_hbm(stepped), before, after, neighbours)
    return out.reshape(shape)


def request_table(grp_ref, cells_ref, ids_ref, out_ref, rank_ref):
    chunks = cells_ref.shape[0]
    owner_at = iota((64, LANES), 0)
    cells = [cells_ref[c : c + 1, :] for c in range(chunks)]
    mine = [jnp.where(owner_at == (cell >> 11), 1.0, 0.0) for cell in cells]
    before = jnp.where(iota((LANES, 2 * LANES), 0) < iota((LANES, 2 * LANES), 1), 1.0, 0.0)
    counts = dot(jnp.concatenate(mine, axis=0).astype(bf16), before.astype(bf16))
    carried = jnp.zeros((64, LANES), f32)
    slots, high, low = [], [], []
    for c, cell in enumerate(cells):
        count = counts[64 * c : 64 * c + 64]
        rank = jnp.sum(mine[c] * (count[:, :LANES] + carried), axis=0, keepdims=True).astype(i32)
        carried = carried + count[:, LANES:]
        rank_ref[c : c + 1, :] = rank
        slots.append(jnp.where(owner_at == rank, 1.0, 0.0).astype(bf16))
        row = cell & 2047
        high.append((mine[c] * (row >> 7).astype(f32)).astype(bf16))
        low.append((mine[c] * (row & 127).astype(f32)).astype(bf16))
    parts = jnp.concatenate([jnp.concatenate(p, axis=1) for p in (high, low)], axis=0)
    wanted = dot_nt(parts, jnp.concatenate(slots, axis=1))
    wanted = wanted[:64] * 128.0 + wanted[64:]
    wanted = jnp.concatenate([wanted, wanted], axis=1)
    share = pltpu.roll(wanted, 64 - 12 * grp_ref[0], 1)
    message = jnp.where(iota((64, LANES), 1) < 64, ids_ref[...].astype(f32), share)
    for y in range(4):
        out_ref[64 * y : 64 * y + 64, :] = message


def requests(grp, ocean_cells, ids):
    chunks = ocean_cells.shape[0] // LANES
    vmem = pl.BlockSpec(memory_space=pltpu.VMEM)
    return pl.pallas_call(
        request_table,
        in_specs=[pl.BlockSpec(memory_space=pltpu.SMEM), vmem, vmem],
        out_shape=[
            jax.ShapeDtypeStruct((256, LANES), f32),
            jax.ShapeDtypeStruct((chunks, LANES), i32),
        ],
        compiler_params=params(),
        name="request_table",
    )(grp, ocean_cells.reshape(chunks, LANES), ids)


QUERIES = 256


def pick_values(table_ref, out_ref, cells_ref, turned_ref, ids_ref, found_ref):
    lane = iota((LANES, LANES), 1)
    asked = table_ref[:, 0, 2 * LANES :]
    ids = jnp.where(lane < 64, asked[:LANES], pltpu.roll(asked[LANES:], 64, 1))
    ids_ref[...] = ids.astype(i32)
    lane = iota((64, LANES), 1)
    wanted = jnp.zeros((64, LANES), f32)
    for y in range(4):
        part = pltpu.roll(asked[64 * y : 64 * y + 64], 64 + 12 * y, 1)
        wanted = jnp.where((lane >= 12 * y) & (lane < 12 * y + 12), part, wanted)
    lane = iota((32, LANES), 1)
    cells_ref[...] = jnp.where(lane < 64, wanted[:32], pltpu.roll(wanted[32:], 64, 1)).astype(i32)

    high, low = split_two(table_ref[:, 0, : 2 * LANES].T)
    for half in range(2):
        turned_ref[half, :LANES] = high[half * LANES : (half + 1) * LANES]
        turned_ref[half, LANES:] = low[half * LANES : (half + 1) * LANES]
    groups = QUERIES // LANES
    device_at = iota((256, QUERIES), 0)
    block_at = iota((LANES, QUERIES), 0)

    def some(step, carry):
        rows = [ids_ref[pl.ds(groups * step + k, 1), :] for k in range(groups)]
        asked = jnp.concatenate(rows, axis=1)
        onehot = jnp.where(device_at == (asked >> 7), 1.0, 0.0).astype(bf16)
        hit = block_at == (asked & 127)
        for half in range(2):
            value = dot(turned_ref[half], onehot)
            part = value[:LANES] + value[LANES:]
            found = jnp.sum(jnp.where(hit, part, 0.0), axis=0, keepdims=True)
            for k in range(groups):
                found_ref[half, pl.ds(groups * step + k, 1), :] = found[
                    :, k * LANES : (k + 1) * LANES
                ]
        return carry

    lax.fori_loop(0, LANES // groups, some, 0, unroll=32)
    for half in range(2):
        for y in range(2):
            at = (2 * half + y) * LANES
            out_ref[:, 0, at : at + LANES] = found_ref[half, 64 * y : 64 * y + 64, :]


def picked(table):
    return pl.pallas_call(
        pick_values,
        out_shape=[
            pltpu.HBM((64, 1, 4 * LANES), f32),
            jax.ShapeDtypeStruct((32, LANES), i32),
        ],
        scratch_shapes=[
            pltpu.VMEM((2, 256, 256), bf16),
            pltpu.VMEM((LANES, LANES), i32),
            pltpu.VMEM((2, LANES, LANES), f32),
        ],
        compiler_params=params(24),
        name="pick_values",
    )(table)


def quarter_weights(grp_ref, w_ref, out_ref):
    column, lane = iota((4 * LANES, LANES), 0), iota((4 * LANES, LANES), 1)
    wanted = (column // LANES == lane // 32) & (
        column % LANES == 32 * grp_ref[0] + lane % 32
    )
    chosen = jnp.where(wanted, 1.0, 0.0).astype(bf16)
    at = [(r, b) for r in range(w_ref.shape[0]) for b in range(4)]
    rows = [
        jnp.concatenate([w_ref[r, 4 * b + q] for q in range(4)], axis=1) for r, b in at
    ]
    packed = dot(jnp.concatenate(rows, axis=0), chosen).astype(bf16)
    for k, (r, b) in enumerate(at):
        out_ref[r, b] = packed[LANES * k : LANES * (k + 1)]


def packed_weights(grp, block_weights):
    count, slots, block = block_weights.shape[:3]
    step = 8
    return pl.pallas_call(
        quarter_weights,
        grid=(count // step,),
        in_specs=[
            pl.BlockSpec(memory_space=pltpu.SMEM),
            pl.BlockSpec((step, slots, block, block), lambda i: (i, 0, 0, 0)),
        ],
        out_specs=pl.BlockSpec((step, slots // 4, block, block), lambda i: (i, 0, 0, 0)),
        out_shape=jax.ShapeDtypeStruct((count, slots // 4, block, block), bf16),
        compiler_params=params(),
        cost_estimate=cost(10**9, 10 << 20),
        name="quarter_weights",
    )(grp, in_hbm(block_weights))


def remap_rows(
    fw_ref, got_ref, index_ref, w_ref, out_ref, field_ref, mapped_ref, sent_ref, pair_ref
):
    values = []
    for v in range(4):
        rows = slice(16 * v, 16 * v + 16)
        tiles = [
            got_ref[rows, 0, (2 * h + y) * LANES : (2 * h + y + 1) * LANES]
            for y in range(2)
            for h in range(2)
        ]
        turned = jnp.concatenate(tiles, axis=0).T
        values.append(jnp.concatenate([turned[:64], turned[64:]], axis=1))
    wind = jnp.sqrt(1.0 + values[0] * values[0] + values[1] * values[1])
    for f in range(16):
        if f < 12:
            total = fw_ref[f, 0] * values[0]
            for v in range(1, 4):
                total += fw_ref[f, v] * values[v]
            total = (total * wind).astype(bf16).astype(f32)
        else:
            total = jnp.zeros((64, LANES), f32)
        field_ref[pl.ds(f, 64, stride=16), :] = total

    for r in range(16):
        total = jnp.zeros((16, LANES), f32)
        for b in range(0, 4, 2):
            at = (r * 4 + b) * 16
            pair = field_ref[at : at + 32, :].astype(bf16)
            pair = jnp.concatenate([pair[:16], pair[16:]], axis=1)
            weights = jnp.concatenate([w_ref[r, b], w_ref[r, b + 1]], axis=1)
            total += dot_nt(pair, weights)
        mapped_ref[16 * r : 16 * r + 16, :] = total

    parts = mapped_ref[...].astype(bf16)
    row_at = iota((LANES, 4 * LANES), 0)

    def some(at, carry):
        rows = [index_ref[pl.ds(4 * at + k, 1), :] for k in range(4)]
        asked = jnp.concatenate(rows, axis=1)
        onehot = jnp.where(row_at == (asked & 127), 1.0, 0.0).astype(bf16)
        value = dot(parts, onehot)
        block = asked >> 7
        found = value[:16]
        for r in range(1, 16):
            found = jnp.where(block == r, value[16 * r : 16 * r + 16], found)
        for k in range(4):
            sent_ref[pl.ds(4 * at + k, 16, stride=32), :] = found[
                :, k * LANES : (k + 1) * LANES
            ]
        return carry

    lax.fori_loop(0, 8, some, 0, unroll=True)
    lane = iota((32, LANES), 1)
    for y in range(4):
        a, b, c = [sent_ref[(3 * y + f) * 32 : (3 * y + f) * 32 + 32, :] for f in range(3)]
        base = 64 * y
        low, high = slice(base, base + 32), slice(base + 32, base + 64)
        pair_ref[low, 0, :] = jnp.where(lane < 64, a, pltpu.roll(b, 64, 1))
        pair_ref[low, 1, :] = c
        pair_ref[high, 0, :] = jnp.where(lane < 64, pltpu.roll(a, 64, 1), b)
        pair_ref[high, 1, :] = pltpu.roll(c, 64, 1)
    out_ref[...] = pair_ref[...].astype(bf16)


def remapped_cells(flux_weight, got, index, block_weights):
    smem = pl.BlockSpec(memory_space=pltpu.SMEM)
    vmem = pl.BlockSpec(memory_space=pltpu.VMEM)
    return pl.pallas_call(
        remap_rows,
        in_specs=[smem, vmem, vmem, vmem],
        out_shape=jax.ShapeDtypeStruct((256, 2, LANES), bf16),
        scratch_shapes=[
            pltpu.VMEM((64 * 16, LANES), f32),
            pltpu.VMEM((256, LANES), f32),
            pltpu.VMEM((16 * 32, LANES), f32),
            pltpu.VMEM((256, 2, LANES), f32),
        ],
        compiler_params=params(),
        name="remap_rows",
    )(flux_weight, got, index, block_weights)


def place_cells(got_ref, cells_ref, rank_ref, out_ref):
    got = got_ref[...].astype(f32)
    got = got[0:64] + got[64:128] + got[128:192] + got[192:256]
    pair, last = got[:, 0, :].T, got[:, 1, :].T
    parts = jnp.concatenate(split_two(jnp.concatenate([pair, last[:64]], axis=0)), axis=1)
    owner_at = iota((64, 4 * LANES), 0)
    for c in range(4):
        rows = range(4 * c, 4 * c + 4)
        cell = jnp.concatenate([cells_ref[r : r + 1, :] for r in rows], axis=1)
        rank = jnp.concatenate([rank_ref[r : r + 1, :] for r in rows], axis=1)
        onehot = jnp.where(owner_at == (cell >> 11), 1.0, 0.0).astype(bf16)
        value = dot(parts, jnp.concatenate([onehot, onehot], axis=0))
        hit = owner_at == rank
        for f in range(3):
            out_ref[f : f + 1, c * 4 * LANES : (c + 1) * 4 * LANES] = jnp.sum(
                jnp.where(hit, value[64 * f : 64 * f + 64], 0.0), axis=0, keepdims=True
            )


def placed(got, ocean_cells, rank):
    count = ocean_cells.shape[0]
    return pl.pallas_call(
        place_cells,
        out_shape=jax.ShapeDtypeStruct((3, count), f32),
        compiler_params=params(),
        name="place_cells",
    )(got, ocean_cells.reshape(count // LANES, LANES), rank)


def upward():
    count = lax.axis_size(both)
    return [(i, (i + 1) % count) for i in range(count)]


def around(first, last):
    up = upward()
    down = [(j, i) for i, j in up]
    return lax.ppermute(last, both, up), lax.ppermute(first, both, down)


def exchange(x, axis):
    return lax.all_to_all(x, axis, split_axis=0, concat_axis=0, tiled=True)


def body(atmos_state, neighbours, flux_weight, block_weights, block_ids, block_counts, ocean_cells):
    size = atmos_state.shape[3]
    elements = size * lax.axis_size(both)
    grp = lax.axis_index("grp").astype(i32).reshape(1)
    first = (lax.axis_index(both) * size).astype(i32).reshape(1)

    stepped, rim = bottom_stepped(atmos_state, neighbours)
    prev = lax.ppermute(rim, both, upward())

    shift = REACH // LANES * 16
    blocks = elements // LANES * 16
    live = jnp.arange(block_ids.shape[1])[None, :] < block_counts[:, None]
    ids = jnp.where(live, (block_ids + shift) % blocks, -1)
    ids = ids.reshape(-1, 4, 4).transpose(2, 0, 1).reshape(4, 64)
    ids = lax.dynamic_slice_in_dim(ids, lax.axis_index("grp"), 1, 0)
    ids = jnp.concatenate([ids, ids], axis=1)
    request, rank = requests(grp, ocean_cells, ids)

    inner = bottom_inner(stepped, neighbours, first, elements)
    slices = bottom_slices(stepped, prev, neighbours, inner, request, first, elements)
    table = exchange(slices, both)
    all_stepped, all_low, all_high = full_stepped(atmos_state)
    all_before, all_after = around(all_low, all_high)
    new_state = full_new_state(
        atmos_state.shape, all_stepped, all_before, all_after, neighbours, first, elements
    )

    answer, wanted = picked(table)
    answer, block_weights = lax.optimization_barrier((answer, block_weights))
    weights = packed_weights(grp, block_weights)
    got = exchange(answer, "blk")
    sent = remapped_cells(flux_weight, got, wanted, weights)
    ocean_flux = placed(exchange(sent, both), ocean_cells, rank)
    return new_state, ocean_flux


def solution(mesh):
    in_specs = (
        P(None, None, None, both),
        P(None, both),
        P(),
        P("blk", None, None, None),
        P("blk", None),
        P("blk"),
        P("blk"),
    )
    out_specs = (P(None, None, None, both), P("grp", "blk"))
    return jax.shard_map(body, mesh=mesh, in_specs=in_specs, out_specs=out_specs, check_vma=False)
```

```python
import functools

import jax
import jax.numpy as jnp
import ml_dtypes
import numpy as np
from jax import lax
from jax.experimental import pallas as pl
from jax.experimental.pallas import tpu as pltpu
from jax.sharding import PartitionSpec as P

time_step = 0.02
viscosity = 0.05
LANES = 128
REACH = 256
f32 = jnp.float32
bf16 = jnp.bfloat16
i32 = jnp.int32
both = ("grp", "blk")


def params(mebibytes=16):
    return pltpu.CompilerParams(vmem_limit_bytes=mebibytes * 1024 * 1024)


def in_hbm(x):
    return pltpu.with_memory_space_constraint(x, pltpu.HBM)


def cost(flops, moved):
    return pl.CostEstimate(flops=flops, bytes_accessed=moved, transcendentals=0)


def whole(shape):
    return pl.BlockSpec(shape, lambda *_: (0,) * len(shape))


def derivative_matrix():
    nodes = np.array([-1.0, -1.0 / np.sqrt(5.0), 1.0 / np.sqrt(5.0), 1.0])
    others = [[k for k in range(4) if k != n] for n in range(4)]
    weights = [np.prod([nodes[n] - nodes[k] for k in others[n]]) for n in range(4)]
    matrix = np.zeros((4, 4))
    for a in range(4):
        for c in range(4):
            if a != c:
                matrix[a, c] = weights[a] / weights[c] / (nodes[a] - nodes[c])
            else:
                matrix[a, a] = sum(1.0 / (nodes[a] - nodes[k]) for k in others[a])
    return matrix


def operators(copies):
    d = derivative_matrix().astype(np.float32).astype(np.float64)
    east, north = np.kron(np.eye(4), d), np.kron(d, np.eye(4))
    bend = east @ east + north @ north
    parts = [-time_step * east, -time_step * north, time_step * viscosity * bend]
    stacked = np.concatenate([np.kron(np.eye(copies), part) for part in parts])
    high = stacked.astype(ml_dtypes.bfloat16)
    low = (stacked - high.astype(np.float64)).astype(ml_dtypes.bfloat16)
    return jnp.asarray(np.concatenate([high, high, low], axis=1))


def split_two(x):
    high = x.astype(bf16)
    return high, (x - high.astype(f32)).astype(bf16)


def dot(a, b):
    return jnp.dot(a, b, preferred_element_type=f32)


def dot_nt(a, b):
    return lax.dot_general(a, b, (((1,), (1,)), ((), ())), preferred_element_type=f32)


def apply_operators(matrix, x):
    high, low = split_two(x)
    return dot(matrix, jnp.concatenate([high, low, high], axis=0))


def iota(shape, dim):
    return lax.broadcasted_iota(i32, shape, dim)


def bottom_step(x_ref, nb_ref, matrix_ref, out_ref, rim_ref):
    x = x_ref[:, 0].reshape(64, -1)
    op = apply_operators(matrix_ref[...], x)
    size = x.shape[1]
    for v in range(4):
        rows = slice(16 * v, 16 * v + 16)
        stepped = (
            x[rows] + x[0:16] * op[rows] + x[16:32] * op[64:128][rows] + op[128:192][rows]
        )
        out_ref[rows] = stepped
        rim_ref[rows] = stepped[:, size - 2 * REACH :]
        rim_ref[16 * v + 5 : 16 * v + 6, :REACH] = nb_ref[v : v + 1].astype(f32)


def bottom_stepped(state, neighbours):
    nvar, levels, points, size = state.shape
    matrix = operators(nvar)
    rim = (nvar * points, 2 * REACH)
    return pl.pallas_call(
        bottom_step,
        grid=(1,),
        in_specs=[
            pl.BlockSpec((nvar, 1, points, size), lambda i: (0, levels - 1, 0, 0)),
            pl.BlockSpec((4, REACH), lambda i: (0, size // REACH - 1)),
            whole(matrix.shape),
        ],
        out_specs=[pl.BlockSpec(memory_space=pltpu.VMEM), whole(rim)],
        out_shape=[pltpu.VMEM((nvar * points, size), f32), jax.ShapeDtypeStruct(rim, f32)],
        compiler_params=params(),
        name="bottom_step",
    )(in_hbm(state), in_hbm(neighbours), in_hbm(matrix))


def line_operators():
    d = derivative_matrix()
    d2 = d @ d
    slope = [
        (
            0.5 * (d[i, 0] - d[i, 3]),
            0.5 * (d[i, 1] - d[i, 2]),
            0.5 * (d[i, 0] + d[i, 3]),
        )
        for i in range(2)
    ]
    bend = [
        (
            0.5 * (d2[i, 0] - d2[i, 3]),
            0.5 * (d2[i, 1] - d2[i, 2]),
            0.5 * (d2[i, 0] + d2[i, 3]),
        )
        for i in range(2)
    ]
    return slope, bend


def along_line(x, slope, bend):
    t0, t1 = x[0] - x[3], x[1] - x[2]
    mean = (x[0] + x[3]) - (x[1] + x[2])
    first, second = [None] * 4, [None] * 4
    for i in range(2):
        a, b, c = [np.float32(-time_step * k) for k in slope[i]]
        even, odd = a * t0 + b * t1, c * mean
        first[i], first[3 - i] = even + odd, even - odd
        a, b, c = [np.float32(time_step * viscosity * k) for k in bend[i]]
        odd, even = a * t0 + b * t1, c * mean
        second[i], second[3 - i] = even + odd, even - odd
    return first, second


edge_points = (0, 1, 2, 3, 4, 7, 8, 11, 12, 13, 14, 15)


def full_step(left_ref, right_ref, out_ref, first_ref, last_ref):
    step = pl.program_id(0)
    slope, bend = line_operators()

    def points(x_ref, v, half):
        start = (v * 16 + half * 8) * 16
        return [x_ref[pl.ds(start + p, 8, stride=16), :] for p in range(16)]

    for part, x_ref in enumerate((left_ref, right_ref)):
        cols = slice(part * LANES, (part + 1) * LANES)
        for half in range(2):
            u, w = points(x_ref, 0, half), points(x_ref, 1, half)
            for v in range(4):
                x = u if v == 0 else w if v == 1 else points(x_ref, v, half)
                total = list(x)
                for a in range(4):
                    at = [4 * a + b for b in range(4)]
                    first, second = along_line([x[p] for p in at], slope, bend)
                    for p, one, two in zip(at, first, second):
                        total[p] = total[p] + (u[p] * one + two)
                for b in range(4):
                    at = [4 * a + b for a in range(4)]
                    first, second = along_line([x[p] for p in at], slope, bend)
                    for p, one, two in zip(at, first, second):
                        total[p] = total[p] + (w[p] * one + two)
                start = v * 16 + half * 8
                for p in range(16):
                    out_ref[p, start : start + 8, cols] = total[p]

    @pl.when(step == 0)
    def _():
        for k, p in enumerate(edge_points):
            first_ref[k] = out_ref[p].astype(bf16)

    @pl.when(step == pl.num_programs(0) - 1)
    def _():
        for k, p in enumerate(edge_points):
            last_ref[k] = out_ref[p].astype(bf16)


def full_stepped(state):
    nvar, levels, points, size = state.shape
    rows = nvar * levels
    rim = (len(edge_points), rows, REACH)
    flat = in_hbm(state.reshape(rows * points, size))
    return pl.pallas_call(
        full_step,
        grid=(size // REACH,),
        in_specs=[
            pl.BlockSpec((rows * points, LANES), lambda i: (0, 2 * i)),
            pl.BlockSpec((rows * points, LANES), lambda i: (0, 2 * i + 1)),
        ],
        out_specs=[
            pl.BlockSpec((points, rows, REACH), lambda i: (0, 0, i)),
            whole(rim),
            whole(rim),
        ],
        out_shape=[
            pltpu.HBM((points, rows, size), f32),
            jax.ShapeDtypeStruct(rim, bf16),
            jax.ShapeDtypeStruct(rim, bf16),
        ],
        compiler_params=params(24),
        cost_estimate=cost(4 * 10**7, 9 << 20),
        name="full_step",
    )(flat, flat)


def local_columns(neighbours, start, elements):
    place = neighbours - start
    place = jnp.where(place < 0, place + elements, place)
    return jnp.where(place >= elements, place - elements, place)


def side_indices(place, rows):
    part = [jnp.broadcast_to(place[s : s + 1], (rows, LANES)) for s in range(4)]
    point = iota((rows, LANES), 0) % 8
    we = jnp.where(point % 4 == 3, part[0], part[1])
    ns = jnp.where(point < 4, part[3], part[2])
    return we, ns


def look_up(columns, index, eb):
    lane = index & (LANES - 1)
    column = (index >> 7) - eb
    value = jnp.take_along_axis(columns[0], lane, axis=1)
    for c in range(1, 5):
        value = jnp.where(column == c, jnp.take_along_axis(columns[c], lane, axis=1), value)
    return value


def halves(x):
    grouped = x.reshape(x.shape[0] // 16, 2, 8, x.shape[1])
    shape = (x.shape[0] // 2, x.shape[1])
    return grouped[:, 0].reshape(shape), grouped[:, 1].reshape(shape)


def edge_update(columns, we, ns, eb):
    pairs = [halves(column) for column in columns]
    rows = pairs[0][0].shape[0]
    point = iota(pairs[0][0].shape, 0) % 8
    first = point < 4
    across = look_up([jnp.where(first, low, high) for low, high in pairs], ns, eb)
    zero = jnp.zeros(first.shape, f32)
    done = []
    for side in range(2):
        own = pairs[2][side]
        beside = look_up([pair[side] for pair in pairs], we, eb)
        total = jnp.where(point % 4 == 0, pltpu.roll(beside, rows - 3, 0) - own, zero)
        total += jnp.where(point % 4 == 3, pltpu.roll(beside, 3, 0) - own, zero)
        if side == 0:
            total += jnp.where(first, pltpu.roll(across, rows - 4, 0) - own, zero)
        else:
            total += jnp.where(first, zero, pltpu.roll(across, 4, 0) - own)
        done.append((own + 0.5 * total).reshape(-1, 1, 8, own.shape[1]))
    return jnp.concatenate(done, axis=1).reshape(columns[0].shape)


def lane_tiles(ref, count):
    return [ref[:, c * LANES : (c + 1) * LANES] for c in range(count)]


def inner_edges(elements, first_ref, s_ref, nb_ref, out_ref):
    size = s_ref.shape[1]
    place = local_columns(nb_ref[...], first_ref[0], elements)
    tiles = lane_tiles(s_ref, size // LANES)
    for eb in range(size // LANES - 4):
        cols = slice(eb * LANES + REACH, eb * LANES + REACH + LANES)
        we, ns = side_indices(place[:, cols], 32)
        out_ref[:, eb * LANES : (eb + 1) * LANES] = edge_update(tiles[eb : eb + 5], we, ns, eb)


def bottom_inner(stepped, neighbours, first, elements):
    rows, size = stepped.shape
    vmem = pl.BlockSpec(memory_space=pltpu.VMEM)
    return pl.pallas_call(
        functools.partial(inner_edges, elements),
        in_specs=[pl.BlockSpec(memory_space=pltpu.SMEM), vmem, vmem],
        out_specs=vmem,
        out_shape=pltpu.VMEM((rows, size - 2 * REACH), f32),
        compiler_params=params(),
        name="bottom_inner",
    )(first, stepped, neighbours)


def bottom_edges(elements, first_ref, s_ref, prev_ref, nb_ref, inner_ref, request_ref, out_ref):
    out_ref[:, 0, 2 * LANES :] = request_ref[...]
    edge = 2 * REACH // LANES
    carried = [prev_ref[16 * v + 5 : 16 * v + 6, :REACH] for v in range(4)]
    neighbours = jnp.concatenate(
        [jnp.concatenate(carried, axis=0).astype(i32), nb_ref[:, :REACH]], axis=1
    )
    place = local_columns(neighbours, first_ref[0] - 2 * REACH, elements)
    tiles = lane_tiles(prev_ref, edge) + lane_tiles(s_ref, edge)
    new = []
    for eb in range(edge):
        we, ns = side_indices(place[:, eb * LANES : (eb + 1) * LANES], 32)
        new.append(edge_update(tiles[eb : eb + 5], we, ns, eb))
    new += lane_tiles(inner_ref, inner_ref.shape[1] // LANES)
    for v in range(4):
        blocks = jnp.concatenate([piece[16 * v : 16 * v + 16] for piece in new], axis=0)
        turned = blocks.T
        for g in range(4):
            rows = slice(64 * g + 16 * v, 64 * g + 16 * v + 16)
            for h in range(2):
                at = 32 * g + 16 * h
                out_ref[rows, 0, h * LANES : (h + 1) * LANES] = turned[at : at + 16]


def bottom_slices(stepped, prev, neighbours, inner, request, first, elements):
    vmem = pl.BlockSpec(memory_space=pltpu.VMEM)
    return pl.pallas_call(
        functools.partial(bottom_edges, elements),
        in_specs=[pl.BlockSpec(memory_space=pltpu.SMEM)] + [vmem] * 5,
        out_shape=jax.ShapeDtypeStruct((256, 1, 3 * LANES), f32),
        compiler_params=params(),
        name="bottom_edges",
    )(first, stepped, prev, neighbours, inner, request)


sides = (
    ((3, 7, 11, 15), (0, 4, 8, 12)),
    ((0, 4, 8, 12), (3, 7, 11, 15)),
    ((12, 13, 14, 15), (0, 1, 2, 3)),
    ((0, 1, 2, 3), (12, 13, 14, 15)),
)


def full_edges(
    elements,
    first_ref,
    ahead_ref,
    before_ref,
    after_ref,
    nb_ref,
    out_ref,
    own_ref,
    split_ref,
    turn_ref,
):
    step = pl.program_id(0)
    tiles = pl.num_programs(0) - 1
    rows = own_ref.shape[1]
    empty = jnp.zeros((rows, REACH), bf16)

    @pl.when(step == 0)
    def _():
        for k, p in enumerate(edge_points):
            split_ref[0, p, :, :REACH] = before_ref[k]
            split_ref[1, p, :, :REACH] = empty

    place_at = pl.multiple_of((step + 1) * REACH, REACH)

    @pl.when(step < tiles)
    def _():
        for p in edge_points:
            high, low = split_two(ahead_ref[p])
            split_ref[0, p, :, pl.ds(place_at, REACH)] = high
            split_ref[1, p, :, pl.ds(place_at, REACH)] = low

    @pl.when(step == tiles)
    def _():
        for k, p in enumerate(edge_points):
            split_ref[0, p, :, pl.ds(place_at, REACH)] = after_ref[k]
            split_ref[1, p, :, pl.ds(place_at, REACH)] = empty

    @pl.when(step > 0)
    def _():
        place = local_columns(nb_ref[...], first_ref[0] - REACH, elements) - (step - 1) * REACH
        start = pl.multiple_of((step - 1) * REACH, REACH)
        change = [None] * 16
        for side, (source, target) in enumerate(sides):
            onehot = jnp.where(
                iota((3 * REACH, REACH), 0) == place[side : side + 1, :], 1.0, 0.0
            ).astype(bf16)
            pieces = [
                split_ref[part, p, :, pl.ds(start, 3 * REACH)]
                for part in range(2)
                for p in source
            ]
            value = dot(jnp.concatenate(pieces, axis=0), onehot)
            for k, p in enumerate(target):
                there = value[k * rows : (k + 1) * rows] + value[(4 + k) * rows : (5 + k) * rows]
                part = there - own_ref[p]
                change[p] = part if change[p] is None else change[p] + part
        for p in range(16):
            new = own_ref[p] if change[p] is None else own_ref[p] + 0.5 * change[p]
            for h in range(2):
                turn_ref[h, pl.ds(p, rows, stride=16), :] = new[:, h * LANES : (h + 1) * LANES]
        for h in range(2):
            out_ref[:, h * LANES : (h + 1) * LANES] = turn_ref[h]

    @pl.when(step < tiles)
    def _():
        own_ref[...] = ahead_ref[...]


def full_new_state(shape, stepped, before, after, neighbours, first, elements):
    points, rows, size = stepped.shape
    tiles = size // REACH
    tile = (points, rows, REACH)
    out = pl.pallas_call(
        functools.partial(full_edges, elements),
        grid=(tiles + 1,),
        in_specs=[
            pl.BlockSpec(memory_space=pltpu.SMEM),
            pl.BlockSpec(tile, lambda i: (0, 0, jnp.minimum(i, tiles - 1))),
            whole(before.shape),
            whole(after.shape),
            pl.BlockSpec((4, REACH), lambda i: (0, jnp.maximum(i - 1, 0))),
        ],
        out_specs=pl.BlockSpec((rows * points, REACH), lambda i: (0, jnp.maximum(i - 1, 0))),
        out_shape=jax.ShapeDtypeStruct((rows * points, size), f32),
        scratch_shapes=[
            pltpu.VMEM(tile, f32),
            pltpu.VMEM((2, 16, rows, size + 2 * REACH), bf16),
            pltpu.VMEM((2, rows * points, LANES), f32),
        ],
        compiler_params=params(24),
        cost_estimate=cost(4 * 10**9, 10 << 20),
        name="full_edges",
    )(first, in_hbm(stepped), before, after, neighbours)
    return out.reshape(shape)


def request_table(grp_ref, cells_ref, ids_ref, out_ref, rank_ref):
    chunks = cells_ref.shape[0]
    owner_at = iota((64, LANES), 0)
    cells = [cells_ref[c : c + 1, :] for c in range(chunks)]
    mine = [jnp.where(owner_at == (cell >> 11), 1.0, 0.0) for cell in cells]
    before = jnp.where(iota((LANES, 2 * LANES), 0) < iota((LANES, 2 * LANES), 1), 1.0, 0.0)
    counts = dot(jnp.concatenate(mine, axis=0).astype(bf16), before.astype(bf16))
    carried = jnp.zeros((64, LANES), f32)
    slots, high, low = [], [], []
    for c, cell in enumerate(cells):
        count = counts[64 * c : 64 * c + 64]
        rank = jnp.sum(mine[c] * (count[:, :LANES] + carried), axis=0, keepdims=True).astype(i32)
        carried = carried + count[:, LANES:]
        rank_ref[c : c + 1, :] = rank
        slots.append(jnp.where(owner_at == rank, 1.0, 0.0).astype(bf16))
        row = cell & 2047
        high.append((mine[c] * (row >> 7).astype(f32)).astype(bf16))
        low.append((mine[c] * (row & 127).astype(f32)).astype(bf16))
    parts = jnp.concatenate([jnp.concatenate(p, axis=1) for p in (high, low)], axis=0)
    wanted = dot_nt(parts, jnp.concatenate(slots, axis=1))
    wanted = wanted[:64] * 128.0 + wanted[64:]
    wanted = jnp.concatenate([wanted, wanted], axis=1)
    share = pltpu.roll(wanted, 64 - 12 * grp_ref[0], 1)
    message = jnp.where(iota((64, LANES), 1) < 64, ids_ref[...].astype(f32), share)
    for y in range(4):
        out_ref[64 * y : 64 * y + 64, :] = message


def requests(grp, ocean_cells, ids):
    chunks = ocean_cells.shape[0] // LANES
    vmem = pl.BlockSpec(memory_space=pltpu.VMEM)
    return pl.pallas_call(
        request_table,
        in_specs=[pl.BlockSpec(memory_space=pltpu.SMEM), vmem, vmem],
        out_shape=[
            jax.ShapeDtypeStruct((256, LANES), f32),
            jax.ShapeDtypeStruct((chunks, LANES), i32),
        ],
        compiler_params=params(),
        name="request_table",
    )(grp, ocean_cells.reshape(chunks, LANES), ids)


QUERIES = 256


def pick_values(table_ref, out_ref, cells_ref, turned_ref, ids_ref, found_ref):
    lane = iota((LANES, LANES), 1)
    asked = table_ref[:, 0, 2 * LANES :]
    ids = jnp.where(lane < 64, asked[:LANES], pltpu.roll(asked[LANES:], 64, 1))
    ids_ref[...] = ids.astype(i32)
    lane = iota((64, LANES), 1)
    wanted = jnp.zeros((64, LANES), f32)
    for y in range(4):
        part = pltpu.roll(asked[64 * y : 64 * y + 64], 64 + 12 * y, 1)
        wanted = jnp.where((lane >= 12 * y) & (lane < 12 * y + 12), part, wanted)
    lane = iota((32, LANES), 1)
    cells_ref[...] = jnp.where(lane < 64, wanted[:32], pltpu.roll(wanted[32:], 64, 1)).astype(i32)

    high, low = split_two(table_ref[:, 0, : 2 * LANES].T)
    for half in range(2):
        turned_ref[half, :LANES] = high[half * LANES : (half + 1) * LANES]
        turned_ref[half, LANES:] = low[half * LANES : (half + 1) * LANES]
    groups = QUERIES // LANES
    device_at = iota((256, QUERIES), 0)
    block_at = iota((LANES, QUERIES), 0)

    def some(step, carry):
        rows = [ids_ref[pl.ds(groups * step + k, 1), :] for k in range(groups)]
        asked = jnp.concatenate(rows, axis=1)
        onehot = jnp.where(device_at == (asked >> 7), 1.0, 0.0).astype(bf16)
        hit = block_at == (asked & 127)
        for half in range(2):
            value = dot(turned_ref[half], onehot)
            part = value[:LANES] + value[LANES:]
            found = jnp.sum(jnp.where(hit, part, 0.0), axis=0, keepdims=True)
            for k in range(groups):
                found_ref[half, pl.ds(groups * step + k, 1), :] = found[
                    :, k * LANES : (k + 1) * LANES
                ]
        return carry

    lax.fori_loop(0, LANES // groups, some, 0, unroll=32)
    for half in range(2):
        for y in range(2):
            at = (2 * half + y) * LANES
            out_ref[:, 0, at : at + LANES] = found_ref[half, 64 * y : 64 * y + 64, :]


def picked(table):
    return pl.pallas_call(
        pick_values,
        out_shape=[
            pltpu.HBM((64, 1, 4 * LANES), f32),
            jax.ShapeDtypeStruct((32, LANES), i32),
        ],
        scratch_shapes=[
            pltpu.VMEM((2, 256, 256), bf16),
            pltpu.VMEM((LANES, LANES), i32),
            pltpu.VMEM((2, LANES, LANES), f32),
        ],
        compiler_params=params(24),
        name="pick_values",
    )(table)


def quarter_weights(grp_ref, w_ref, out_ref):
    column, lane = iota((4 * LANES, LANES), 0), iota((4 * LANES, LANES), 1)
    wanted = (column // LANES == lane // 32) & (
        column % LANES == 32 * grp_ref[0] + lane % 32
    )
    chosen = jnp.where(wanted, 1.0, 0.0).astype(bf16)
    at = [(r, b) for r in range(w_ref.shape[0]) for b in range(4)]
    rows = [
        jnp.concatenate([w_ref[r, 4 * b + q] for q in range(4)], axis=1) for r, b in at
    ]
    packed = dot(jnp.concatenate(rows, axis=0), chosen).astype(bf16)
    for k, (r, b) in enumerate(at):
        out_ref[r, b] = packed[LANES * k : LANES * (k + 1)]


def packed_weights(grp, block_weights):
    count, slots, block = block_weights.shape[:3]
    step = 8
    return pl.pallas_call(
        quarter_weights,
        grid=(count // step,),
        in_specs=[
            pl.BlockSpec(memory_space=pltpu.SMEM),
            pl.BlockSpec((step, slots, block, block), lambda i: (i, 0, 0, 0)),
        ],
        out_specs=pl.BlockSpec((step, slots // 4, block, block), lambda i: (i, 0, 0, 0)),
        out_shape=jax.ShapeDtypeStruct((count, slots // 4, block, block), bf16),
        compiler_params=params(),
        cost_estimate=cost(10**9, 10 << 20),
        name="quarter_weights",
    )(grp, in_hbm(block_weights))


def remap_rows(
    fw_ref, got_ref, index_ref, w_ref, out_ref, field_ref, mapped_ref, sent_ref, pair_ref
):
    values = []
    for v in range(4):
        rows = slice(16 * v, 16 * v + 16)
        tiles = [
            got_ref[rows, 0, (2 * h + y) * LANES : (2 * h + y + 1) * LANES]
            for y in range(2)
            for h in range(2)
        ]
        turned = jnp.concatenate(tiles, axis=0).T
        values.append(jnp.concatenate([turned[:64], turned[64:]], axis=1))
    wind = jnp.sqrt(1.0 + values[0] * values[0] + values[1] * values[1])
    for f in range(16):
        if f < 12:
            total = fw_ref[f, 0] * values[0]
            for v in range(1, 4):
                total += fw_ref[f, v] * values[v]
            total = (total * wind).astype(bf16).astype(f32)
        else:
            total = jnp.zeros((64, LANES), f32)
        field_ref[pl.ds(f, 64, stride=16), :] = total

    for r in range(16):
        total = jnp.zeros((16, LANES), f32)
        for b in range(0, 4, 2):
            at = (r * 4 + b) * 16
            pair = field_ref[at : at + 32, :].astype(bf16)
            pair = jnp.concatenate([pair[:16], pair[16:]], axis=1)
            weights = jnp.concatenate([w_ref[r, b], w_ref[r, b + 1]], axis=1)
            total += dot_nt(pair, weights)
        mapped_ref[16 * r : 16 * r + 16, :] = total

    parts = mapped_ref[...].astype(bf16)
    row_at = iota((LANES, 4 * LANES), 0)

    def some(at, carry):
        rows = [index_ref[pl.ds(4 * at + k, 1), :] for k in range(4)]
        asked = jnp.concatenate(rows, axis=1)
        onehot = jnp.where(row_at == (asked & 127), 1.0, 0.0).astype(bf16)
        value = dot(parts, onehot)
        block = asked >> 7
        found = value[:16]
        for r in range(1, 16):
            found = jnp.where(block == r, value[16 * r : 16 * r + 16], found)
        for k in range(4):
            sent_ref[pl.ds(4 * at + k, 16, stride=32), :] = found[
                :, k * LANES : (k + 1) * LANES
            ]
        return carry

    lax.fori_loop(0, 8, some, 0, unroll=True)
    lane = iota((32, LANES), 1)
    for y in range(4):
        a, b, c = [sent_ref[(3 * y + f) * 32 : (3 * y + f) * 32 + 32, :] for f in range(3)]
        base = 64 * y
        low, high = slice(base, base + 32), slice(base + 32, base + 64)
        pair_ref[low, 0, :] = jnp.where(lane < 64, a, pltpu.roll(b, 64, 1))
        pair_ref[low, 1, :] = c
        pair_ref[high, 0, :] = jnp.where(lane < 64, pltpu.roll(a, 64, 1), b)
        pair_ref[high, 1, :] = pltpu.roll(c, 64, 1)
    out_ref[...] = pair_ref[...].astype(bf16)


def remapped_cells(flux_weight, got, index, block_weights):
    smem = pl.BlockSpec(memory_space=pltpu.SMEM)
    vmem = pl.BlockSpec(memory_space=pltpu.VMEM)
    return pl.pallas_call(
        remap_rows,
        in_specs=[smem, vmem, vmem, vmem],
        out_shape=jax.ShapeDtypeStruct((256, 2, LANES), bf16),
        scratch_shapes=[
            pltpu.VMEM((64 * 16, LANES), f32),
            pltpu.VMEM((256, LANES), f32),
            pltpu.VMEM((17 * 32, LANES), f32),
            pltpu.VMEM((256, 2, LANES), f32),
        ],
        compiler_params=params(),
        name="remap_rows",
    )(flux_weight, got, index, block_weights)


def place_cells(got_ref, cells_ref, rank_ref, out_ref):
    got = got_ref[...].astype(f32)
    got = got[0:64] + got[64:128] + got[128:192] + got[192:256]
    pair, last = got[:, 0, :].T, got[:, 1, :].T
    parts = jnp.concatenate(split_two(jnp.concatenate([pair, last[:64]], axis=0)), axis=1)
    owner_at = iota((64, 4 * LANES), 0)
    for c in range(4):
        rows = range(4 * c, 4 * c + 4)
        cell = jnp.concatenate([cells_ref[r : r + 1, :] for r in rows], axis=1)
        rank = jnp.concatenate([rank_ref[r : r + 1, :] for r in rows], axis=1)
        onehot = jnp.where(owner_at == (cell >> 11), 1.0, 0.0).astype(bf16)
        value = dot(parts, jnp.concatenate([onehot, onehot], axis=0))
        hit = owner_at == rank
        for f in range(3):
            out_ref[f : f + 1, c * 4 * LANES : (c + 1) * 4 * LANES] = jnp.sum(
                jnp.where(hit, value[64 * f : 64 * f + 64], 0.0), axis=0, keepdims=True
            )


def placed(got, ocean_cells, rank):
    count = ocean_cells.shape[0]
    return pl.pallas_call(
        place_cells,
        out_shape=jax.ShapeDtypeStruct((3, count), f32),
        compiler_params=params(),
        name="place_cells",
    )(got, ocean_cells.reshape(count // LANES, LANES), rank)


def upward():
    count = lax.axis_size(both)
    return [(i, (i + 1) % count) for i in range(count)]


def around(first, last):
    up = upward()
    down = [(j, i) for i, j in up]
    return lax.ppermute(last, both, up), lax.ppermute(first, both, down)


def exchange(x, axis):
    return lax.all_to_all(x, axis, split_axis=0, concat_axis=0, tiled=True)


def body(atmos_state, neighbours, flux_weight, block_weights, block_ids, block_counts, ocean_cells):
    size = atmos_state.shape[3]
    elements = size * lax.axis_size(both)
    grp = lax.axis_index("grp").astype(i32).reshape(1)
    first = (lax.axis_index(both) * size).astype(i32).reshape(1)

    stepped, rim = bottom_stepped(atmos_state, neighbours)
    prev = lax.ppermute(rim, both, upward())

    shift = REACH // LANES * 16
    blocks = elements // LANES * 16
    live = jnp.arange(block_ids.shape[1])[None, :] < block_counts[:, None]
    ids = jnp.where(live, (block_ids + shift) % blocks, -1)
    ids = ids.reshape(-1, 4, 4).transpose(2, 0, 1).reshape(4, 64)
    ids = lax.dynamic_slice_in_dim(ids, lax.axis_index("grp"), 1, 0)
    ids = jnp.concatenate([ids, ids], axis=1)
    request, rank = requests(grp, ocean_cells, ids)

    inner = bottom_inner(stepped, neighbours, first, elements)
    slices = bottom_slices(stepped, prev, neighbours, inner, request, first, elements)
    table = exchange(slices, both)
    all_stepped, all_low, all_high = full_stepped(atmos_state)
    all_before, all_after = around(all_low, all_high)
    new_state = full_new_state(
        atmos_state.shape, all_stepped, all_before, all_after, neighbours, first, elements
    )

    answer, wanted = picked(table)
    answer, block_weights = lax.optimization_barrier((answer, block_weights))
    weights = packed_weights(grp, block_weights)
    got = exchange(answer, "blk")
    sent = remapped_cells(flux_weight, got, wanted, weights)
    ocean_flux = placed(exchange(sent, both), ocean_cells, rank)
    return new_state, ocean_flux


def solution(mesh):
    in_specs = (
        P(None, None, None, both),
        P(None, both),
        P(),
        P("blk", None, None, None),
        P("blk", None),
        P("blk"),
        P("blk"),
    )
    out_specs = (P(None, None, None, both), P("grp", "blk"))
    return jax.shard_map(body, mesh=mesh, in_specs=in_specs, out_specs=out_specs, check_vma=False)
```

```python
import functools

import jax
import jax.numpy as jnp
import ml_dtypes
import numpy as np
from jax import lax
from jax.experimental import pallas as pl
from jax.experimental.pallas import tpu as pltpu
from jax.sharding import PartitionSpec as P

time_step = 0.02
viscosity = 0.05
LANES = 128
REACH = 256
f32 = jnp.float32
bf16 = jnp.bfloat16
i32 = jnp.int32
both = ("grp", "blk")


def params(mebibytes=16):
    return pltpu.CompilerParams(vmem_limit_bytes=mebibytes * 1024 * 1024)


def in_hbm(x):
    return pltpu.with_memory_space_constraint(x, pltpu.HBM)


def cost(flops, moved):
    return pl.CostEstimate(flops=flops, bytes_accessed=moved, transcendentals=0)


def whole(shape):
    return pl.BlockSpec(shape, lambda *_: (0,) * len(shape))


def derivative_matrix():
    nodes = np.array([-1.0, -1.0 / np.sqrt(5.0), 1.0 / np.sqrt(5.0), 1.0])
    others = [[k for k in range(4) if k != n] for n in range(4)]
    weights = [np.prod([nodes[n] - nodes[k] for k in others[n]]) for n in range(4)]
    matrix = np.zeros((4, 4))
    for a in range(4):
        for c in range(4):
            if a != c:
                matrix[a, c] = weights[a] / weights[c] / (nodes[a] - nodes[c])
            else:
                matrix[a, a] = sum(1.0 / (nodes[a] - nodes[k]) for k in others[a])
    return matrix


def operators(copies):
    d = derivative_matrix().astype(np.float32).astype(np.float64)
    east, north = np.kron(np.eye(4), d), np.kron(d, np.eye(4))
    bend = east @ east + north @ north
    parts = [-time_step * east, -time_step * north, time_step * viscosity * bend]
    stacked = np.concatenate([np.kron(np.eye(copies), part) for part in parts])
    high = stacked.astype(ml_dtypes.bfloat16)
    low = (stacked - high.astype(np.float64)).astype(ml_dtypes.bfloat16)
    return jnp.asarray(np.concatenate([high, high, low], axis=1))


def split_two(x):
    high = x.astype(bf16)
    return high, (x - high.astype(f32)).astype(bf16)


def dot(a, b):
    return jnp.dot(a, b, preferred_element_type=f32)


def dot_nt(a, b):
    return lax.dot_general(a, b, (((1,), (1,)), ((), ())), preferred_element_type=f32)


def apply_operators(matrix, x):
    high, low = split_two(x)
    return dot(matrix, jnp.concatenate([high, low, high], axis=0))


def iota(shape, dim):
    return lax.broadcasted_iota(i32, shape, dim)


def bottom_step(x_ref, nb_ref, matrix_ref, out_ref, rim_ref):
    x = x_ref[:, 0].reshape(64, -1)
    op = apply_operators(matrix_ref[...], x)
    size = x.shape[1]
    for v in range(4):
        rows = slice(16 * v, 16 * v + 16)
        stepped = (
            x[rows] + x[0:16] * op[rows] + x[16:32] * op[64:128][rows] + op[128:192][rows]
        )
        out_ref[rows] = stepped
        rim_ref[rows] = stepped[:, size - 2 * REACH :]
        rim_ref[16 * v + 5 : 16 * v + 6, :REACH] = nb_ref[v : v + 1].astype(f32)


def bottom_stepped(state, neighbours):
    nvar, levels, points, size = state.shape
    matrix = operators(nvar)
    rim = (nvar * points, 2 * REACH)
    return pl.pallas_call(
        bottom_step,
        grid=(1,),
        in_specs=[
            pl.BlockSpec((nvar, 1, points, size), lambda i: (0, levels - 1, 0, 0)),
            pl.BlockSpec((4, REACH), lambda i: (0, size // REACH - 1)),
            whole(matrix.shape),
        ],
        out_specs=[pl.BlockSpec(memory_space=pltpu.VMEM), whole(rim)],
        out_shape=[pltpu.VMEM((nvar * points, size), f32), jax.ShapeDtypeStruct(rim, f32)],
        compiler_params=params(),
        name="bottom_step",
    )(in_hbm(state), in_hbm(neighbours), in_hbm(matrix))


def line_operators():
    d = derivative_matrix()
    d2 = d @ d
    slope = [
        (
            0.5 * (d[i, 0] - d[i, 3]),
            0.5 * (d[i, 1] - d[i, 2]),
            0.5 * (d[i, 0] + d[i, 3]),
        )
        for i in range(2)
    ]
    bend = [
        (
            0.5 * (d2[i, 0] - d2[i, 3]),
            0.5 * (d2[i, 1] - d2[i, 2]),
            0.5 * (d2[i, 0] + d2[i, 3]),
        )
        for i in range(2)
    ]
    return slope, bend


def along_line(x, slope, bend):
    t0, t1 = x[0] - x[3], x[1] - x[2]
    mean = (x[0] + x[3]) - (x[1] + x[2])
    first, second = [None] * 4, [None] * 4
    for i in range(2):
        a, b, c = [np.float32(-time_step * k) for k in slope[i]]
        even, odd = a * t0 + b * t1, c * mean
        first[i], first[3 - i] = even + odd, even - odd
        a, b, c = [np.float32(time_step * viscosity * k) for k in bend[i]]
        odd, even = a * t0 + b * t1, c * mean
        second[i], second[3 - i] = even + odd, even - odd
    return first, second


edge_points = (0, 1, 2, 3, 4, 7, 8, 11, 12, 13, 14, 15)


def full_step(left_ref, right_ref, out_ref, first_ref, last_ref):
    step = pl.program_id(0)
    slope, bend = line_operators()

    def points(x_ref, v, half):
        start = (v * 16 + half * 8) * 16
        return [x_ref[pl.ds(start + p, 8, stride=16), :] for p in range(16)]

    for part, x_ref in enumerate((left_ref, right_ref)):
        cols = slice(part * LANES, (part + 1) * LANES)
        for half in range(2):
            u, w = points(x_ref, 0, half), points(x_ref, 1, half)
            for v in range(4):
                x = u if v == 0 else w if v == 1 else points(x_ref, v, half)
                total = list(x)
                for a in range(4):
                    at = [4 * a + b for b in range(4)]
                    first, second = along_line([x[p] for p in at], slope, bend)
                    for p, one, two in zip(at, first, second):
                        total[p] = total[p] + (u[p] * one + two)
                for b in range(4):
                    at = [4 * a + b for a in range(4)]
                    first, second = along_line([x[p] for p in at], slope, bend)
                    for p, one, two in zip(at, first, second):
                        total[p] = total[p] + (w[p] * one + two)
                start = v * 16 + half * 8
                for p in range(16):
                    out_ref[p, start : start + 8, cols] = total[p]

    @pl.when(step == 0)
    def _():
        for k, p in enumerate(edge_points):
            first_ref[k] = out_ref[p].astype(bf16)

    @pl.when(step == pl.num_programs(0) - 1)
    def _():
        for k, p in enumerate(edge_points):
            last_ref[k] = out_ref[p].astype(bf16)


def full_stepped(state):
    nvar, levels, points, size = state.shape
    rows = nvar * levels
    rim = (len(edge_points), rows, REACH)
    flat = in_hbm(state.reshape(rows * points, size))
    return pl.pallas_call(
        full_step,
        grid=(size // REACH,),
        in_specs=[
            pl.BlockSpec((rows * points, LANES), lambda i: (0, 2 * i)),
            pl.BlockSpec((rows * points, LANES), lambda i: (0, 2 * i + 1)),
        ],
        out_specs=[
            pl.BlockSpec((points, rows, REACH), lambda i: (0, 0, i)),
            whole(rim),
            whole(rim),
        ],
        out_shape=[
            pltpu.HBM((points, rows, size), f32),
            jax.ShapeDtypeStruct(rim, bf16),
            jax.ShapeDtypeStruct(rim, bf16),
        ],
        compiler_params=params(24),
        cost_estimate=cost(4 * 10**7, 9 << 20),
        name="full_step",
    )(flat, flat)


def local_columns(neighbours, start, elements):
    place = neighbours - start
    place = jnp.where(place < 0, place + elements, place)
    return jnp.where(place >= elements, place - elements, place)


def side_indices(place, rows):
    part = [jnp.broadcast_to(place[s : s + 1], (rows, LANES)) for s in range(4)]
    point = iota((rows, LANES), 0) % 8
    we = jnp.where(point % 4 == 3, part[0], part[1])
    ns = jnp.where(point < 4, part[3], part[2])
    return we, ns


def look_up(columns, index, eb):
    lane = index & (LANES - 1)
    column = (index >> 7) - eb
    value = jnp.take_along_axis(columns[0], lane, axis=1)
    for c in range(1, 5):
        value = jnp.where(column == c, jnp.take_along_axis(columns[c], lane, axis=1), value)
    return value


def halves(x):
    grouped = x.reshape(x.shape[0] // 16, 2, 8, x.shape[1])
    shape = (x.shape[0] // 2, x.shape[1])
    return grouped[:, 0].reshape(shape), grouped[:, 1].reshape(shape)


def edge_update(columns, we, ns, eb):
    pairs = [halves(column) for column in columns]
    rows = pairs[0][0].shape[0]
    point = iota(pairs[0][0].shape, 0) % 8
    first = point < 4
    across = look_up([jnp.where(first, low, high) for low, high in pairs], ns, eb)
    zero = jnp.zeros(first.shape, f32)
    done = []
    for side in range(2):
        own = pairs[2][side]
        beside = look_up([pair[side] for pair in pairs], we, eb)
        total = jnp.where(point % 4 == 0, pltpu.roll(beside, rows - 3, 0) - own, zero)
        total += jnp.where(point % 4 == 3, pltpu.roll(beside, 3, 0) - own, zero)
        if side == 0:
            total += jnp.where(first, pltpu.roll(across, rows - 4, 0) - own, zero)
        else:
            total += jnp.where(first, zero, pltpu.roll(across, 4, 0) - own)
        done.append((own + 0.5 * total).reshape(-1, 1, 8, own.shape[1]))
    return jnp.concatenate(done, axis=1).reshape(columns[0].shape)


def lane_tiles(ref, count):
    return [ref[:, c * LANES : (c + 1) * LANES] for c in range(count)]


def inner_edges(elements, first_ref, s_ref, nb_ref, out_ref):
    size = s_ref.shape[1]
    place = local_columns(nb_ref[...], first_ref[0], elements)
    tiles = lane_tiles(s_ref, size // LANES)
    for eb in range(size // LANES - 4):
        cols = slice(eb * LANES + REACH, eb * LANES + REACH + LANES)
        we, ns = side_indices(place[:, cols], 32)
        out_ref[:, eb * LANES : (eb + 1) * LANES] = edge_update(tiles[eb : eb + 5], we, ns, eb)


def bottom_inner(stepped, neighbours, first, elements):
    rows, size = stepped.shape
    vmem = pl.BlockSpec(memory_space=pltpu.VMEM)
    return pl.pallas_call(
        functools.partial(inner_edges, elements),
        in_specs=[pl.BlockSpec(memory_space=pltpu.SMEM), vmem, vmem],
        out_specs=vmem,
        out_shape=pltpu.VMEM((rows, size - 2 * REACH), f32),
        compiler_params=params(),
        name="bottom_inner",
    )(first, stepped, neighbours)


def bottom_edges(elements, first_ref, s_ref, prev_ref, nb_ref, inner_ref, request_ref, out_ref):
    out_ref[:, 0, 2 * LANES :] = request_ref[...]
    edge = 2 * REACH // LANES
    carried = [prev_ref[16 * v + 5 : 16 * v + 6, :REACH] for v in range(4)]
    neighbours = jnp.concatenate(
        [jnp.concatenate(carried, axis=0).astype(i32), nb_ref[:, :REACH]], axis=1
    )
    place = local_columns(neighbours, first_ref[0] - 2 * REACH, elements)
    tiles = lane_tiles(prev_ref, edge) + lane_tiles(s_ref, edge)
    new = []
    for eb in range(edge):
        we, ns = side_indices(place[:, eb * LANES : (eb + 1) * LANES], 32)
        new.append(edge_update(tiles[eb : eb + 5], we, ns, eb))
    new += lane_tiles(inner_ref, inner_ref.shape[1] // LANES)
    for v in range(4):
        blocks = jnp.concatenate([piece[16 * v : 16 * v + 16] for piece in new], axis=0)
        turned = blocks.T
        for g in range(4):
            rows = slice(64 * g + 16 * v, 64 * g + 16 * v + 16)
            for h in range(2):
                at = 32 * g + 16 * h
                out_ref[rows, 0, h * LANES : (h + 1) * LANES] = turned[at : at + 16]


def bottom_slices(stepped, prev, neighbours, inner, request, first, elements):
    vmem = pl.BlockSpec(memory_space=pltpu.VMEM)
    return pl.pallas_call(
        functools.partial(bottom_edges, elements),
        in_specs=[pl.BlockSpec(memory_space=pltpu.SMEM)] + [vmem] * 5,
        out_shape=jax.ShapeDtypeStruct((256, 1, 3 * LANES), f32),
        compiler_params=params(),
        name="bottom_edges",
    )(first, stepped, prev, neighbours, inner, request)


sides = (
    ((3, 7, 11, 15), (0, 4, 8, 12)),
    ((0, 4, 8, 12), (3, 7, 11, 15)),
    ((12, 13, 14, 15), (0, 1, 2, 3)),
    ((0, 1, 2, 3), (12, 13, 14, 15)),
)


def full_edges(
    elements,
    first_ref,
    ahead_ref,
    before_ref,
    after_ref,
    nb_ref,
    out_ref,
    own_ref,
    split_ref,
    turn_ref,
):
    step = pl.program_id(0)
    tiles = pl.num_programs(0) - 1
    rows = own_ref.shape[1]
    empty = jnp.zeros((rows, REACH), bf16)

    @pl.when(step == 0)
    def _():
        for k, p in enumerate(edge_points):
            split_ref[0, p, :, :REACH] = before_ref[k]
            split_ref[1, p, :, :REACH] = empty

    place_at = pl.multiple_of((step + 1) * REACH, REACH)

    @pl.when(step < tiles)
    def _():
        for p in edge_points:
            high, low = split_two(ahead_ref[p])
            split_ref[0, p, :, pl.ds(place_at, REACH)] = high
            split_ref[1, p, :, pl.ds(place_at, REACH)] = low

    @pl.when(step == tiles)
    def _():
        for k, p in enumerate(edge_points):
            split_ref[0, p, :, pl.ds(place_at, REACH)] = after_ref[k]
            split_ref[1, p, :, pl.ds(place_at, REACH)] = empty

    @pl.when(step > 0)
    def _():
        place = local_columns(nb_ref[...], first_ref[0] - REACH, elements) - (step - 1) * REACH
        start = pl.multiple_of((step - 1) * REACH, REACH)
        change = [None] * 16
        for side, (source, target) in enumerate(sides):
            onehot = jnp.where(
                iota((3 * REACH, REACH), 0) == place[side : side + 1, :], 1.0, 0.0
            ).astype(bf16)
            pieces = [
                split_ref[part, p, :, pl.ds(start, 3 * REACH)]
                for part in range(2)
                for p in source
            ]
            value = dot(jnp.concatenate(pieces, axis=0), onehot)
            for k, p in enumerate(target):
                there = value[k * rows : (k + 1) * rows] + value[(4 + k) * rows : (5 + k) * rows]
                part = there - own_ref[p]
                change[p] = part if change[p] is None else change[p] + part
        for p in range(16):
            new = own_ref[p] if change[p] is None else own_ref[p] + 0.5 * change[p]
            for h in range(2):
                turn_ref[h, pl.ds(p, rows, stride=16), :] = new[:, h * LANES : (h + 1) * LANES]
        for h in range(2):
            out_ref[:, h * LANES : (h + 1) * LANES] = turn_ref[h]

    @pl.when(step < tiles)
    def _():
        own_ref[...] = ahead_ref[...]


def full_new_state(shape, stepped, before, after, neighbours, first, elements):
    points, rows, size = stepped.shape
    tiles = size // REACH
    tile = (points, rows, REACH)
    out = pl.pallas_call(
        functools.partial(full_edges, elements),
        grid=(tiles + 1,),
        in_specs=[
            pl.BlockSpec(memory_space=pltpu.SMEM),
            pl.BlockSpec(tile, lambda i: (0, 0, jnp.minimum(i, tiles - 1))),
            whole(before.shape),
            whole(after.shape),
            pl.BlockSpec((4, REACH), lambda i: (0, jnp.maximum(i - 1, 0))),
        ],
        out_specs=pl.BlockSpec((rows * points, REACH), lambda i: (0, jnp.maximum(i - 1, 0))),
        out_shape=jax.ShapeDtypeStruct((rows * points, size), f32),
        scratch_shapes=[
            pltpu.VMEM(tile, f32),
            pltpu.VMEM((2, 16, rows, size + 2 * REACH), bf16),
            pltpu.VMEM((2, rows * points, LANES), f32),
        ],
        compiler_params=params(24),
        cost_estimate=cost(4 * 10**9, 10 << 20),
        name="full_edges",
    )(first, in_hbm(stepped), before, after, neighbours)
    return out.reshape(shape)


def request_table(grp_ref, cells_ref, ids_ref, out_ref, rank_ref):
    chunks = cells_ref.shape[0]
    owner_at = iota((64, LANES), 0)
    cells = [cells_ref[c : c + 1, :] for c in range(chunks)]
    mine = [jnp.where(owner_at == (cell >> 11), 1.0, 0.0) for cell in cells]
    before = jnp.where(iota((LANES, 2 * LANES), 0) < iota((LANES, 2 * LANES), 1), 1.0, 0.0)
    counts = dot(jnp.concatenate(mine, axis=0).astype(bf16), before.astype(bf16))
    carried = jnp.zeros((64, LANES), f32)
    slots, high, low = [], [], []
    for c, cell in enumerate(cells):
        count = counts[64 * c : 64 * c + 64]
        rank = jnp.sum(mine[c] * (count[:, :LANES] + carried), axis=0, keepdims=True).astype(i32)
        carried = carried + count[:, LANES:]
        rank_ref[c : c + 1, :] = rank
        slots.append(jnp.where(owner_at == rank, 1.0, 0.0).astype(bf16))
        row = cell & 2047
        high.append((mine[c] * (row >> 7).astype(f32)).astype(bf16))
        low.append((mine[c] * (row & 127).astype(f32)).astype(bf16))
    parts = jnp.concatenate([jnp.concatenate(p, axis=1) for p in (high, low)], axis=0)
    wanted = dot_nt(parts, jnp.concatenate(slots, axis=1))
    wanted = wanted[:64] * 128.0 + wanted[64:]
    wanted = jnp.concatenate([wanted, wanted], axis=1)
    share = pltpu.roll(wanted, 64 - 12 * grp_ref[0], 1)
    message = jnp.where(iota((64, LANES), 1) < 64, ids_ref[...].astype(f32), share)
    for y in range(4):
        out_ref[64 * y : 64 * y + 64, :] = message


def requests(grp, ocean_cells, ids):
    chunks = ocean_cells.shape[0] // LANES
    vmem = pl.BlockSpec(memory_space=pltpu.VMEM)
    return pl.pallas_call(
        request_table,
        in_specs=[pl.BlockSpec(memory_space=pltpu.SMEM), vmem, vmem],
        out_shape=[
            jax.ShapeDtypeStruct((256, LANES), f32),
            jax.ShapeDtypeStruct((chunks, LANES), i32),
        ],
        compiler_params=params(),
        name="request_table",
    )(grp, ocean_cells.reshape(chunks, LANES), ids)


QUERIES = 256


def pick_values(table_ref, out_ref, cells_ref, turned_ref, ids_ref, found_ref):
    lane = iota((LANES, LANES), 1)
    asked = table_ref[:, 0, 2 * LANES :]
    ids = jnp.where(lane < 64, asked[:LANES], pltpu.roll(asked[LANES:], 64, 1))
    ids_ref[...] = ids.astype(i32)
    lane = iota((64, LANES), 1)
    wanted = jnp.zeros((64, LANES), f32)
    for y in range(4):
        part = pltpu.roll(asked[64 * y : 64 * y + 64], 64 + 12 * y, 1)
        wanted = jnp.where((lane >= 12 * y) & (lane < 12 * y + 12), part, wanted)
    lane = iota((32, LANES), 1)
    cells_ref[...] = jnp.where(lane < 64, wanted[:32], pltpu.roll(wanted[32:], 64, 1)).astype(i32)

    high, low = split_two(table_ref[:, 0, : 2 * LANES].T)
    for half in range(2):
        turned_ref[half, :LANES] = high[half * LANES : (half + 1) * LANES]
        turned_ref[half, LANES:] = low[half * LANES : (half + 1) * LANES]
    groups = QUERIES // LANES
    device_at = iota((256, QUERIES), 0)
    block_at = iota((LANES, QUERIES), 0)

    def some(step, carry):
        rows = [ids_ref[pl.ds(groups * step + k, 1), :] for k in range(groups)]
        asked = jnp.concatenate(rows, axis=1)
        onehot = jnp.where(device_at == (asked >> 7), 1.0, 0.0).astype(bf16)
        hit = block_at == (asked & 127)
        for half in range(2):
            value = dot(turned_ref[half], onehot)
            part = value[:LANES] + value[LANES:]
            found = jnp.sum(jnp.where(hit, part, 0.0), axis=0, keepdims=True)
            for k in range(groups):
                found_ref[half, pl.ds(groups * step + k, 1), :] = found[
                    :, k * LANES : (k + 1) * LANES
                ]
        return carry

    lax.fori_loop(0, LANES // groups, some, 0, unroll=32)
    for half in range(2):
        for y in range(2):
            at = (2 * half + y) * LANES
            out_ref[:, 0, at : at + LANES] = found_ref[half, 64 * y : 64 * y + 64, :]


def picked(table):
    return pl.pallas_call(
        pick_values,
        out_shape=[
            pltpu.HBM((64, 1, 4 * LANES), f32),
            jax.ShapeDtypeStruct((32, LANES), i32),
        ],
        scratch_shapes=[
            pltpu.VMEM((2, 256, 256), bf16),
            pltpu.VMEM((LANES, LANES), i32),
            pltpu.VMEM((2, LANES, LANES), f32),
        ],
        compiler_params=params(24),
        name="pick_values",
    )(table)


def quarter_weights(grp_ref, w_ref, out_ref):
    column, lane = iota((4 * LANES, LANES), 0), iota((4 * LANES, LANES), 1)
    wanted = (column // LANES == lane // 32) & (
        column % LANES == 32 * grp_ref[0] + lane % 32
    )
    chosen = jnp.where(wanted, 1.0, 0.0).astype(bf16)
    at = [(r, b) for r in range(w_ref.shape[0]) for b in range(4)]
    rows = [
        jnp.concatenate([w_ref[r, 4 * b + q] for q in range(4)], axis=1) for r, b in at
    ]
    packed = dot(jnp.concatenate(rows, axis=0), chosen).astype(bf16)
    for k, (r, b) in enumerate(at):
        out_ref[r, b] = packed[LANES * k : LANES * (k + 1)]


def packed_weights(grp, block_weights):
    count, slots, block = block_weights.shape[:3]
    step = 8
    return pl.pallas_call(
        quarter_weights,
        grid=(count // step,),
        in_specs=[
            pl.BlockSpec(memory_space=pltpu.SMEM),
            pl.BlockSpec((step, slots, block, block), lambda i: (i, 0, 0, 0)),
        ],
        out_specs=pl.BlockSpec((step, slots // 4, block, block), lambda i: (i, 0, 0, 0)),
        out_shape=jax.ShapeDtypeStruct((count, slots // 4, block, block), bf16),
        compiler_params=params(),
        cost_estimate=cost(10**9, 10 << 20),
        name="quarter_weights",
    )(grp, in_hbm(block_weights))


def remap_rows(
    fw_ref, got_ref, index_ref, w_ref, out_ref, field_ref, mapped_ref, sent_ref, pair_ref
):
    values = []
    for v in range(4):
        rows = slice(16 * v, 16 * v + 16)
        tiles = [
            got_ref[rows, 0, (2 * h + y) * LANES : (2 * h + y + 1) * LANES]
            for y in range(2)
            for h in range(2)
        ]
        turned = jnp.concatenate(tiles, axis=0).T
        values.append(jnp.concatenate([turned[:64], turned[64:]], axis=1))
    wind = jnp.sqrt(1.0 + values[0] * values[0] + values[1] * values[1])
    for f in range(16):
        if f < 12:
            total = fw_ref[f, 0] * values[0]
            for v in range(1, 4):
                total += fw_ref[f, v] * values[v]
            total = (total * wind).astype(bf16).astype(f32)
        else:
            total = jnp.zeros((64, LANES), f32)
        field_ref[pl.ds(f, 64, stride=16), :] = total

    for r in range(16):
        total = jnp.zeros((16, LANES), f32)
        for b in range(0, 4, 2):
            at = (r * 4 + b) * 16
            pair = field_ref[at : at + 32, :].astype(bf16)
            pair = jnp.concatenate([pair[:16], pair[16:]], axis=1)
            weights = jnp.concatenate([w_ref[r, b], w_ref[r, b + 1]], axis=1)
            total += dot_nt(pair, weights)
        mapped_ref[16 * r : 16 * r + 16, :] = total

    parts = mapped_ref[...].astype(bf16)
    row_at = iota((LANES, 4 * LANES), 0)

    def some(at, carry):
        rows = [index_ref[pl.ds(4 * at + k, 1), :] for k in range(4)]
        asked = jnp.concatenate(rows, axis=1)
        onehot = jnp.where(row_at == (asked & 127), 1.0, 0.0).astype(bf16)
        value = dot(parts, onehot)
        block = asked >> 7
        found = value[:16]
        for r in range(1, 16):
            found = jnp.where(block == r, value[16 * r : 16 * r + 16], found)
        for k in range(4):
            sent_ref[pl.ds(4 * at + k, 16, stride=32), :] = found[
                :, k * LANES : (k + 1) * LANES
            ]
        return carry

    lax.fori_loop(0, 8, some, 0, unroll=True)
    lane = iota((32, LANES), 1)
    for y in range(4):
        a, b, c = [sent_ref[(3 * y + f) * 32 : (3 * y + f) * 32 + 32, :] for f in range(3)]
        base = 64 * y
        low, high = slice(base, base + 32), slice(base + 32, base + 64)
        pair_ref[low, 0, :] = jnp.where(lane < 64, a, pltpu.roll(b, 64, 1))
        pair_ref[low, 1, :] = c
        pair_ref[high, 0, :] = jnp.where(lane < 64, pltpu.roll(a, 64, 1), b)
        pair_ref[high, 1, :] = pltpu.roll(c, 64, 1)
    out_ref[...] = pair_ref[...].astype(bf16)


def remapped_cells(flux_weight, got, index, block_weights):
    smem = pl.BlockSpec(memory_space=pltpu.SMEM)
    vmem = pl.BlockSpec(memory_space=pltpu.VMEM)
    return pl.pallas_call(
        remap_rows,
        in_specs=[smem, vmem, vmem, vmem],
        out_shape=jax.ShapeDtypeStruct((256, 2, LANES), bf16),
        scratch_shapes=[
            pltpu.VMEM((64 * 16, LANES), f32),
            pltpu.VMEM((256, LANES), f32),
            pltpu.VMEM((17 * 32, LANES), f32),
            pltpu.VMEM((256, 2, LANES), f32),
        ],
        compiler_params=params(),
        name="remap_rows",
    )(flux_weight, got, index, block_weights)


def place_cells(got_ref, cells_ref, rank_ref, out_ref):
    got = got_ref[...].astype(f32)
    got = got[0:64] + got[64:128] + got[128:192] + got[192:256]
    pair, last = got[:, 0, :].T, got[:, 1, :].T
    parts = jnp.concatenate(split_two(jnp.concatenate([pair, last[:64]], axis=0)), axis=1)
    owner_at = iota((64, 4 * LANES), 0)
    for c in range(4):
        rows = range(4 * c, 4 * c + 4)
        cell = jnp.concatenate([cells_ref[r : r + 1, :] for r in rows], axis=1)
        rank = jnp.concatenate([rank_ref[r : r + 1, :] for r in rows], axis=1)
        onehot = jnp.where(owner_at == (cell >> 11), 1.0, 0.0).astype(bf16)
        value = dot(parts, jnp.concatenate([onehot, onehot], axis=0))
        hit = owner_at == rank
        for f in range(3):
            out_ref[f : f + 1, c * 4 * LANES : (c + 1) * 4 * LANES] = jnp.sum(
                jnp.where(hit, value[64 * f : 64 * f + 64], 0.0), axis=0, keepdims=True
            )


def placed(got, ocean_cells, rank):
    count = ocean_cells.shape[0]
    return pl.pallas_call(
        place_cells,
        out_shape=jax.ShapeDtypeStruct((3, count), f32),
        compiler_params=params(),
        name="place_cells",
    )(got, ocean_cells.reshape(count // LANES, LANES), rank)


def upward():
    count = lax.axis_size(both)
    return [(i, (i + 1) % count) for i in range(count)]


def exchange(x, axis):
    return lax.all_to_all(x, axis, split_axis=0, concat_axis=0, tiled=True)


def body(atmos_state, neighbours, flux_weight, block_weights, block_ids, block_counts, ocean_cells):
    size = atmos_state.shape[3]
    elements = size * lax.axis_size(both)
    grp = lax.axis_index("grp").astype(i32).reshape(1)
    first = (lax.axis_index(both) * size).astype(i32).reshape(1)

    stepped, rim = bottom_stepped(atmos_state, neighbours)
    prev = lax.ppermute(rim, both, upward())

    shift = REACH // LANES * 16
    blocks = elements // LANES * 16
    live = jnp.arange(block_ids.shape[1])[None, :] < block_counts[:, None]
    ids = jnp.where(live, (block_ids + shift) % blocks, -1)
    ids = ids.reshape(-1, 4, 4).transpose(2, 0, 1).reshape(4, 64)
    ids = lax.dynamic_slice_in_dim(ids, lax.axis_index("grp"), 1, 0)
    ids = jnp.concatenate([ids, ids], axis=1)
    request, rank = requests(grp, ocean_cells, ids)

    inner = bottom_inner(stepped, neighbours, first, elements)
    slices = bottom_slices(stepped, prev, neighbours, inner, request, first, elements)
    table = exchange(slices, both)
    all_stepped, all_low, all_high = full_stepped(atmos_state)
    all_before = lax.ppermute(all_high, both, upward())
    answer, wanted = picked(table)
    answer, block_weights, all_low = lax.optimization_barrier((answer, block_weights, all_low))
    weights = packed_weights(grp, block_weights)
    got = exchange(answer, "blk")
    all_after = lax.ppermute(all_low, both, [(j, i) for i, j in upward()])
    new_state = full_new_state(
        atmos_state.shape, all_stepped, all_before, all_after, neighbours, first, elements
    )
    sent = remapped_cells(flux_weight, got, wanted, weights)
    ocean_flux = placed(exchange(sent, both), ocean_cells, rank)
    return new_state, ocean_flux


def solution(mesh):
    in_specs = (
        P(None, None, None, both),
        P(None, both),
        P(),
        P("blk", None, None, None),
        P("blk", None),
        P("blk"),
        P("blk"),
    )
    out_specs = (P(None, None, None, both), P("grp", "blk"))
    return jax.shard_map(body, mesh=mesh, in_specs=in_specs, out_specs=out_specs, check_vma=False)
```

```python
import functools

import jax
import jax.numpy as jnp
import ml_dtypes
import numpy as np
from jax import lax
from jax.experimental import pallas as pl
from jax.experimental.pallas import tpu as pltpu
from jax.sharding import PartitionSpec as P

time_step = 0.02
viscosity = 0.05
LANES = 128
REACH = 256
f32 = jnp.float32
bf16 = jnp.bfloat16
i32 = jnp.int32
both = ("grp", "blk")


def params(mebibytes=16):
    return pltpu.CompilerParams(vmem_limit_bytes=mebibytes * 1024 * 1024)


def in_hbm(x):
    return pltpu.with_memory_space_constraint(x, pltpu.HBM)


def cost(flops, moved):
    return pl.CostEstimate(flops=flops, bytes_accessed=moved, transcendentals=0)


def whole(shape):
    return pl.BlockSpec(shape, lambda *_: (0,) * len(shape))


def derivative_matrix():
    nodes = np.array([-1.0, -1.0 / np.sqrt(5.0), 1.0 / np.sqrt(5.0), 1.0])
    others = [[k for k in range(4) if k != n] for n in range(4)]
    weights = [np.prod([nodes[n] - nodes[k] for k in others[n]]) for n in range(4)]
    matrix = np.zeros((4, 4))
    for a in range(4):
        for c in range(4):
            if a != c:
                matrix[a, c] = weights[a] / weights[c] / (nodes[a] - nodes[c])
            else:
                matrix[a, a] = sum(1.0 / (nodes[a] - nodes[k]) for k in others[a])
    return matrix


def operators(copies):
    d = derivative_matrix().astype(np.float32).astype(np.float64)
    east, north = np.kron(np.eye(4), d), np.kron(d, np.eye(4))
    bend = east @ east + north @ north
    parts = [-time_step * east, -time_step * north, time_step * viscosity * bend]
    stacked = np.concatenate([np.kron(np.eye(copies), part) for part in parts])
    high = stacked.astype(ml_dtypes.bfloat16)
    low = (stacked - high.astype(np.float64)).astype(ml_dtypes.bfloat16)
    return jnp.asarray(np.concatenate([high, high, low], axis=1))


def split_two(x):
    high = x.astype(bf16)
    return high, (x - high.astype(f32)).astype(bf16)


def dot(a, b):
    return jnp.dot(a, b, preferred_element_type=f32)


def dot_nt(a, b):
    return lax.dot_general(a, b, (((1,), (1,)), ((), ())), preferred_element_type=f32)


def apply_operators(matrix, x):
    high, low = split_two(x)
    return dot(matrix, jnp.concatenate([high, low, high], axis=0))


def iota(shape, dim):
    return lax.broadcasted_iota(i32, shape, dim)


def bottom_step(x_ref, nb_ref, matrix_ref, out_ref, rim_ref):
    x = x_ref[:, 0].reshape(64, -1)
    op = apply_operators(matrix_ref[...], x)
    size = x.shape[1]
    for v in range(4):
        rows = slice(16 * v, 16 * v + 16)
        stepped = (
            x[rows] + x[0:16] * op[rows] + x[16:32] * op[64:128][rows] + op[128:192][rows]
        )
        out_ref[rows] = stepped
        rim_ref[rows] = stepped[:, size - 2 * REACH :]
        rim_ref[16 * v + 5 : 16 * v + 6, :REACH] = nb_ref[v : v + 1].astype(f32)


def bottom_stepped(state, neighbours):
    nvar, levels, points, size = state.shape
    matrix = operators(nvar)
    rim = (nvar * points, 2 * REACH)
    return pl.pallas_call(
        bottom_step,
        grid=(1,),
        in_specs=[
            pl.BlockSpec((nvar, 1, points, size), lambda i: (0, levels - 1, 0, 0)),
            pl.BlockSpec((4, REACH), lambda i: (0, size // REACH - 1)),
            whole(matrix.shape),
        ],
        out_specs=[pl.BlockSpec(memory_space=pltpu.VMEM), whole(rim)],
        out_shape=[pltpu.VMEM((nvar * points, size), f32), jax.ShapeDtypeStruct(rim, f32)],
        compiler_params=params(),
        name="bottom_step",
    )(in_hbm(state), in_hbm(neighbours), in_hbm(matrix))


def line_operators():
    d = derivative_matrix()
    d2 = d @ d
    slope = [
        (
            0.5 * (d[i, 0] - d[i, 3]),
            0.5 * (d[i, 1] - d[i, 2]),
            0.5 * (d[i, 0] + d[i, 3]),
        )
        for i in range(2)
    ]
    bend = [
        (
            0.5 * (d2[i, 0] - d2[i, 3]),
            0.5 * (d2[i, 1] - d2[i, 2]),
            0.5 * (d2[i, 0] + d2[i, 3]),
        )
        for i in range(2)
    ]
    return slope, bend


def along_line(x, slope, bend):
    t0, t1 = x[0] - x[3], x[1] - x[2]
    mean = (x[0] + x[3]) - (x[1] + x[2])
    first, second = [None] * 4, [None] * 4
    for i in range(2):
        a, b, c = [np.float32(-time_step * k) for k in slope[i]]
        even, odd = a * t0 + b * t1, c * mean
        first[i], first[3 - i] = even + odd, even - odd
        a, b, c = [np.float32(time_step * viscosity * k) for k in bend[i]]
        odd, even = a * t0 + b * t1, c * mean
        second[i], second[3 - i] = even + odd, even - odd
    return first, second


edge_points = (0, 1, 2, 3, 4, 7, 8, 11, 12, 13, 14, 15)


def full_step(left_ref, right_ref, out_ref, first_ref, last_ref):
    step = pl.program_id(0)
    slope, bend = line_operators()

    def points(x_ref, v, half):
        start = (v * 16 + half * 8) * 16
        return [x_ref[pl.ds(start + p, 8, stride=16), :] for p in range(16)]

    for part, x_ref in enumerate((left_ref, right_ref)):
        cols = slice(part * LANES, (part + 1) * LANES)
        for half in range(2):
            u, w = points(x_ref, 0, half), points(x_ref, 1, half)
            for v in range(4):
                x = u if v == 0 else w if v == 1 else points(x_ref, v, half)
                total = list(x)
                for a in range(4):
                    at = [4 * a + b for b in range(4)]
                    first, second = along_line([x[p] for p in at], slope, bend)
                    for p, one, two in zip(at, first, second):
                        total[p] = total[p] + (u[p] * one + two)
                for b in range(4):
                    at = [4 * a + b for a in range(4)]
                    first, second = along_line([x[p] for p in at], slope, bend)
                    for p, one, two in zip(at, first, second):
                        total[p] = total[p] + (w[p] * one + two)
                start = v * 16 + half * 8
                for p in range(16):
                    out_ref[p, start : start + 8, cols] = total[p]

    @pl.when(step == 0)
    def _():
        for k, p in enumerate(edge_points):
            first_ref[k] = out_ref[p].astype(bf16)

    @pl.when(step == pl.num_programs(0) - 1)
    def _():
        for k, p in enumerate(edge_points):
            last_ref[k] = out_ref[p].astype(bf16)


def full_stepped(state):
    nvar, levels, points, size = state.shape
    rows = nvar * levels
    rim = (len(edge_points), rows, REACH)
    flat = in_hbm(state.reshape(rows * points, size))
    return pl.pallas_call(
        full_step,
        grid=(size // REACH,),
        in_specs=[
            pl.BlockSpec((rows * points, LANES), lambda i: (0, 2 * i)),
            pl.BlockSpec((rows * points, LANES), lambda i: (0, 2 * i + 1)),
        ],
        out_specs=[
            pl.BlockSpec((points, rows, REACH), lambda i: (0, 0, i)),
            whole(rim),
            whole(rim),
        ],
        out_shape=[
            pltpu.HBM((points, rows, size), f32),
            jax.ShapeDtypeStruct(rim, bf16),
            jax.ShapeDtypeStruct(rim, bf16),
        ],
        compiler_params=params(24),
        cost_estimate=cost(4 * 10**7, 9 << 20),
        name="full_step",
    )(flat, flat)


def local_columns(neighbours, start, elements):
    place = neighbours - start
    place = jnp.where(place < 0, place + elements, place)
    return jnp.where(place >= elements, place - elements, place)


def side_indices(place, rows):
    part = [jnp.broadcast_to(place[s : s + 1], (rows, LANES)) for s in range(4)]
    point = iota((rows, LANES), 0) % 8
    we = jnp.where(point % 4 == 3, part[0], part[1])
    ns = jnp.where(point < 4, part[3], part[2])
    return we, ns


def look_up(columns, index, eb):
    lane = index & (LANES - 1)
    column = (index >> 7) - eb
    value = jnp.take_along_axis(columns[0], lane, axis=1)
    for c in range(1, 5):
        value = jnp.where(column == c, jnp.take_along_axis(columns[c], lane, axis=1), value)
    return value


def halves(x):
    grouped = x.reshape(x.shape[0] // 16, 2, 8, x.shape[1])
    shape = (x.shape[0] // 2, x.shape[1])
    return grouped[:, 0].reshape(shape), grouped[:, 1].reshape(shape)


def edge_update(columns, we, ns, eb):
    pairs = [halves(column) for column in columns]
    rows = pairs[0][0].shape[0]
    point = iota(pairs[0][0].shape, 0) % 8
    first = point < 4
    across = look_up([jnp.where(first, low, high) for low, high in pairs], ns, eb)
    zero = jnp.zeros(first.shape, f32)
    done = []
    for side in range(2):
        own = pairs[2][side]
        beside = look_up([pair[side] for pair in pairs], we, eb)
        total = jnp.where(point % 4 == 0, pltpu.roll(beside, rows - 3, 0) - own, zero)
        total += jnp.where(point % 4 == 3, pltpu.roll(beside, 3, 0) - own, zero)
        if side == 0:
            total += jnp.where(first, pltpu.roll(across, rows - 4, 0) - own, zero)
        else:
            total += jnp.where(first, zero, pltpu.roll(across, 4, 0) - own)
        done.append((own + 0.5 * total).reshape(-1, 1, 8, own.shape[1]))
    return jnp.concatenate(done, axis=1).reshape(columns[0].shape)


def lane_tiles(ref, count):
    return [ref[:, c * LANES : (c + 1) * LANES] for c in range(count)]


def inner_edges(elements, first_ref, s_ref, nb_ref, out_ref):
    size = s_ref.shape[1]
    place = local_columns(nb_ref[...], first_ref[0], elements)
    tiles = lane_tiles(s_ref, size // LANES)
    for eb in range(size // LANES - 4):
        cols = slice(eb * LANES + REACH, eb * LANES + REACH + LANES)
        we, ns = side_indices(place[:, cols], 32)
        out_ref[:, eb * LANES : (eb + 1) * LANES] = edge_update(tiles[eb : eb + 5], we, ns, eb)


def bottom_inner(stepped, neighbours, first, elements):
    rows, size = stepped.shape
    vmem = pl.BlockSpec(memory_space=pltpu.VMEM)
    return pl.pallas_call(
        functools.partial(inner_edges, elements),
        in_specs=[pl.BlockSpec(memory_space=pltpu.SMEM), vmem, vmem],
        out_specs=vmem,
        out_shape=pltpu.VMEM((rows, size - 2 * REACH), f32),
        compiler_params=params(),
        name="bottom_inner",
    )(first, stepped, neighbours)


def bottom_edges(elements, first_ref, s_ref, prev_ref, nb_ref, inner_ref, request_ref, out_ref):
    out_ref[:, 0, 2 * LANES :] = request_ref[...]
    edge = 2 * REACH // LANES
    carried = [prev_ref[16 * v + 5 : 16 * v + 6, :REACH] for v in range(4)]
    neighbours = jnp.concatenate(
        [jnp.concatenate(carried, axis=0).astype(i32), nb_ref[:, :REACH]], axis=1
    )
    place = local_columns(neighbours, first_ref[0] - 2 * REACH, elements)
    tiles = lane_tiles(prev_ref, edge) + lane_tiles(s_ref, edge)
    new = []
    for eb in range(edge):
        we, ns = side_indices(place[:, eb * LANES : (eb + 1) * LANES], 32)
        new.append(edge_update(tiles[eb : eb + 5], we, ns, eb))
    new += lane_tiles(inner_ref, inner_ref.shape[1] // LANES)
    for v in range(4):
        blocks = jnp.concatenate([piece[16 * v : 16 * v + 16] for piece in new], axis=0)
        turned = blocks.T
        for g in range(4):
            rows = slice(64 * g + 16 * v, 64 * g + 16 * v + 16)
            for h in range(2):
                at = 32 * g + 16 * h
                out_ref[rows, 0, h * LANES : (h + 1) * LANES] = turned[at : at + 16]


def bottom_slices(stepped, prev, neighbours, inner, request, first, elements):
    vmem = pl.BlockSpec(memory_space=pltpu.VMEM)
    return pl.pallas_call(
        functools.partial(bottom_edges, elements),
        in_specs=[pl.BlockSpec(memory_space=pltpu.SMEM)] + [vmem] * 5,
        out_shape=jax.ShapeDtypeStruct((256, 1, 3 * LANES), f32),
        compiler_params=params(),
        name="bottom_edges",
    )(first, stepped, prev, neighbours, inner, request)


sides = (
    ((3, 7, 11, 15), (0, 4, 8, 12)),
    ((0, 4, 8, 12), (3, 7, 11, 15)),
    ((12, 13, 14, 15), (0, 1, 2, 3)),
    ((0, 1, 2, 3), (12, 13, 14, 15)),
)


def full_edges(
    elements,
    first_ref,
    ahead_ref,
    before_ref,
    after_ref,
    nb_ref,
    out_ref,
    own_ref,
    split_ref,
    turn_ref,
):
    step = pl.program_id(0)
    tiles = pl.num_programs(0) - 1
    rows = own_ref.shape[1]
    empty = jnp.zeros((rows, REACH), bf16)

    @pl.when(step == 0)
    def _():
        for k, p in enumerate(edge_points):
            split_ref[0, p, :, :REACH] = before_ref[k]
            split_ref[1, p, :, :REACH] = empty

    place_at = pl.multiple_of((step + 1) * REACH, REACH)

    @pl.when(step < tiles)
    def _():
        for p in edge_points:
            high, low = split_two(ahead_ref[p])
            split_ref[0, p, :, pl.ds(place_at, REACH)] = high
            split_ref[1, p, :, pl.ds(place_at, REACH)] = low

    @pl.when(step == tiles)
    def _():
        for k, p in enumerate(edge_points):
            split_ref[0, p, :, pl.ds(place_at, REACH)] = after_ref[k]
            split_ref[1, p, :, pl.ds(place_at, REACH)] = empty

    @pl.when(step > 0)
    def _():
        place = local_columns(nb_ref[...], first_ref[0] - REACH, elements) - (step - 1) * REACH
        start = pl.multiple_of((step - 1) * REACH, REACH)
        change = [None] * 16
        for side, (source, target) in enumerate(sides):
            onehot = jnp.where(
                iota((3 * REACH, REACH), 0) == place[side : side + 1, :], 1.0, 0.0
            ).astype(bf16)
            pieces = [
                split_ref[part, p, :, pl.ds(start, 3 * REACH)]
                for part in range(2)
                for p in source
            ]
            value = dot(jnp.concatenate(pieces, axis=0), onehot)
            for k, p in enumerate(target):
                there = value[k * rows : (k + 1) * rows] + value[(4 + k) * rows : (5 + k) * rows]
                part = there - own_ref[p]
                change[p] = part if change[p] is None else change[p] + part
        for p in range(16):
            new = own_ref[p] if change[p] is None else own_ref[p] + 0.5 * change[p]
            for h in range(2):
                turn_ref[h, pl.ds(p, rows, stride=16), :] = new[:, h * LANES : (h + 1) * LANES]
        for h in range(2):
            out_ref[:, h * LANES : (h + 1) * LANES] = turn_ref[h]

    @pl.when(step < tiles)
    def _():
        own_ref[...] = ahead_ref[...]


def full_new_state(shape, stepped, before, after, neighbours, first, elements):
    points, rows, size = stepped.shape
    tiles = size // REACH
    tile = (points, rows, REACH)
    out = pl.pallas_call(
        functools.partial(full_edges, elements),
        grid=(tiles + 1,),
        in_specs=[
            pl.BlockSpec(memory_space=pltpu.SMEM),
            pl.BlockSpec(tile, lambda i: (0, 0, jnp.minimum(i, tiles - 1))),
            whole(before.shape),
            whole(after.shape),
            pl.BlockSpec((4, REACH), lambda i: (0, jnp.maximum(i - 1, 0))),
        ],
        out_specs=pl.BlockSpec((rows * points, REACH), lambda i: (0, jnp.maximum(i - 1, 0))),
        out_shape=jax.ShapeDtypeStruct((rows * points, size), f32),
        scratch_shapes=[
            pltpu.VMEM(tile, f32),
            pltpu.VMEM((2, 16, rows, size + 2 * REACH), bf16),
            pltpu.VMEM((2, rows * points, LANES), f32),
        ],
        compiler_params=params(24),
        cost_estimate=cost(4 * 10**9, 10 << 20),
        name="full_edges",
    )(first, in_hbm(stepped), before, after, neighbours)
    return out.reshape(shape)


def request_table(grp_ref, cells_ref, ids_ref, out_ref, rank_ref):
    chunks = cells_ref.shape[0]
    owner_at = iota((64, LANES), 0)
    cells = [cells_ref[c : c + 1, :] for c in range(chunks)]
    mine = [jnp.where(owner_at == (cell >> 11), 1.0, 0.0) for cell in cells]
    before = jnp.where(iota((LANES, 2 * LANES), 0) < iota((LANES, 2 * LANES), 1), 1.0, 0.0)
    counts = dot(jnp.concatenate(mine, axis=0).astype(bf16), before.astype(bf16))
    carried = jnp.zeros((64, LANES), f32)
    slots, high, low = [], [], []
    for c, cell in enumerate(cells):
        count = counts[64 * c : 64 * c + 64]
        rank = jnp.sum(mine[c] * (count[:, :LANES] + carried), axis=0, keepdims=True).astype(i32)
        carried = carried + count[:, LANES:]
        rank_ref[c : c + 1, :] = rank
        slots.append(jnp.where(owner_at == rank, 1.0, 0.0).astype(bf16))
        row = cell & 2047
        high.append((mine[c] * (row >> 7).astype(f32)).astype(bf16))
        low.append((mine[c] * (row & 127).astype(f32)).astype(bf16))
    parts = jnp.concatenate([jnp.concatenate(p, axis=1) for p in (high, low)], axis=0)
    wanted = dot_nt(parts, jnp.concatenate(slots, axis=1))
    wanted = wanted[:64] * 128.0 + wanted[64:]
    wanted = jnp.concatenate([wanted, wanted], axis=1)
    share = pltpu.roll(wanted, 64 - 12 * grp_ref[0], 1)
    message = jnp.where(iota((64, LANES), 1) < 64, ids_ref[...].astype(f32), share)
    for y in range(4):
        out_ref[64 * y : 64 * y + 64, :] = message


def requests(grp, ocean_cells, ids):
    chunks = ocean_cells.shape[0] // LANES
    vmem = pl.BlockSpec(memory_space=pltpu.VMEM)
    return pl.pallas_call(
        request_table,
        in_specs=[pl.BlockSpec(memory_space=pltpu.SMEM), vmem, vmem],
        out_shape=[
            jax.ShapeDtypeStruct((256, LANES), f32),
            jax.ShapeDtypeStruct((chunks, LANES), i32),
        ],
        compiler_params=params(),
        name="request_table",
    )(grp, ocean_cells.reshape(chunks, LANES), ids)


QUERIES = 256


def pick_values(table_ref, out_ref, cells_ref, turned_ref, ids_ref, found_ref):
    lane = iota((LANES, LANES), 1)
    asked = table_ref[:, 0, 2 * LANES :]
    ids = jnp.where(lane < 64, asked[:LANES], pltpu.roll(asked[LANES:], 64, 1))
    ids_ref[...] = ids.astype(i32)
    lane = iota((64, LANES), 1)
    wanted = jnp.zeros((64, LANES), f32)
    for y in range(4):
        part = pltpu.roll(asked[64 * y : 64 * y + 64], 64 + 12 * y, 1)
        wanted = jnp.where((lane >= 12 * y) & (lane < 12 * y + 12), part, wanted)
    lane = iota((32, LANES), 1)
    cells_ref[...] = jnp.where(lane < 64, wanted[:32], pltpu.roll(wanted[32:], 64, 1)).astype(i32)

    high, low = split_two(table_ref[:, 0, : 2 * LANES].T)
    for half in range(2):
        turned_ref[half, :LANES] = high[half * LANES : (half + 1) * LANES]
        turned_ref[half, LANES:] = low[half * LANES : (half + 1) * LANES]
    groups = QUERIES // LANES
    device_at = iota((256, QUERIES), 0)
    block_at = iota((LANES, QUERIES), 0)

    def some(step, carry):
        rows = [ids_ref[pl.ds(groups * step + k, 1), :] for k in range(groups)]
        asked = jnp.concatenate(rows, axis=1)
        onehot = jnp.where(device_at == (asked >> 7), 1.0, 0.0).astype(bf16)
        hit = block_at == (asked & 127)
        for half in range(2):
            value = dot(turned_ref[half], onehot)
            part = value[:LANES] + value[LANES:]
            found = jnp.sum(jnp.where(hit, part, 0.0), axis=0, keepdims=True)
            for k in range(groups):
                found_ref[half, pl.ds(groups * step + k, 1), :] = found[
                    :, k * LANES : (k + 1) * LANES
                ]
        return carry

    lax.fori_loop(0, LANES // groups, some, 0, unroll=32)
    for half in range(2):
        for y in range(2):
            at = (2 * half + y) * LANES
            out_ref[:, 0, at : at + LANES] = found_ref[half, 64 * y : 64 * y + 64, :]


def picked(table):
    return pl.pallas_call(
        pick_values,
        out_shape=[
            pltpu.HBM((64, 1, 4 * LANES), f32),
            jax.ShapeDtypeStruct((32, LANES), i32),
        ],
        scratch_shapes=[
            pltpu.VMEM((2, 256, 256), bf16),
            pltpu.VMEM((LANES, LANES), i32),
            pltpu.VMEM((2, LANES, LANES), f32),
        ],
        compiler_params=params(24),
        name="pick_values",
    )(table)


def quarter_weights(grp_ref, w_ref, out_ref):
    column, lane = iota((4 * LANES, LANES), 0), iota((4 * LANES, LANES), 1)
    wanted = (column // LANES == lane // 32) & (
        column % LANES == 32 * grp_ref[0] + lane % 32
    )
    chosen = jnp.where(wanted, 1.0, 0.0).astype(bf16)
    at = [(r, b) for r in range(w_ref.shape[0]) for b in range(4)]
    rows = [
        jnp.concatenate([w_ref[r, 4 * b + q] for q in range(4)], axis=1) for r, b in at
    ]
    packed = dot(jnp.concatenate(rows, axis=0), chosen).astype(bf16)
    for k, (r, b) in enumerate(at):
        out_ref[r, b] = packed[LANES * k : LANES * (k + 1)]


def packed_weights(grp, block_weights):
    count, slots, block = block_weights.shape[:3]
    step = 8
    return pl.pallas_call(
        quarter_weights,
        grid=(count // step,),
        in_specs=[
            pl.BlockSpec(memory_space=pltpu.SMEM),
            pl.BlockSpec((step, slots, block, block), lambda i: (i, 0, 0, 0)),
        ],
        out_specs=pl.BlockSpec((step, slots // 4, block, block), lambda i: (i, 0, 0, 0)),
        out_shape=jax.ShapeDtypeStruct((count, slots // 4, block, block), bf16),
        compiler_params=params(),
        cost_estimate=cost(10**9, 10 << 20),
        name="quarter_weights",
    )(grp, in_hbm(block_weights))


def remap_rows(
    fw_ref, got_ref, index_ref, w_ref, out_ref, field_ref, mapped_ref, sent_ref, pair_ref
):
    values = []
    for v in range(4):
        rows = slice(16 * v, 16 * v + 16)
        tiles = [
            got_ref[rows, 0, (2 * h + y) * LANES : (2 * h + y + 1) * LANES]
            for y in range(2)
            for h in range(2)
        ]
        turned = jnp.concatenate(tiles, axis=0).T
        values.append(jnp.concatenate([turned[:64], turned[64:]], axis=1))
    wind = jnp.sqrt(1.0 + values[0] * values[0] + values[1] * values[1])
    for f in range(16):
        if f < 12:
            total = fw_ref[f, 0] * values[0]
            for v in range(1, 4):
                total += fw_ref[f, v] * values[v]
            total = (total * wind).astype(bf16).astype(f32)
        else:
            total = jnp.zeros((64, LANES), f32)
        field_ref[pl.ds(f, 64, stride=16), :] = total

    for r in range(16):
        total = jnp.zeros((16, LANES), f32)
        for b in range(0, 4, 2):
            at = (r * 4 + b) * 16
            pair = field_ref[at : at + 32, :].astype(bf16)
            pair = jnp.concatenate([pair[:16], pair[16:]], axis=1)
            weights = jnp.concatenate([w_ref[r, b], w_ref[r, b + 1]], axis=1)
            total += dot_nt(pair, weights)
        mapped_ref[16 * r : 16 * r + 16, :] = total

    parts = mapped_ref[...].astype(bf16)
    row_at = iota((LANES, 8 * LANES), 0)

    def some(at, carry):
        rows = [index_ref[pl.ds(8 * at + k, 1), :] for k in range(8)]
        asked = jnp.concatenate(rows, axis=1)
        onehot = jnp.where(row_at == (asked & 127), 1.0, 0.0).astype(bf16)
        value = dot(parts, onehot)
        block = asked >> 7
        found = value[:16]
        for r in range(1, 16):
            found = jnp.where(block == r, value[16 * r : 16 * r + 16], found)
        for k in range(8):
            sent_ref[pl.ds(8 * at + k, 16, stride=32), :] = found[
                :, k * LANES : (k + 1) * LANES
            ]
        return carry

    lax.fori_loop(0, 4, some, 0, unroll=True)
    lane = iota((32, LANES), 1)
    for y in range(4):
        a, b, c = [sent_ref[(3 * y + f) * 32 : (3 * y + f) * 32 + 32, :] for f in range(3)]
        base = 64 * y
        low, high = slice(base, base + 32), slice(base + 32, base + 64)
        pair_ref[low, 0, :] = jnp.where(lane < 64, a, pltpu.roll(b, 64, 1))
        pair_ref[low, 1, :] = c
        pair_ref[high, 0, :] = jnp.where(lane < 64, pltpu.roll(a, 64, 1), b)
        pair_ref[high, 1, :] = pltpu.roll(c, 64, 1)
    out_ref[...] = pair_ref[...].astype(bf16)


def remapped_cells(flux_weight, got, index, block_weights):
    smem = pl.BlockSpec(memory_space=pltpu.SMEM)
    vmem = pl.BlockSpec(memory_space=pltpu.VMEM)
    return pl.pallas_call(
        remap_rows,
        in_specs=[smem, vmem, vmem, vmem],
        out_shape=jax.ShapeDtypeStruct((256, 2, LANES), bf16),
        scratch_shapes=[
            pltpu.VMEM((64 * 16, LANES), f32),
            pltpu.VMEM((256, LANES), f32),
            pltpu.VMEM((17 * 32, LANES), f32),
            pltpu.VMEM((256, 2, LANES), f32),
        ],
        compiler_params=params(),
        name="remap_rows",
    )(flux_weight, got, index, block_weights)


def place_cells(got_ref, cells_ref, rank_ref, out_ref):
    got = got_ref[...].astype(f32)
    got = got[0:64] + got[64:128] + got[128:192] + got[192:256]
    pair, last = got[:, 0, :].T, got[:, 1, :].T
    parts = jnp.concatenate(split_two(jnp.concatenate([pair, last[:64]], axis=0)), axis=1)
    owner_at = iota((64, 4 * LANES), 0)
    for c in range(4):
        rows = range(4 * c, 4 * c + 4)
        cell = jnp.concatenate([cells_ref[r : r + 1, :] for r in rows], axis=1)
        rank = jnp.concatenate([rank_ref[r : r + 1, :] for r in rows], axis=1)
        onehot = jnp.where(owner_at == (cell >> 11), 1.0, 0.0).astype(bf16)
        value = dot(parts, jnp.concatenate([onehot, onehot], axis=0))
        hit = owner_at == rank
        for f in range(3):
            out_ref[f : f + 1, c * 4 * LANES : (c + 1) * 4 * LANES] = jnp.sum(
                jnp.where(hit, value[64 * f : 64 * f + 64], 0.0), axis=0, keepdims=True
            )


def placed(got, ocean_cells, rank):
    count = ocean_cells.shape[0]
    return pl.pallas_call(
        place_cells,
        out_shape=jax.ShapeDtypeStruct((3, count), f32),
        compiler_params=params(),
        name="place_cells",
    )(got, ocean_cells.reshape(count // LANES, LANES), rank)


def upward():
    count = lax.axis_size(both)
    return [(i, (i + 1) % count) for i in range(count)]


def around(first, last):
    up = upward()
    down = [(j, i) for i, j in up]
    return lax.ppermute(last, both, up), lax.ppermute(first, both, down)


def exchange(x, axis):
    return lax.all_to_all(x, axis, split_axis=0, concat_axis=0, tiled=True)


def body(atmos_state, neighbours, flux_weight, block_weights, block_ids, block_counts, ocean_cells):
    size = atmos_state.shape[3]
    elements = size * lax.axis_size(both)
    grp = lax.axis_index("grp").astype(i32).reshape(1)
    first = (lax.axis_index(both) * size).astype(i32).reshape(1)

    stepped, rim = bottom_stepped(atmos_state, neighbours)
    prev = lax.ppermute(rim, both, upward())

    shift = REACH // LANES * 16
    blocks = elements // LANES * 16
    live = jnp.arange(block_ids.shape[1])[None, :] < block_counts[:, None]
    ids = jnp.where(live, (block_ids + shift) % blocks, -1)
    ids = ids.reshape(-1, 4, 4).transpose(2, 0, 1).reshape(4, 64)
    ids = lax.dynamic_slice_in_dim(ids, lax.axis_index("grp"), 1, 0)
    ids = jnp.concatenate([ids, ids], axis=1)
    request, rank = requests(grp, ocean_cells, ids)

    inner = bottom_inner(stepped, neighbours, first, elements)
    slices = bottom_slices(stepped, prev, neighbours, inner, request, first, elements)
    table = exchange(slices, both)
    all_stepped, all_low, all_high = full_stepped(atmos_state)
    all_before, all_after = around(all_low, all_high)
    new_state = full_new_state(
        atmos_state.shape, all_stepped, all_before, all_after, neighbours, first, elements
    )

    answer, wanted = picked(table)
    answer, block_weights = lax.optimization_barrier((answer, block_weights))
    weights = packed_weights(grp, block_weights)
    got = exchange(answer, "blk")
    sent = remapped_cells(flux_weight, got, wanted, weights)
    ocean_flux = placed(exchange(sent, both), ocean_cells, rank)
    return new_state, ocean_flux


def solution(mesh):
    in_specs = (
        P(None, None, None, both),
        P(None, both),
        P(),
        P("blk", None, None, None),
        P("blk", None),
        P("blk"),
        P("blk"),
    )
    out_specs = (P(None, None, None, both), P("grp", "blk"))
    return jax.shard_map(body, mesh=mesh, in_specs=in_specs, out_specs=out_specs, check_vma=False)
```
